32 devices in a mesh: row: 4 (over x, core), sector: 8 (over z, y).
Axes of the slice: x: 2, y: 2, z: 4, core: 2. Of those that a mesh axis runs over, the one named last changes fastest.
Arguments:
- state: float32 [6, 256, 128, 128], P(None, 'row', 'sector'), may hold values from -6 to 6
- interp_blocks: float32 [16, 16, 32], replicated, may hold values from -0.1 to 0.8
- rotor_offset: int32 [4, 3], replicated, may hold values from 0 to 127
- axial_speed: float32 [6], replicated, may hold values from 0.3 to 1.5
- row_swirl: float32 [4], P('row'), may hold values from -1.5 to 1.5
- diffusivity: float32 [6], replicated, may hold values from 0.05 to 0.3
- coupling: float32 [6, 6], replicated, may hold values from -1.5 to 1.5
Outputs:
- advanced: float32 [6, 256, 128, 128], P(None, 'row', 'sector')
The draws below stay inside these ranges and needn't reach their ends.
All inputs are finite; a program needn't handle non-finite values.
Results may differ from the reference program's by a relative error of at most 0.0001.
Values sent between devices are 32-bit elements; how exact they have to be, the bound alone decides.
No kernel may reach another device: no remote copies, remote signals or barrier semaphores. Data moves between devices by JAX's collectives and lax.ppermute only.
A program may use at most 128 MiB of HBM per device.

```python
import math
import jax
import jax.numpy as jnp
from jax import lax

FIELDS = 6
SECTIONS = 4
CA = 64
CT = 16
CR = 128
ROWS = 4
INTERFACES = 3
NA = 256
NT = 128
N_ROW = 4
N_SECTOR = 8


def draw_interp_blocks(key, part):
    cell_ids = jnp.arange(CT)[:, None, None]
    target_ids = jnp.arange(CT)[None, :, None]
    source_ids = jnp.arange(2 * CT)[None, None, :]
    main_weight = jnp.where(source_ids == target_ids + cell_ids, 0.7, 0.0)
    side_weight = jnp.where(source_ids == target_ids + cell_ids + 1, 0.3, 0.0)
    spread = 0.15 / jnp.sqrt(2.0 * CT)
    noise = jax.random.truncated_normal(jax.random.fold_in(key, 11), -3.0, 3.0, (CT, CT, 2 * CT), jnp.float32)
    values = main_weight + side_weight + spread * noise
    return jnp.clip(values, -0.1, 0.8).astype(jnp.float32)


def touch_ends(values, stream_key, least, high):
    shape = values.shape
    spot = [jax.random.randint(jax.random.fold_in(stream_key, axis), (), 0, shape[axis]) for axis in range(len(shape))]
    values = values.at[tuple(spot)].set(least)
    longest = shape.index(max(shape))
    spot[longest] = (spot[longest] + 1) % shape[longest]
    return values.at[tuple(spot)].set(high)


def steps_of(stream_key, shape, cuts, smallest, largest):
    def one(axis_at, parts):
        heights = jax.random.uniform(jax.random.fold_in(jax.random.fold_in(stream_key, 6), axis_at), (parts,), jnp.float32, smallest / len(cuts), largest / len(cuts))
        return jnp.repeat(jnp.exp(heights), shape[axis_at] // parts).reshape((-1,) + (1,) * (len(shape) - axis_at - 1))

    loudness = one(*cuts[0])
    for cut in cuts[1:]:
        loudness = loudness * one(*cut)
    return loudness


def gaussian(rng, shape, scale, most, split=(), held_as=jnp.bfloat16):
    values = scale * jax.random.normal(rng, shape, jnp.float32)
    if split:
        values = values * steps_of(rng, shape, split, -0.22, 0.18)
    return jnp.clip(values, -most, most).astype(held_as)


def setup_inputs(seed: int = 0) -> dict:
    key_of = jax.random.split(jax.random.key(seed), 8)
    state = gaussian(key_of[0], (FIELDS, NA, NT, CR), 1.0, 6.0, ((1, 4), (2, 8)), jnp.float32)
    interp_blocks = draw_interp_blocks(jax.random.fold_in(key_of[7], 71), 0)
    rotor_offset = touch_ends(jax.random.randint(key_of[2], (SECTIONS, INTERFACES), 0, NT), jax.random.fold_in(key_of[2], 1), 0, NT - 1).astype(jnp.int32)
    axial_speed = jnp.clip(jnp.exp(jax.random.uniform(key_of[3], (FIELDS,), jnp.float32, math.log(0.3), math.log(1.5))), 0.3, 1.5)
    row_swirl = jnp.clip(jax.random.uniform(key_of[4], (ROWS,), jnp.float32, -1.5, 1.5) * steps_of(key_of[4], (ROWS,), ((0, 4),), -0.4, 0.0), -1.5, 1.5)
    diffusivity = jnp.clip(jnp.exp(jax.random.uniform(key_of[5], (FIELDS,), jnp.float32, math.log(0.05), math.log(0.3))), 0.05, 0.3)
    coupling = gaussian(key_of[6], (FIELDS, FIELDS), 0.3, 1.5, (), jnp.float32)
    return dict(state=state, interp_blocks=interp_blocks, rotor_offset=rotor_offset, axial_speed=axial_speed, row_swirl=row_swirl, diffusivity=diffusivity, coupling=coupling)


time_step = 0.4
highest = lax.Precision.HIGHEST


def residual_of(center, axial_pad, cycle_pad, axial_speed, swirl_speed, diffusivity, coupling):
    d_axial = (-axial_pad[:, 4:] + 8.0 * axial_pad[:, 3:-1] - 8.0 * axial_pad[:, 1:-3] + axial_pad[:, :-4]) / 12.0
    l_axial = (-axial_pad[:, 4:] + 16.0 * axial_pad[:, 3:-1] - 30.0 * center + 16.0 * axial_pad[:, 1:-3] - axial_pad[:, :-4]) / 12.0
    d_cycle = (-cycle_pad[:, :, 4:] + 8.0 * cycle_pad[:, :, 3:-1] - 8.0 * cycle_pad[:, :, 1:-3] + cycle_pad[:, :, :-4]) / 12.0
    l_cycle = (-cycle_pad[:, :, 4:] + 16.0 * cycle_pad[:, :, 3:-1] - 30.0 * center + 16.0 * cycle_pad[:, :, 1:-3] - cycle_pad[:, :, :-4]) / 12.0
    radial_pad = jnp.pad(center, ((0, 0), (0, 0), (0, 0), (1, 1)))
    l_radial = radial_pad[..., 2:] - 2.0 * center + radial_pad[..., :-2]
    mixing = jnp.einsum("fg,gatr->fatr", coupling, center, precision=highest)
    speed_col = axial_speed[:, None, None, None]
    diff_col = diffusivity[:, None, None, None]
    return -speed_col * d_axial - swirl_speed * d_cycle + diff_col * (l_axial + l_cycle + l_radial) + mixing


def interface(planes, offset, interp_blocks):
    sector_shift = offset // CT
    cell_shift = offset % CT
    blocks = planes.reshape(FIELDS, 2, N_SECTOR, CT, CR)
    first_part = jnp.roll(blocks, -sector_shift, axis=2)
    second_part = jnp.roll(first_part, -1, axis=2)
    paired = jnp.concatenate([first_part, second_part], axis=3)
    weights = interp_blocks[cell_shift]
    result = jnp.einsum("jk,faskr->fasjr", weights, paired, precision=highest)
    return result.reshape(FIELDS, 2, NT, CR)


def reference(state, interp_blocks, rotor_offset, axial_speed, row_swirl, diffusivity, coupling):
    def residual(current, section_index):
        blade_rows = current.reshape(FIELDS, N_ROW, CA, NT, CR)
        pieces = []
        for row_number in range(N_ROW):
            center = blade_rows[:, row_number]
            empty = jnp.zeros_like(center[:, :2])
            if row_number > 0:
                ghost_up = interface(blade_rows[:, row_number - 1, CA - 2:], rotor_offset[section_index, row_number - 1], interp_blocks)
            else:
                ghost_up = empty
            if row_number < N_ROW - 1:
                ghost_down = interface(blade_rows[:, row_number + 1, :2], (NT - rotor_offset[section_index, row_number]) % NT, interp_blocks)
            else:
                ghost_down = empty
            axial_pad = jnp.concatenate([ghost_up, center, ghost_down], axis=1)
            cycle_pad = jnp.concatenate([center[:, :, NT - 2:], center, center[:, :, :2]], axis=2)
            pieces.append(residual_of(center, axial_pad, cycle_pad, axial_speed, row_swirl[row_number], diffusivity, coupling))
        return jnp.concatenate(pieces, axis=1)

    first_rate = residual(state, 0)
    second_rate = residual(state + (0.5 * time_step) * first_rate, 1)
    third_rate = residual(state + (0.5 * time_step) * second_rate, 2)
    fourth_rate = residual(state + time_step * third_rate, 3)
    return state + (time_step / 6.0) * (first_rate + 2.0 * second_rate + 2.0 * third_rate + fourth_rate)
```

```python
import functools

import jax
import jax.numpy as jnp
from jax import lax
from jax.experimental import pallas as pl
from jax.experimental.pallas import tpu as pltpu
from jax.sharding import PartitionSpec as P

time_step = 0.4
highest = lax.Precision.HIGHEST
VMEM = pltpu.VMEM
SMEM = pltpu.SMEM
LOW = 8


def whole(space):
    return pl.BlockSpec(memory_space=space)


def params():
    return pltpu.CompilerParams(vmem_limit_bytes=56 * 1024 * 1024)


class Plan:
    def __init__(self, state, sectors):
        self.fields, self.axial, self.cycle, self.radial = state.shape
        self.sectors = sectors
        quarter = self.axial // 4
        self.outer = ((0, quarter), (self.axial - quarter, self.axial))
        self.inner = ((quarter, self.axial - quarter),)
        self.half = sectors // 2
        self.per = -(-2 * self.fields // self.half)
        self.combos = self.per * sectors

    def combo(self, side, field, plane):
        place = side * self.per * self.half + field * 2 + plane
        return place // self.per, place % self.per


def count(ranges):
    return sum(high - low for low, high in ranges)


def write_edges(plan, value, field, place, low_ref, high_ref):
    tile, row = place
    low_ref[field, tile, row : row + 2, :] = value[:2]
    high_ref[field, tile, row : row + 2, :] = value[plan.cycle - 2 :]


def first_kernel(plan, state, b_ref, lo_o, hi_o, lo_i, hi_i):
    planes = ((0, 1), (plan.axial - 1, plan.axial))
    for field in range(plan.fields):
        for plane in range(2):
            piece, slot = plan.combo(0, field, plane)
            b_ref[piece, slot] = state[field, plan.axial - 2 + plane]
            piece, slot = plan.combo(1, field, plane)
            b_ref[piece, slot] = state[field, plane]
    for ranges, low_ref, high_ref in ((plan.outer, lo_o, hi_o), (plan.inner, lo_i, hi_i)):
        start = 0
        for low, high in ranges:

            def body(tile, carry, low=low, start=start, low_ref=low_ref, high_ref=high_ref):
                for field in range(plan.fields):
                    for step in range(4):
                        at = low + tile * 4 + step
                        low_ref[field, start + tile, 2 * step : 2 * step + 2, :] = state[field, at, 0:2, :]
                        high_ref[field, start + tile, 2 * step : 2 * step + 2, :] = state[
                            field, at, plan.cycle - 2 : plan.cycle, :
                        ]
                return carry

            lax.fori_loop(0, (high - low) // 4, body, 0)
            start += (high - low) // 4


def edge_shape(plan, ranges):
    return jax.ShapeDtypeStruct((plan.fields, count(ranges) // 4, 8, plan.radial), jnp.float32)


def first(plan, state):
    return pl.pallas_call(
        functools.partial(first_kernel, plan),
        in_specs=[whole(VMEM)],
        out_specs=[whole(VMEM)] * 5,
        out_shape=[
            jax.ShapeDtypeStruct((plan.sectors, plan.per, plan.cycle, plan.radial), jnp.float32),
            edge_shape(plan, plan.outer),
            edge_shape(plan, plan.outer),
            edge_shape(plan, plan.inner),
            edge_shape(plan, plan.inner),
        ],
        compiler_params=params(),
        name="first_edges",
    )(state)


def interp_kernel(plan, section, place, offsets, weights, got, out):
    full = plan.cycle * plan.sectors
    row, sector = place[0], place[1]
    up = sector < plan.half
    at = jnp.where(up, jnp.minimum(row, offsets.shape[1] - 1), jnp.maximum(row - 1, 0))
    offset = offsets[section, at]
    offset = jnp.where(up, offset, lax.rem(full - offset, full))
    turn = offset // plan.cycle
    cell = lax.rem(offset, plan.cycle)
    matrix = weights[cell]
    for target in range(plan.sectors):
        here = lax.rem(target + turn, plan.sectors)
        after = lax.rem(target + turn + 1, plan.sectors)
        for slot in range(plan.per):
            pair = jnp.concatenate([got[here, slot], got[after, slot]], axis=0)
            out[target, slot] = jnp.dot(
                matrix, pair, precision=highest, preferred_element_type=jnp.float32
            )


def interp(plan, section, place, offsets, weights, got):
    return pl.pallas_call(
        functools.partial(interp_kernel, plan, section),
        in_specs=[whole(SMEM), whole(SMEM), whole(VMEM), whole(VMEM)],
        out_specs=whole(VMEM),
        out_shape=jax.ShapeDtypeStruct(got.shape, jnp.float32),
        compiler_params=params(),
        name="interpolate",
    )(place, offsets, weights, got)


def coefficients(plan, speed, swirl, diffusion, coupling):
    twelfth = 1.0 / 12.0
    w = swirl[0]
    table = []
    for f in range(plan.fields):
        v, d = speed[f], diffusion[f]
        axial = ((-v - d) * twelfth, (8.0 * v + 16.0 * d) * twelfth, (16.0 * d - 8.0 * v) * twelfth, (v - d) * twelfth)
        cycle = ((-w - d) * twelfth, (8.0 * w + 16.0 * d) * twelfth, (16.0 * d - 8.0 * w) * twelfth, (w - d) * twelfth)
        mix = [coupling[f, e] - 7.0 * d if e == f else coupling[f, e] for e in range(plan.fields)]
        table.append((axial, cycle, d, mix))
    return table


def stage_kernel(plan, stage, outer, speed, swirl, diffusion, coupling, *refs):
    refs = list(refs)
    ranges = plan.outer if outer else plan.inner
    state = refs.pop(0)
    if stage == 0:
        chunks = {"state": state}
    else:
        chunks = {"outer": refs.pop(0), "inner": refs.pop(0)}
    ghosts = refs.pop(0) if outer else None
    low_in, high_in = refs.pop(0), refs.pop(0)
    if stage == 3:
        older = (refs.pop(0), refs.pop(0))
        if not outer:
            refs.pop(0)
        out_any = refs.pop(0)
        out_buf, sem, work = refs
    else:
        out = refs.pop(0)
        low_out, high_out = refs.pop(0), refs.pop(0)
        b_out = refs.pop(0) if outer else None
        (work,) = refs
    table = coefficients(plan, speed, swirl, diffusion, coupling)
    cycle, radial = plan.cycle, plan.radial
    lane = lax.broadcasted_iota(jnp.int32, (cycle, radial), 1)
    not_first = lane > 0
    not_last = lane < radial - 1

    def source(at):
        if at < 0:
            return ghosts, 0, at + 2
        if at >= plan.axial:
            return ghosts, 1, at - plan.axial
        if stage == 0:
            return state, None, at
        start = 0
        for low, high in plan.outer:
            if low <= at < high:
                return chunks["outer"], None, start + at - low
            start += high - low
        return chunks["inner"], None, at - plan.inner[0][0]

    def fill(field, at, to):
        ref, side, place = source(at)
        if side is not None:
            piece, slot = plan.combo(side, field, place)
            work[field, to, LOW : LOW + cycle, :] = ref[piece, slot]
        else:
            work[field, to, LOW : LOW + cycle, :] = ref[field, place]

    begin = 0
    for low, high in ranges:
        size = high - low
        for field in range(plan.fields):
            for at, to in ((low - 2, 0), (low - 1, 1), (high, size + 2), (high + 1, size + 3)):
                fill(field, at, to)
        ref, _, first_place = source(low)

        def copy(tile, carry, ref=ref, first_place=first_place, begin=begin):
            for field in range(plan.fields):
                for step in range(4):
                    place = tile * 4 + step
                    work[field, place + 2, LOW : LOW + cycle, :] = ref[field, first_place + place]
                    work[field, place + 2, LOW - 2 : LOW, :] = low_in[field, begin // 4 + tile, 2 * step : 2 * step + 2, :]
                    work[field, place + 2, LOW + cycle : LOW + cycle + 2, :] = high_in[
                        field, begin // 4 + tile, 2 * step : 2 * step + 2, :
                    ]
            return carry

        lax.fori_loop(0, size // 4, copy, 0)

        def compute(tile, carry, low=low, begin=begin):
            for step in range(4):
                place = tile * 4 + step
                center = [work[e, place + 2, LOW : LOW + cycle, :] for e in range(plan.fields)]
                for f in range(plan.fields):
                    axial, around, d, mix = table[f]
                    total = mix[0] * center[0]
                    for e in range(1, plan.fields):
                        total += mix[e] * center[e]
                    for by, factor in zip((0, 1, 3, 4), axial):
                        total += factor * work[f, place + by, LOW : LOW + cycle, :]
                    for by, factor in zip((-2, -1, 1, 2), around):
                        total += factor * work[f, place + 2, LOW + by : LOW + by + cycle, :]
                    left = jnp.where(not_first, pltpu.roll(center[f], 1, 1), 0.0)
                    right = jnp.where(not_last, pltpu.roll(center[f], radial - 1, 1), 0.0)
                    total += d * (left + right)
                    base = state[f, low + place]
                    if stage == 3:
                        second, third = older
                        value = (
                            second[f, begin + place] + 2.0 * third[f, begin + place] + center[f] - base
                        ) * (1.0 / 3.0) + (time_step / 6.0) * total
                        out_buf[f, begin + place] = value
                    else:
                        value = base + (time_step if stage == 2 else 0.5 * time_step) * total
                        out[f, begin + place] = value
                        low_out[f, begin // 4 + tile, 2 * step : 2 * step + 2, :] = value[:2]
                        high_out[f, begin // 4 + tile, 2 * step : 2 * step + 2, :] = value[cycle - 2 :]
            return carry

        lax.fori_loop(0, size // 4, compute, 0)
        begin += size

    if stage == 3:
        begin = 0
        copies = []
        for number, (low, high) in enumerate(ranges):
            copies.append(
                pltpu.make_async_copy(
                    out_buf.at[:, begin : begin + high - low], out_any.at[:, low:high], sem.at[number]
                )
            )
            copies[-1].start()
            begin += high - low
        for item in copies:
            item.wait()
    elif outer:
        total = count(ranges)
        for field in range(plan.fields):
            for plane in range(2):
                piece, slot = plan.combo(0, field, plane)
                b_out[piece, slot] = out[field, total - 2 + plane]
                piece, slot = plan.combo(1, field, plane)
                b_out[piece, slot] = out[field, plane]


def stage_call(plan, stage, outer, scalars, state, chunks, ghosts, halos, older=None, whole_out=None):
    ranges = plan.outer if outer else plan.inner
    planes = count(ranges)
    operands = [*scalars, state]
    if stage > 0:
        operands += list(chunks)
    if outer:
        operands.append(ghosts)
    operands += list(halos)
    specs = [whole(SMEM)] * len(scalars) + [whole(VMEM)] * (len(operands) - len(scalars))
    chunk = jax.ShapeDtypeStruct((plan.fields, planes, plan.cycle, plan.radial), jnp.float32)
    longest = max(high - low for low, high in ranges)
    scratch = [pltpu.VMEM((plan.fields, longest + 4, plan.cycle + 16, plan.radial), jnp.float32)]
    aliases = {}
    if stage == 3:
        operands += list(older)
        specs += [whole(VMEM)] * 2
        if whole_out is not None:
            aliases = {len(operands): 0}
            operands.append(whole_out)
            specs.append(whole(pl.ANY))
        out_shape = [jax.ShapeDtypeStruct(state.shape, jnp.float32)]
        out_specs = [whole(pl.ANY)]
        scratch = [pltpu.VMEM(chunk.shape, jnp.float32), pltpu.SemaphoreType.DMA((len(ranges),))] + scratch
    else:
        out_shape = [chunk, edge_shape(plan, ranges), edge_shape(plan, ranges)]
        if outer:
            out_shape.append(
                jax.ShapeDtypeStruct((plan.sectors, plan.per, plan.cycle, plan.radial), jnp.float32)
            )
        out_specs = [whole(VMEM)] * len(out_shape)
    return pl.pallas_call(
        functools.partial(stage_kernel, plan, stage, outer),
        in_specs=specs,
        out_specs=out_specs,
        out_shape=out_shape,
        scratch_shapes=scratch,
        input_output_aliases=aliases,
        compiler_params=params(),
        name=f"stage{stage}_{'outer' if outer else 'inner'}",
    )(*operands)


def exchange(edges):
    size = lax.axis_size("sector")
    ahead = [(i, (i + 1) % size) for i in range(size)]
    back = [(i, (i - 1) % size) for i in range(size)]
    low_edges, high_edges = edges
    return lax.ppermute(high_edges, "sector", ahead), lax.ppermute(low_edges, "sector", back)


def row_hop(plan, value):
    rows, sectors = lax.axis_size("row"), plan.sectors
    pairs = []
    for row in range(rows):
        for sector in range(sectors):
            target = row + 1 if sector < plan.half else row - 1
            if 0 <= target < rows:
                pairs.append((row * sectors + sector, target * sectors + sector))
    return lax.ppermute(value, ("row", "sector"), pairs)


def on_device(state, interp_blocks, rotor_offset, axial_speed, row_swirl, diffusivity, coupling):
    plan = Plan(state, lax.axis_size("sector"))
    place = jnp.stack([lax.axis_index("row"), lax.axis_index("sector")]).astype(jnp.int32)
    scalars = (axial_speed, row_swirl, diffusivity, coupling)

    def ghosts_of(section, planes):
        got = lax.all_to_all(planes, "sector", 0, 0, tiled=True)
        made = interp(plan, section, place, rotor_offset, interp_blocks, got)
        return lax.all_to_all(row_hop(plan, made), "sector", 0, 0, tiled=True)

    planes, lo_o, hi_o, lo_i, hi_i = first(plan, state)
    chunks = None
    history = []
    outer_edges, inner_edges = (lo_o, hi_o), (lo_i, hi_i)
    for stage in range(4):
        outer_halos = exchange(outer_edges)
        inner_halos = exchange(inner_edges)
        ghosts = ghosts_of(stage, planes)
        if stage < 3:
            out_o, lo_o, hi_o, planes = stage_call(
                plan, stage, True, scalars, state, chunks, ghosts, outer_halos
            )
            out_i, lo_i, hi_i = stage_call(
                plan, stage, False, scalars, state, chunks, None, inner_halos
            )
            chunks = (out_o, out_i)
            history.append(chunks)
            outer_edges, inner_edges = (lo_o, hi_o), (lo_i, hi_i)
        else:
            older = history[0], history[1]
            (part,) = stage_call(
                plan, stage, True, scalars, state, chunks, ghosts, outer_halos, (older[0][0], older[1][0])
            )
            (result,) = stage_call(
                plan, stage, False, scalars, state, chunks, None, inner_halos, (older[0][1], older[1][1]), part
            )
    return result


def solution(mesh):
    return jax.shard_map(
        on_device,
        mesh=mesh,
        in_specs=(P(None, "row", "sector", None), P(), P(), P(), P("row"), P(), P()),
        out_specs=P(None, "row", "sector", None),
        check_vma=False,
    )
```

```python
import functools

import jax
import jax.numpy as jnp
from jax import lax
from jax.experimental import pallas as pl
from jax.experimental.pallas import tpu as pltpu
from jax.sharding import PartitionSpec as P

time_step = 0.4
highest = lax.Precision.HIGHEST
VMEM = pltpu.VMEM
SMEM = pltpu.SMEM
LOW = 8


def whole(space):
    return pl.BlockSpec(memory_space=space)


def params():
    return pltpu.CompilerParams(vmem_limit_bytes=20 * 1024 * 1024)


class Plan:
    def __init__(self, state, sectors):
        self.fields, self.axial, self.cycle, self.radial = state.shape
        self.sectors = sectors
        quarter = self.axial // 4
        self.outer = ((0, quarter), (self.axial - quarter, self.axial))
        self.inner = ((quarter, self.axial - quarter),)
        self.half = sectors // 2
        self.per = -(-2 * self.fields // self.half)
        self.combos = self.per * sectors

    def combo(self, side, field, plane):
        place = side * self.per * self.half + field * 2 + plane
        return place // self.per, place % self.per


def count(ranges):
    return sum(high - low for low, high in ranges)


def write_edges(plan, value, field, place, low_ref, high_ref):
    tile, row = place
    low_ref[field, tile, row : row + 2, :] = value[:2]
    high_ref[field, tile, row : row + 2, :] = value[plan.cycle - 2 :]


def first_kernel(plan, state, b_ref, lo_o, hi_o, lo_i, hi_i):
    planes = ((0, 1), (plan.axial - 1, plan.axial))
    for field in range(plan.fields):
        for plane in range(2):
            piece, slot = plan.combo(0, field, plane)
            b_ref[piece, slot] = state[field, plan.axial - 2 + plane]
            piece, slot = plan.combo(1, field, plane)
            b_ref[piece, slot] = state[field, plane]
    for ranges, low_ref, high_ref in ((plan.outer, lo_o, hi_o), (plan.inner, lo_i, hi_i)):
        start = 0
        for low, high in ranges:

            def body(tile, carry, low=low, start=start, low_ref=low_ref, high_ref=high_ref):
                for field in range(plan.fields):
                    for step in range(4):
                        at = low + tile * 4 + step
                        low_ref[field, start + tile, 2 * step : 2 * step + 2, :] = state[field, at, 0:2, :]
                        high_ref[field, start + tile, 2 * step : 2 * step + 2, :] = state[
                            field, at, plan.cycle - 2 : plan.cycle, :
                        ]
                return carry

            lax.fori_loop(0, (high - low) // 4, body, 0)
            start += (high - low) // 4


def edge_shape(plan, ranges):
    return jax.ShapeDtypeStruct((plan.fields, count(ranges) // 4, 8, plan.radial), jnp.float32)


def first(plan, state):
    return pl.pallas_call(
        functools.partial(first_kernel, plan),
        in_specs=[whole(VMEM)],
        out_specs=[whole(VMEM)] * 5,
        out_shape=[
            jax.ShapeDtypeStruct((plan.sectors, plan.per, plan.cycle, plan.radial), jnp.float32),
            edge_shape(plan, plan.outer),
            edge_shape(plan, plan.outer),
            edge_shape(plan, plan.inner),
            edge_shape(plan, plan.inner),
        ],
        compiler_params=params(),
        name="first_edges",
    )(state)


def interp_kernel(plan, section, place, offsets, weights, got, out, spread):
    full = plan.cycle * plan.sectors
    row, sector = place[0], place[1]
    up = sector < plan.half
    at = jnp.where(up, jnp.minimum(row, offsets.shape[1] - 1), jnp.maximum(row - 1, 0))
    offset = offsets[section, at]
    offset = jnp.where(up, offset, lax.rem(full - offset, full))
    turn = offset // plan.cycle
    cell = lax.rem(offset, plan.cycle)
    matrix = weights[cell]
    for k in range(2 * plan.cycle):
        spread[k] = jnp.broadcast_to(matrix[:, k : k + 1], (plan.cycle, plan.radial))
    for target in range(plan.sectors):
        here = lax.rem(target + turn, plan.sectors)
        after = lax.rem(target + turn + 1, plan.sectors)
        for slot in range(plan.per):
            total = None
            for k in range(2 * plan.cycle):
                cell_at = k % plan.cycle
                row_value = got[here if k < plan.cycle else after, slot, cell_at : cell_at + 1, :]
                term = spread[k] * jnp.broadcast_to(row_value, (plan.cycle, plan.radial))
                total = term if total is None else total + term
            out[target, slot] = total


def interp(plan, section, place, offsets, weights, got):
    return pl.pallas_call(
        functools.partial(interp_kernel, plan, section),
        in_specs=[whole(SMEM), whole(SMEM), whole(VMEM), whole(VMEM)],
        out_specs=whole(VMEM),
        out_shape=jax.ShapeDtypeStruct(got.shape, jnp.float32),
        scratch_shapes=[pltpu.VMEM((2 * plan.cycle, plan.cycle, plan.radial), jnp.float32)],
        compiler_params=params(),
        name="interpolate",
    )(place, offsets, weights, got)


def coefficients(plan, speed, swirl, diffusion, coupling):
    twelfth = 1.0 / 12.0
    w = swirl[0]
    table = []
    for f in range(plan.fields):
        v, d = speed[f], diffusion[f]
        axial = ((-v - d) * twelfth, (8.0 * v + 16.0 * d) * twelfth, (16.0 * d - 8.0 * v) * twelfth, (v - d) * twelfth)
        cycle = ((-w - d) * twelfth, (8.0 * w + 16.0 * d) * twelfth, (16.0 * d - 8.0 * w) * twelfth, (w - d) * twelfth)
        mix = [coupling[f, e] - 7.0 * d if e == f else coupling[f, e] for e in range(plan.fields)]
        table.append((axial, cycle, d, mix))
    return table


def stage_kernel(plan, stage, outer, speed, swirl, diffusion, coupling, *refs):
    refs = list(refs)
    ranges = plan.outer if outer else plan.inner
    state = refs.pop(0)
    if stage == 0:
        chunks = {"state": state}
    else:
        chunks = {"outer": refs.pop(0), "inner": refs.pop(0)}
    ghosts = refs.pop(0) if outer else None
    low_in, high_in = refs.pop(0), refs.pop(0)
    if stage == 3:
        older = (refs.pop(0), refs.pop(0))
        if not outer:
            refs.pop(0)
        out_any = refs.pop(0)
        out_buf, sem, work, spread = refs
    else:
        out = refs.pop(0)
        low_out, high_out = refs.pop(0), refs.pop(0)
        b_out = refs.pop(0) if outer else None
        work, spread = refs
    cycle, radial = plan.cycle, plan.radial
    terms = plan.fields + 9
    for f, (axial, around, d, mix) in enumerate(coefficients(plan, speed, swirl, diffusion, coupling)):
        for number, factor in enumerate((d, *mix, *axial, *around)):
            spread[f * terms + number] = jnp.full((8, radial), factor, jnp.float32)
    lane = lax.broadcasted_iota(jnp.int32, (8, radial), 1)
    not_first = lane > 0
    not_last = lane < radial - 1

    def source(at):
        if at < 0:
            return ghosts, 0, at + 2
        if at >= plan.axial:
            return ghosts, 1, at - plan.axial
        if stage == 0:
            return state, None, at
        start = 0
        for low, high in plan.outer:
            if low <= at < high:
                return chunks["outer"], None, start + at - low
            start += high - low
        return chunks["inner"], None, at - plan.inner[0][0]

    def fill(field, at, to):
        ref, side, place = source(at)
        if side is not None:
            piece, slot = plan.combo(side, field, place)
            work[field, to, LOW : LOW + cycle, :] = ref[piece, slot]
        else:
            work[field, to, LOW : LOW + cycle, :] = ref[field, place]

    begin = 0
    for low, high in ranges:
        size = high - low
        for field in range(plan.fields):
            for at, to in ((low - 2, 0), (low - 1, 1), (high, size + 2), (high + 1, size + 3)):
                fill(field, at, to)
        ref, _, first_place = source(low)

        def copy(tile, carry, ref=ref, first_place=first_place, begin=begin):
            for field in range(plan.fields):
                for step in range(4):
                    place = tile * 4 + step
                    work[field, place + 2, LOW : LOW + cycle, :] = ref[field, first_place + place]
                    work[field, place + 2, LOW - 2 : LOW, :] = low_in[field, begin // 4 + tile, 2 * step : 2 * step + 2, :]
                    work[field, place + 2, LOW + cycle : LOW + cycle + 2, :] = high_in[
                        field, begin // 4 + tile, 2 * step : 2 * step + 2, :
                    ]
            return carry

        lax.fori_loop(0, size // 4, copy, 0)

        def compute(tile, carry, low=low, begin=begin):
            for f in range(plan.fields):
                factors = [spread[f * terms + number] for number in range(terms)]
                values = {}
                for step in range(4):
                    at = tile * 4 + step + 2
                    for row in range(0, cycle, 8):
                        here = slice(LOW + row, LOW + row + 8)
                        center = work[f, at, here, :]
                        left = jnp.where(not_first, pltpu.roll(center, 1, 1), 0.0)
                        right = jnp.where(not_last, pltpu.roll(center, radial - 1, 1), 0.0)
                        total = factors[0] * (left + right)
                        for e in range(plan.fields):
                            total += factors[1 + e] * (center if e == f else work[e, at, here, :])
                        for number, by in enumerate((-2, -1, 1, 2)):
                            total += factors[1 + plan.fields + number] * work[f, at + by, here, :]
                            total += factors[5 + plan.fields + number] * work[f, at, LOW + row + by : LOW + row + by + 8, :]
                        place = begin + tile * 4 + step
                        base = state[f, low + tile * 4 + step, row : row + 8, :]
                        if stage == 3:
                            second, third = older
                            kept = second[f, place, row : row + 8, :] + 2.0 * third[f, place, row : row + 8, :]
                            value = (kept + center - base) * (1.0 / 3.0) + (time_step / 6.0) * total
                        else:
                            value = base + (time_step if stage == 2 else 0.5 * time_step) * total
                        values[step, row] = value
                for (step, row), value in values.items():
                    place = begin + tile * 4 + step
                    if stage == 3:
                        out_buf[f, place, row : row + 8, :] = value
                        continue
                    out[f, place, row : row + 8, :] = value
                    if row == 0:
                        low_out[f, begin // 4 + tile, 2 * step : 2 * step + 2, :] = value[:2]
                    if row == cycle - 8:
                        high_out[f, begin // 4 + tile, 2 * step : 2 * step + 2, :] = value[6:]
            return carry

        lax.fori_loop(0, size // 4, compute, 0)
        begin += size

    if stage == 3:
        begin = 0
        copies = []
        for number, (low, high) in enumerate(ranges):
            copies.append(
                pltpu.make_async_copy(
                    out_buf.at[:, begin : begin + high - low], out_any.at[:, low:high], sem.at[number]
                )
            )
            copies[-1].start()
            begin += high - low
        for item in copies:
            item.wait()
    elif outer:
        total = count(ranges)
        for field in range(plan.fields):
            for plane in range(2):
                piece, slot = plan.combo(0, field, plane)
                b_out[piece, slot] = out[field, total - 2 + plane]
                piece, slot = plan.combo(1, field, plane)
                b_out[piece, slot] = out[field, plane]


def stage_call(plan, stage, outer, scalars, state, chunks, ghosts, halos, older=None, whole_out=None):
    ranges = plan.outer if outer else plan.inner
    planes = count(ranges)
    operands = [*scalars, state]
    if stage > 0:
        operands += list(chunks)
    if outer:
        operands.append(ghosts)
    operands += list(halos)
    specs = [whole(SMEM)] * len(scalars) + [whole(VMEM)] * (len(operands) - len(scalars))
    chunk = jax.ShapeDtypeStruct((plan.fields, planes, plan.cycle, plan.radial), jnp.float32)
    longest = max(high - low for low, high in ranges)
    scratch = [
        pltpu.VMEM((plan.fields, longest + 4, plan.cycle + 16, plan.radial), jnp.float32),
        pltpu.VMEM((plan.fields * (plan.fields + 9), 8, plan.radial), jnp.float32),
    ]
    aliases = {}
    if stage == 3:
        operands += list(older)
        specs += [whole(VMEM)] * 2
        if whole_out is not None:
            aliases = {len(operands): 0}
            operands.append(whole_out)
            specs.append(whole(pl.ANY))
        out_shape = [jax.ShapeDtypeStruct(state.shape, jnp.float32)]
        out_specs = [whole(pl.ANY)]
        scratch = [pltpu.VMEM(chunk.shape, jnp.float32), pltpu.SemaphoreType.DMA((len(ranges),))] + scratch
    else:
        out_shape = [chunk, edge_shape(plan, ranges), edge_shape(plan, ranges)]
        if outer:
            out_shape.append(
                jax.ShapeDtypeStruct((plan.sectors, plan.per, plan.cycle, plan.radial), jnp.float32)
            )
        out_specs = [whole(VMEM)] * len(out_shape)
    return pl.pallas_call(
        functools.partial(stage_kernel, plan, stage, outer),
        in_specs=specs,
        out_specs=out_specs,
        out_shape=out_shape,
        scratch_shapes=scratch,
        input_output_aliases=aliases,
        compiler_params=params(),
        name=f"stage{stage}_{'outer' if outer else 'inner'}",
    )(*operands)


def exchange(edges):
    size = lax.axis_size("sector")
    ahead = [(i, (i + 1) % size) for i in range(size)]
    back = [(i, (i - 1) % size) for i in range(size)]
    low_edges, high_edges = edges
    return lax.ppermute(high_edges, "sector", ahead), lax.ppermute(low_edges, "sector", back)


def row_hop(plan, value):
    rows, sectors = lax.axis_size("row"), plan.sectors
    pairs = []
    for row in range(rows):
        for sector in range(sectors):
            target = row + 1 if sector < plan.half else row - 1
            if 0 <= target < rows:
                pairs.append((row * sectors + sector, target * sectors + sector))
    return lax.ppermute(value, ("row", "sector"), pairs)


def on_device(state, interp_blocks, rotor_offset, axial_speed, row_swirl, diffusivity, coupling):
    plan = Plan(state, lax.axis_size("sector"))
    place = jnp.stack([lax.axis_index("row"), lax.axis_index("sector")]).astype(jnp.int32)
    scalars = (axial_speed, row_swirl, diffusivity, coupling)

    def ghosts_of(section, planes):
        got = lax.all_to_all(planes, "sector", 0, 0, tiled=True)
        made = interp(plan, section, place, rotor_offset, interp_blocks, got)
        return lax.all_to_all(row_hop(plan, made), "sector", 0, 0, tiled=True)

    planes, lo_o, hi_o, lo_i, hi_i = first(plan, state)
    chunks = None
    history = []
    outer_edges, inner_edges = (lo_o, hi_o), (lo_i, hi_i)
    for stage in range(4):
        outer_halos = exchange(outer_edges)
        inner_halos = exchange(inner_edges)
        ghosts = ghosts_of(stage, planes)
        if stage < 3:
            out_o, lo_o, hi_o, planes = stage_call(
                plan, stage, True, scalars, state, chunks, ghosts, outer_halos
            )
            out_i, lo_i, hi_i = stage_call(
                plan, stage, False, scalars, state, chunks, None, inner_halos
            )
            chunks = (out_o, out_i)
            history.append(chunks)
            outer_edges, inner_edges = (lo_o, hi_o), (lo_i, hi_i)
        else:
            older = history[0], history[1]
            (part,) = stage_call(
                plan, stage, True, scalars, state, chunks, ghosts, outer_halos, (older[0][0], older[1][0])
            )
            (result,) = stage_call(
                plan, stage, False, scalars, state, chunks, None, inner_halos, (older[0][1], older[1][1]), part
            )
    return result


def solution(mesh):
    return jax.shard_map(
        on_device,
        mesh=mesh,
        in_specs=(P(None, "row", "sector", None), P(), P(), P(), P("row"), P(), P()),
        out_specs=P(None, "row", "sector", None),
        check_vma=False,
    )
```

```python
import functools

import jax
import jax.numpy as jnp
from jax import lax
from jax.experimental import pallas as pl
from jax.experimental.pallas import tpu as pltpu
from jax.sharding import PartitionSpec as P

time_step = 0.4
highest = lax.Precision.HIGHEST
VMEM = pltpu.VMEM
SMEM = pltpu.SMEM
LOW = 8


def whole(space):
    return pl.BlockSpec(memory_space=space)


def held(shape):
    return pltpu.VMEM(tuple(shape), jnp.float32)


def near(value):
    return pltpu.with_memory_space_constraint(value, pltpu.VMEM)


def params():
    return pltpu.CompilerParams(vmem_limit_bytes=16 * 1024 * 1024)


class Plan:
    def __init__(self, state, sectors):
        self.fields, self.axial, self.cycle, self.radial = state.shape
        self.sectors = sectors
        quarter = self.axial // 4
        self.outer = ((0, quarter), (self.axial - quarter, self.axial))
        self.inner = ((quarter, self.axial - quarter),)
        self.half = sectors // 2
        self.per = -(-2 * self.fields // self.half)
        self.piece = (self.per, self.cycle, self.radial)

    def combo(self, side, field, plane):
        place = side * self.per * self.half + field * 2 + plane
        return place // self.per, place % self.per


def count(ranges):
    return sum(high - low for low, high in ranges)


def write_edges(plan, value, field, place, low_ref, high_ref):
    tile, row = place
    low_ref[field, tile, row : row + 2, :] = value[:2]
    high_ref[field, tile, row : row + 2, :] = value[plan.cycle - 2 :]


def deal(plan, sector, buffer, pieces):
    for ahead, piece in enumerate(pieces):
        piece[...] = buffer[lax.rem(sector + ahead, plan.sectors)]


def gather_planes(plan, buffer, upper, lower):
    for field in range(plan.fields):
        for plane in range(2):
            piece, slot = plan.combo(0, field, plane)
            buffer[piece, slot] = upper(field, plane)
            piece, slot = plan.combo(1, field, plane)
            buffer[piece, slot] = lower(field, plane)


def clear_spare(plan, buffer):
    used = {plan.combo(side, field, plane) for side in range(2) for field in range(plan.fields) for plane in range(2)}
    for piece in range(plan.sectors):
        for slot in range(plan.per):
            if (piece, slot) not in used:
                buffer[piece, slot] = jnp.zeros((plan.cycle, plan.radial), jnp.float32)


def planes_kernel(plan, place, state, *refs):
    *pieces, buffer, planes, sems = refs
    copies = [
        pltpu.make_async_copy(state.at[:, plan.axial - 2 : plan.axial], planes.at[0], sems.at[0]),
        pltpu.make_async_copy(state.at[:, 0:2], planes.at[1], sems.at[1]),
    ]
    for item in copies:
        item.start()
    clear_spare(plan, buffer)
    for item in copies:
        item.wait()
    gather_planes(plan, buffer, lambda f, p: planes[0, f, p], lambda f, p: planes[1, f, p])
    deal(plan, place[1], buffer, pieces)


def first_planes(plan, place, state):
    return pl.pallas_call(
        functools.partial(planes_kernel, plan),
        in_specs=[whole(SMEM), whole(pl.ANY)],
        out_specs=[whole(VMEM)] * plan.sectors,
        out_shape=[held(plan.piece)] * plan.sectors,
        scratch_shapes=[
            held((plan.sectors, *plan.piece)),
            held((2, plan.fields, 2, plan.cycle, plan.radial)),
            pltpu.SemaphoreType.DMA((2,)),
        ],
        compiler_params=params(),
        name="first_planes",
    )(place, state)


def first_kernel(plan, state, lo_o, hi_o, lo_i, hi_i):
    for ranges, low_ref, high_ref in ((plan.outer, lo_o, hi_o), (plan.inner, lo_i, hi_i)):
        start = 0
        for low, high in ranges:

            def body(tile, carry, low=low, start=start, low_ref=low_ref, high_ref=high_ref):
                for field in range(plan.fields):
                    for step in range(4):
                        at = low + tile * 4 + step
                        low_ref[field, start + tile, 2 * step : 2 * step + 2, :] = state[field, at, 0:2, :]
                        high_ref[field, start + tile, 2 * step : 2 * step + 2, :] = state[
                            field, at, plan.cycle - 2 : plan.cycle, :
                        ]
                return carry

            lax.fori_loop(0, (high - low) // 4, body, 0)
            start += (high - low) // 4


def edge_shape(plan, ranges):
    return held((plan.fields, count(ranges) // 4, 8, plan.radial))


def first_edges(plan, state):
    return pl.pallas_call(
        functools.partial(first_kernel, plan),
        in_specs=[whole(VMEM)],
        out_specs=[whole(VMEM)] * 4,
        out_shape=[edge_shape(plan, ranges) for ranges in (plan.outer, plan.outer, plan.inner, plan.inner)],
        compiler_params=params(),
        name="first_edges",
    )(state)


def interp_kernel(plan, section, place, offsets, weights, *refs):
    *refs, ring, spread = refs
    pieces, outs = refs[: plan.sectors], refs[-plan.sectors :]
    full = plan.cycle * plan.sectors
    row, sector = place[0], place[1]
    up = sector < plan.half
    at = jnp.where(up, jnp.minimum(row, offsets.shape[1] - 1), jnp.maximum(row - 1, 0))
    offset = offsets[section, at]
    offset = jnp.where(up, offset, lax.rem(full - offset, full))
    turn = offset // plan.cycle
    cell = lax.rem(offset, plan.cycle)
    matrix = weights[cell]
    for k in range(2 * plan.cycle):
        spread[k] = jnp.broadcast_to(matrix[:, k : k + 1], (plan.cycle, plan.radial))
    for ahead, piece in enumerate(pieces):
        ring[lax.rem(sector + plan.sectors - ahead, plan.sectors)] = piece[...]
    for ahead, out in enumerate(outs):
        here = lax.rem(sector + ahead + turn, plan.sectors)
        after = lax.rem(here + 1, plan.sectors)
        for slot in range(plan.per):
            total = None
            for k in range(2 * plan.cycle):
                cell_at = k % plan.cycle
                row_value = ring[here if k < plan.cycle else after, slot, cell_at : cell_at + 1, :]
                term = spread[k] * jnp.broadcast_to(row_value, (plan.cycle, plan.radial))
                total = term if total is None else total + term
            out[slot] = total


def interp(plan, section, place, offsets, weights, pieces, after):
    operands = [place, offsets, weights, *map(near, pieces), *map(near, after)]
    return pl.pallas_call(
        functools.partial(interp_kernel, plan, section),
        in_specs=[whole(SMEM), whole(SMEM)] + [whole(VMEM)] * (len(operands) - 2),
        out_specs=[whole(VMEM)] * plan.sectors,
        out_shape=[held(plan.piece)] * plan.sectors,
        scratch_shapes=[
            held((plan.sectors, *plan.piece)),
            held((2 * plan.cycle, plan.cycle, plan.radial)),
        ],
        compiler_params=params(),
        name="interpolate",
    )(*operands)


def coefficients(plan, speed, swirl, diffusion, coupling):
    twelfth = 1.0 / 12.0
    w = swirl[0]
    table = []
    for f in range(plan.fields):
        v, d = speed[f], diffusion[f]
        axial = ((-v - d) * twelfth, (8.0 * v + 16.0 * d) * twelfth, (16.0 * d - 8.0 * v) * twelfth, (v - d) * twelfth)
        cycle = ((-w - d) * twelfth, (8.0 * w + 16.0 * d) * twelfth, (16.0 * d - 8.0 * w) * twelfth, (w - d) * twelfth)
        mix = [coupling[f, e] - 7.0 * d if e == f else coupling[f, e] for e in range(plan.fields)]
        table.append((axial, cycle, d, mix))
    return table


def stage_kernel(plan, stage, outer, speed, swirl, diffusion, coupling, *refs):
    refs = list(refs)
    take = lambda number: [refs.pop(0) for _ in range(number)]
    ranges = plan.outer if outer else plan.inner
    (state,) = take(1)
    chunks = {"state": state} if stage == 0 else dict(zip(("outer", "inner"), take(2)))
    low_in, high_in = take(2)
    if outer:
        (place,) = take(1)
        pieces = take(plan.sectors)
    else:
        take(1)
    if stage == 3:
        older = take(2)
        if not outer:
            take(1)
        (out_any,) = take(1)
        if outer:
            (token,) = take(1)
        out_buf, sem = take(2)
    else:
        out, low_out, high_out, token = take(4)
        if outer:
            pieces_out = take(plan.sectors)
    work, spread = take(2)
    if outer:
        (ghosts,) = take(1)
        for ahead, piece in enumerate(pieces):
            ghosts[lax.rem(place[1] + plan.sectors - ahead, plan.sectors)] = piece[...]
    cycle, radial = plan.cycle, plan.radial
    terms = plan.fields + 9
    for f, (axial, around, d, mix) in enumerate(coefficients(plan, speed, swirl, diffusion, coupling)):
        for number, factor in enumerate((d, *mix, *axial, *around)):
            spread[f * terms + number] = jnp.full((8, radial), factor, jnp.float32)
    lane = lax.broadcasted_iota(jnp.int32, (8, radial), 1)
    not_first = lane > 0
    not_last = lane < radial - 1

    def source(at):
        if at < 0:
            return ghosts, 0, at + 2
        if at >= plan.axial:
            return ghosts, 1, at - plan.axial
        if stage == 0:
            return state, None, at
        start = 0
        for low, high in plan.outer:
            if low <= at < high:
                return chunks["outer"], None, start + at - low
            start += high - low
        return chunks["inner"], None, at - plan.inner[0][0]

    def fill(field, at, to):
        ref, side, place = source(at)
        if side is not None:
            piece, slot = plan.combo(side, field, place)
            work[field, to, LOW : LOW + cycle, :] = ref[piece, slot]
        else:
            work[field, to, LOW : LOW + cycle, :] = ref[field, place]

    begin = 0
    for low, high in ranges:
        size = high - low
        for field in range(plan.fields):
            for at, to in ((low - 2, 0), (low - 1, 1), (high, size + 2), (high + 1, size + 3)):
                fill(field, at, to)
        ref, _, first_place = source(low)

        def copy(tile, carry, ref=ref, first_place=first_place, begin=begin):
            for field in range(plan.fields):
                for step in range(4):
                    place = tile * 4 + step
                    work[field, place + 2, LOW : LOW + cycle, :] = ref[field, first_place + place]
                    work[field, place + 2, LOW - 2 : LOW, :] = low_in[field, begin // 4 + tile, 2 * step : 2 * step + 2, :]
                    work[field, place + 2, LOW + cycle : LOW + cycle + 2, :] = high_in[
                        field, begin // 4 + tile, 2 * step : 2 * step + 2, :
                    ]
            return carry

        lax.fori_loop(0, size // 4, copy, 0)

        def compute(tile, carry, low=low, begin=begin):
            for f in range(plan.fields):
                factors = [spread[f * terms + number] for number in range(terms)]
                values = {}
                for step in range(4):
                    at = tile * 4 + step + 2
                    for row in range(0, cycle, 8):
                        here = slice(LOW + row, LOW + row + 8)
                        center = work[f, at, here, :]
                        left = jnp.where(not_first, pltpu.roll(center, 1, 1), 0.0)
                        right = jnp.where(not_last, pltpu.roll(center, radial - 1, 1), 0.0)
                        total = factors[0] * (left + right)
                        for e in range(plan.fields):
                            total += factors[1 + e] * (center if e == f else work[e, at, here, :])
                        for number, by in enumerate((-2, -1, 1, 2)):
                            total += factors[1 + plan.fields + number] * work[f, at + by, here, :]
                            total += factors[5 + plan.fields + number] * work[f, at, LOW + row + by : LOW + row + by + 8, :]
                        place = begin + tile * 4 + step
                        base = state[f, low + tile * 4 + step, row : row + 8, :]
                        if stage == 3:
                            second, third = older
                            kept = second[f, place, row : row + 8, :] + 2.0 * third[f, place, row : row + 8, :]
                            value = (kept + center - base) * (1.0 / 3.0) + (time_step / 6.0) * total
                        else:
                            value = base + (time_step if stage == 2 else 0.5 * time_step) * total
                        values[step, row] = value
                for (step, row), value in values.items():
                    place = begin + tile * 4 + step
                    if stage == 3:
                        out_buf[f, place, row : row + 8, :] = value
                        continue
                    out[f, place, row : row + 8, :] = value
                    if row == 0:
                        low_out[f, begin // 4 + tile, 2 * step : 2 * step + 2, :] = value[:2]
                    if row == cycle - 8:
                        high_out[f, begin // 4 + tile, 2 * step : 2 * step + 2, :] = value[6:]
            return carry

        lax.fori_loop(0, size // 4, compute, 0)
        begin += size

    if stage == 3:
        begin = 0
        copies = []
        for number, (low, high) in enumerate(ranges):
            copies.append(
                pltpu.make_async_copy(
                    out_buf.at[:, begin : begin + high - low], out_any.at[:, low:high], sem.at[number]
                )
            )
            copies[-1].start()
            begin += high - low
        for item in copies:
            item.wait()
    elif outer:
        total = count(ranges)
        clear_spare(plan, ghosts)
        gather_planes(plan, ghosts, lambda f, p: out[f, total - 2 + p], lambda f, p: out[f, p])
        deal(plan, place[1], ghosts, pieces_out)
    if stage < 3 or outer:
        token[...] = jnp.zeros(token.shape, jnp.float32)


def stage_call(plan, stage, outer, scalars, state, chunks, halos, extra, older=(), whole_out=None):
    ranges = plan.outer if outer else plan.inner
    chunk = (plan.fields, count(ranges), plan.cycle, plan.radial)
    longest = max(high - low for low, high in ranges)
    operands, specs = list(scalars), [whole(SMEM)] * len(scalars)

    def add(values):
        operands.extend(map(near, values))
        specs.extend([whole(VMEM)] * len(values))

    add([state, *(chunks or ()), *halos])
    if outer:
        operands.append(extra[0])
        specs.append(whole(SMEM))
        add(extra[1])
    else:
        add([extra])
    scratch = [
        held((plan.fields, longest + 4, plan.cycle + 16, plan.radial)),
        held((plan.fields * (plan.fields + 9), 8, plan.radial)),
    ]
    if outer:
        scratch.append(held((plan.sectors, *plan.piece)))
    aliases = {}
    token = held((8, plan.radial))
    if stage == 3:
        add(older)
        if whole_out is not None:
            aliases = {len(operands): 0}
            operands.append(whole_out)
            specs.append(whole(pl.ANY))
        out_shape = [jax.ShapeDtypeStruct(state.shape, jnp.float32)] + [token] * outer
        out_specs = [whole(pl.ANY)] + [whole(VMEM)] * outer
        scratch = [held(chunk), pltpu.SemaphoreType.DMA((len(ranges),))] + scratch
    else:
        out_shape = [held(chunk), edge_shape(plan, ranges), edge_shape(plan, ranges), token]
        if outer:
            out_shape += [held(plan.piece)] * plan.sectors
        out_specs = [whole(VMEM)] * len(out_shape)
    return pl.pallas_call(
        functools.partial(stage_kernel, plan, stage, outer),
        in_specs=specs,
        out_specs=out_specs,
        out_shape=out_shape,
        scratch_shapes=scratch,
        input_output_aliases=aliases,
        compiler_params=params(),
        name=f"stage{stage}_{'outer' if outer else 'inner'}",
    )(*operands)


def exchange(edges):
    size = lax.axis_size("sector")
    ahead = [(i, (i + 1) % size) for i in range(size)]
    back = [(i, (i - 1) % size) for i in range(size)]
    low_edges, high_edges = edges
    return lax.ppermute(high_edges, "sector", ahead), lax.ppermute(low_edges, "sector", back)


def send_within_row(plan, pieces):
    sent = [pieces[0]]
    for ahead in range(1, plan.sectors):
        route = [(i, (i + ahead) % plan.sectors) for i in range(plan.sectors)]
        sent.append(lax.ppermute(pieces[ahead], "sector", route))
    return sent


def send_to_next_row(plan, pieces):
    rows = lax.axis_size("row")
    sent = []
    for ahead in range(plan.sectors):
        route = []
        for row in range(rows):
            for sector in range(plan.sectors):
                target = row + 1 if sector < plan.half else row - 1
                if 0 <= target < rows:
                    to = target * plan.sectors + (sector + ahead) % plan.sectors
                    route.append((row * plan.sectors + sector, to))
        sent.append(lax.ppermute(pieces[ahead], ("row", "sector"), route))
    return sent


def on_device(state, interp_blocks, rotor_offset, axial_speed, row_swirl, diffusivity, coupling):
    plan = Plan(state, lax.axis_size("sector"))
    place = jnp.stack([lax.axis_index("row"), lax.axis_index("sector")]).astype(jnp.int32)
    scalars = (axial_speed, row_swirl, diffusivity, coupling)

    pieces = first_planes(plan, place, state)
    lo_o, hi_o, lo_i, hi_i = first_edges(plan, state)
    outer_edges, inner_edges = (lo_o, hi_o), (lo_i, hi_i)
    chunks, waited = None, ()
    history = []
    for stage in range(4):
        turned = send_within_row(plan, pieces)
        outer_halos = exchange(outer_edges)
        made = interp(plan, stage, place, rotor_offset, interp_blocks, turned, waited)
        ghosts = send_to_next_row(plan, made)
        inner_edges = lax.optimization_barrier((*inner_edges, made[0]))[:2]
        inner_halos = exchange(inner_edges)
        last = stage == 3
        older = [(history[0][i], history[1][i]) if last else () for i in range(2)]
        out_o, *rest = stage_call(
            plan, stage, True, scalars, state, chunks, outer_halos, (place, ghosts), older[0]
        )
        token = rest[0] if last else rest[2]
        out_i, *rest_i = stage_call(
            plan, stage, False, scalars, state, chunks, inner_halos, token, older[1], out_o if last else None
        )
        if last:
            return out_i
        outer_edges, pieces = rest[:2], rest[3:]
        inner_edges, waited = rest_i[:2], rest_i[2:]
        chunks = (out_o, out_i)
        history.append(chunks)


def solution(mesh):
    return jax.shard_map(
        on_device,
        mesh=mesh,
        in_specs=(P(None, "row", "sector", None), P(), P(), P(), P("row"), P(), P()),
        out_specs=P(None, "row", "sector", None),
        check_vma=False,
    )
```

```python
import functools

import jax
import jax.numpy as jnp
from jax import lax
from jax.experimental import pallas as pl
from jax.experimental.pallas import tpu as pltpu
from jax.sharding import PartitionSpec as P

time_step = 0.4
highest = lax.Precision.HIGHEST
VMEM = pltpu.VMEM
SMEM = pltpu.SMEM
LOW = 8


def whole(space):
    return pl.BlockSpec(memory_space=space)


def held(shape):
    return pltpu.VMEM(tuple(shape), jnp.float32)


def near(value):
    return pltpu.with_memory_space_constraint(value, pltpu.VMEM)


def params():
    return pltpu.CompilerParams(vmem_limit_bytes=16 * 1024 * 1024)


class Plan:
    def __init__(self, state, sectors):
        self.fields, self.axial, self.cycle, self.radial = state.shape
        self.sectors = sectors
        strip = self.axial // 4
        self.outer = ((0, strip), (self.axial - strip, self.axial))
        self.inner = ((strip, self.axial - strip),)
        self.half = sectors // 2
        self.per = -(-2 * self.fields // self.half)
        self.dealt = (sectors, self.per, self.cycle, self.radial)

    def combo(self, side, field, plane):
        place = side * self.per * self.half + field * 2 + plane
        return place // self.per, place % self.per


def count(ranges):
    return sum(high - low for low, high in ranges)


def write_edges(plan, value, field, place, low_ref, high_ref):
    tile, row = place
    low_ref[field, tile, row : row + 2, :] = value[:2]
    high_ref[field, tile, row : row + 2, :] = value[plan.cycle - 2 :]


def gather_planes(plan, buffer, upper, lower):
    for field in range(plan.fields):
        for plane in range(2):
            piece, slot = plan.combo(0, field, plane)
            buffer[piece, slot] = upper(field, plane)
            piece, slot = plan.combo(1, field, plane)
            buffer[piece, slot] = lower(field, plane)


def clear_spare(plan, buffer):
    used = {plan.combo(side, field, plane) for side in range(2) for field in range(plan.fields) for plane in range(2)}
    for piece in range(plan.sectors):
        for slot in range(plan.per):
            if (piece, slot) not in used:
                buffer[piece, slot] = jnp.zeros((plan.cycle, plan.radial), jnp.float32)


def planes_kernel(plan, state, dealt, planes, sems):
    copies = [
        pltpu.make_async_copy(state.at[:, plan.axial - 2 : plan.axial], planes.at[0], sems.at[0]),
        pltpu.make_async_copy(state.at[:, 0:2], planes.at[1], sems.at[1]),
    ]
    for item in copies:
        item.start()
    clear_spare(plan, dealt)
    for item in copies:
        item.wait()
    gather_planes(plan, dealt, lambda f, p: planes[0, f, p], lambda f, p: planes[1, f, p])


def first_planes(plan, state):
    return pl.pallas_call(
        functools.partial(planes_kernel, plan),
        in_specs=[whole(pl.ANY)],
        out_specs=whole(VMEM),
        out_shape=held(plan.dealt),
        scratch_shapes=[
            held((2, plan.fields, 2, plan.cycle, plan.radial)),
            pltpu.SemaphoreType.DMA((2,)),
        ],
        compiler_params=params(),
        name="first_planes",
    )(state)


def first_kernel(plan, state, lo_o, hi_o, lo_i, hi_i):
    for ranges, low_ref, high_ref in ((plan.outer, lo_o, hi_o), (plan.inner, lo_i, hi_i)):
        start = 0
        for low, high in ranges:

            def body(tile, carry, low=low, start=start, low_ref=low_ref, high_ref=high_ref):
                for field in range(plan.fields):
                    for step in range(4):
                        at = low + tile * 4 + step
                        low_ref[field, start + tile, 2 * step : 2 * step + 2, :] = state[field, at, 0:2, :]
                        high_ref[field, start + tile, 2 * step : 2 * step + 2, :] = state[
                            field, at, plan.cycle - 2 : plan.cycle, :
                        ]
                return carry

            lax.fori_loop(0, (high - low) // 4, body, 0)
            start += (high - low) // 4


def edge_shape(plan, ranges):
    return held((plan.fields, count(ranges) // 4, 8, plan.radial))


def first_edges(plan, state):
    return pl.pallas_call(
        functools.partial(first_kernel, plan),
        in_specs=[whole(VMEM)],
        out_specs=[whole(VMEM)] * 4,
        out_shape=[edge_shape(plan, ranges) for ranges in (plan.outer, plan.outer, plan.inner, plan.inner)],
        compiler_params=params(),
        name="first_edges",
    )(state)


def interp_kernel(plan, section, place, offsets, weights, ring, *refs):
    *_, out, spread = refs
    full = plan.cycle * plan.sectors
    row, sector = place[0], place[1]
    up = sector < plan.half
    at = jnp.where(up, jnp.minimum(row, offsets.shape[1] - 1), jnp.maximum(row - 1, 0))
    offset = offsets[section, at]
    offset = jnp.where(up, offset, lax.rem(full - offset, full))
    turn = offset // plan.cycle
    cell = lax.rem(offset, plan.cycle)
    matrix = weights[cell]
    for k in range(2 * plan.cycle):
        spread[k] = jnp.broadcast_to(matrix[:, k : k + 1], (plan.cycle, plan.radial))
    for target in range(plan.sectors):
        here = lax.rem(target + turn, plan.sectors)
        after = lax.rem(here + 1, plan.sectors)
        for slot in range(plan.per):
            total = None
            for k in range(2 * plan.cycle):
                cell_at = k % plan.cycle
                row_value = ring[here if k < plan.cycle else after, slot, cell_at : cell_at + 1, :]
                term = spread[k] * jnp.broadcast_to(row_value, (plan.cycle, plan.radial))
                total = term if total is None else total + term
            out[target, slot] = total


def interp(plan, section, place, offsets, weights, got, after):
    operands = [place, offsets, weights, near(got), *map(near, after)]
    return pl.pallas_call(
        functools.partial(interp_kernel, plan, section),
        in_specs=[whole(SMEM), whole(SMEM)] + [whole(VMEM)] * (len(operands) - 2),
        out_specs=whole(VMEM),
        out_shape=held(plan.dealt),
        scratch_shapes=[held((2 * plan.cycle, plan.cycle, plan.radial))],
        compiler_params=params(),
        name="interpolate",
    )(*operands)


def coefficients(plan, speed, swirl, diffusion, coupling):
    twelfth = 1.0 / 12.0
    w = swirl[0]
    table = []
    for f in range(plan.fields):
        v, d = speed[f], diffusion[f]
        axial = ((-v - d) * twelfth, (8.0 * v + 16.0 * d) * twelfth, (16.0 * d - 8.0 * v) * twelfth, (v - d) * twelfth)
        cycle = ((-w - d) * twelfth, (8.0 * w + 16.0 * d) * twelfth, (16.0 * d - 8.0 * w) * twelfth, (w - d) * twelfth)
        mix = [coupling[f, e] - 7.0 * d if e == f else coupling[f, e] for e in range(plan.fields)]
        table.append((axial, cycle, d, mix))
    return table


def stage_kernel(plan, stage, outer, speed, swirl, diffusion, coupling, *refs):
    refs = list(refs)
    take = lambda number: [refs.pop(0) for _ in range(number)]
    ranges = plan.outer if outer else plan.inner
    (state,) = take(1)
    chunks = {"state": state} if stage == 0 else dict(zip(("outer", "inner"), take(2)))
    low_in, high_in = take(2)
    if outer:
        (ghosts,) = take(1)
    else:
        take(1)
    if stage == 3:
        older = take(2)
        if not outer:
            take(1)
        (out_any,) = take(1)
        if outer:
            (token,) = take(1)
        out_buf, sem = take(2)
    else:
        out, low_out, high_out, token = take(4)
        if outer:
            (dealt,) = take(1)
    work, spread = take(2)
    cycle, radial = plan.cycle, plan.radial
    terms = plan.fields + 9
    for f, (axial, around, d, mix) in enumerate(coefficients(plan, speed, swirl, diffusion, coupling)):
        for number, factor in enumerate((d, *mix, *axial, *around)):
            spread[f * terms + number] = jnp.full((8, radial), factor, jnp.float32)
    lane = lax.broadcasted_iota(jnp.int32, (8, radial), 1)
    not_first = lane > 0
    not_last = lane < radial - 1

    def source(at):
        if at < 0:
            return ghosts, 0, at + 2
        if at >= plan.axial:
            return ghosts, 1, at - plan.axial
        if stage == 0:
            return state, None, at
        start = 0
        for low, high in plan.outer:
            if low <= at < high:
                return chunks["outer"], None, start + at - low
            start += high - low
        return chunks["inner"], None, at - plan.inner[0][0]

    def fill(field, at, to):
        ref, side, place = source(at)
        if side is not None:
            piece, slot = plan.combo(side, field, place)
            work[field, to, LOW : LOW + cycle, :] = ref[piece, slot]
        else:
            work[field, to, LOW : LOW + cycle, :] = ref[field, place]

    begin = 0
    for low, high in ranges:
        size = high - low
        for field in range(plan.fields):
            for at, to in ((low - 2, 0), (low - 1, 1), (high, size + 2), (high + 1, size + 3)):
                fill(field, at, to)
        ref, _, first_place = source(low)

        def copy(tile, carry, ref=ref, first_place=first_place, begin=begin):
            for field in range(plan.fields):
                for step in range(4):
                    place = tile * 4 + step
                    work[field, place + 2, LOW : LOW + cycle, :] = ref[field, first_place + place]
                    work[field, place + 2, LOW - 2 : LOW, :] = low_in[field, begin // 4 + tile, 2 * step : 2 * step + 2, :]
                    work[field, place + 2, LOW + cycle : LOW + cycle + 2, :] = high_in[
                        field, begin // 4 + tile, 2 * step : 2 * step + 2, :
                    ]
            return carry

        lax.fori_loop(0, size // 4, copy, 0)

        def compute(tile, carry, low=low, begin=begin):
            for f in range(plan.fields):
                factors = [spread[f * terms + number] for number in range(terms)]
                values = {}
                for step in range(4):
                    at = tile * 4 + step + 2
                    for row in range(0, cycle, 8):
                        here = slice(LOW + row, LOW + row + 8)
                        center = work[f, at, here, :]
                        left = jnp.where(not_first, pltpu.roll(center, 1, 1), 0.0)
                        right = jnp.where(not_last, pltpu.roll(center, radial - 1, 1), 0.0)
                        total = factors[0] * (left + right)
                        for e in range(plan.fields):
                            total += factors[1 + e] * (center if e == f else work[e, at, here, :])
                        for number, by in enumerate((-2, -1, 1, 2)):
                            total += factors[1 + plan.fields + number] * work[f, at + by, here, :]
                            total += factors[5 + plan.fields + number] * work[f, at, LOW + row + by : LOW + row + by + 8, :]
                        place = begin + tile * 4 + step
                        base = state[f, low + tile * 4 + step, row : row + 8, :]
                        if stage == 3:
                            second, third = older
                            kept = second[f, place, row : row + 8, :] + 2.0 * third[f, place, row : row + 8, :]
                            value = (kept + center - base) * (1.0 / 3.0) + (time_step / 6.0) * total
                        else:
                            value = base + (time_step if stage == 2 else 0.5 * time_step) * total
                        values[step, row] = value
                for (step, row), value in values.items():
                    place = begin + tile * 4 + step
                    if stage == 3:
                        out_buf[f, place, row : row + 8, :] = value
                        continue
                    out[f, place, row : row + 8, :] = value
                    if row == 0:
                        low_out[f, begin // 4 + tile, 2 * step : 2 * step + 2, :] = value[:2]
                    if row == cycle - 8:
                        high_out[f, begin // 4 + tile, 2 * step : 2 * step + 2, :] = value[6:]
            return carry

        lax.fori_loop(0, size // 4, compute, 0)
        begin += size

    if stage == 3:
        begin = 0
        copies = []
        for number, (low, high) in enumerate(ranges):
            copies.append(
                pltpu.make_async_copy(
                    out_buf.at[:, begin : begin + high - low], out_any.at[:, low:high], sem.at[number]
                )
            )
            copies[-1].start()
            begin += high - low
        for item in copies:
            item.wait()
    elif outer:
        total = count(ranges)
        clear_spare(plan, dealt)
        gather_planes(plan, dealt, lambda f, p: out[f, total - 2 + p], lambda f, p: out[f, p])
    if stage < 3 or outer:
        token[...] = jnp.zeros(token.shape, jnp.float32)


def stage_call(plan, stage, outer, scalars, state, chunks, halos, extra, older=(), whole_out=None):
    ranges = plan.outer if outer else plan.inner
    chunk = (plan.fields, count(ranges), plan.cycle, plan.radial)
    longest = max(high - low for low, high in ranges)
    operands, specs = list(scalars), [whole(SMEM)] * len(scalars)

    def add(values):
        operands.extend(map(near, values))
        specs.extend([whole(VMEM)] * len(values))

    add([state, *(chunks or ()), *halos, extra])
    scratch = [
        held((plan.fields, longest + 4, plan.cycle + 16, plan.radial)),
        held((plan.fields * (plan.fields + 9), 8, plan.radial)),
    ]
    aliases = {}
    token = held((8, plan.radial))
    if stage == 3:
        add(older)
        if whole_out is not None:
            aliases = {len(operands): 0}
            operands.append(whole_out)
            specs.append(whole(pl.ANY))
        out_shape = [jax.ShapeDtypeStruct(state.shape, jnp.float32)] + [token] * outer
        out_specs = [whole(pl.ANY)] + [whole(VMEM)] * outer
        scratch = [held(chunk), pltpu.SemaphoreType.DMA((len(ranges),))] + scratch
    else:
        out_shape = [held(chunk), edge_shape(plan, ranges), edge_shape(plan, ranges), token]
        if outer:
            out_shape.append(held(plan.dealt))
        out_specs = [whole(VMEM)] * len(out_shape)
    return pl.pallas_call(
        functools.partial(stage_kernel, plan, stage, outer),
        in_specs=specs,
        out_specs=out_specs,
        out_shape=out_shape,
        scratch_shapes=scratch,
        input_output_aliases=aliases,
        compiler_params=params(),
        name=f"stage{stage}_{'outer' if outer else 'inner'}",
    )(*operands)


def exchange(edges):
    size = lax.axis_size("sector")
    ahead = [(i, (i + 1) % size) for i in range(size)]
    back = [(i, (i - 1) % size) for i in range(size)]
    low_edges, high_edges = edges
    return lax.ppermute(high_edges, "sector", ahead), lax.ppermute(low_edges, "sector", back)


def row_hop(plan, value):
    rows = lax.axis_size("row")
    route = []
    for row in range(rows):
        for sector in range(plan.sectors):
            target = row + 1 if sector < plan.half else row - 1
            if 0 <= target < rows:
                route.append((row * plan.sectors + sector, target * plan.sectors + sector))
    return lax.ppermute(value, ("row", "sector"), route)


def on_device(state, interp_blocks, rotor_offset, axial_speed, row_swirl, diffusivity, coupling):
    plan = Plan(state, lax.axis_size("sector"))
    place = jnp.stack([lax.axis_index("row"), lax.axis_index("sector")]).astype(jnp.int32)
    scalars = (axial_speed, row_swirl, diffusivity, coupling)

    dealt = first_planes(plan, state)
    lo_o, hi_o, lo_i, hi_i = first_edges(plan, state)
    outer_edges, inner_edges = (lo_o, hi_o), (lo_i, hi_i)
    chunks, waited = None, ()
    history = []
    for stage in range(4):
        got = lax.all_to_all(dealt, "sector", 0, 0, tiled=True)
        outer_halos = exchange(outer_edges)
        made = interp(plan, stage, place, rotor_offset, interp_blocks, got, waited)
        hopped = row_hop(plan, made)
        ghosts = lax.all_to_all(hopped, "sector", 0, 0, tiled=True)
        inner_edges = lax.optimization_barrier((*inner_edges, ghosts))[:2]
        inner_halos = exchange(inner_edges)
        last = stage == 3
        older = [(history[0][i], history[1][i]) if last else () for i in range(2)]
        out_o, *rest = stage_call(plan, stage, True, scalars, state, chunks, outer_halos, ghosts, older[0])
        token = rest[0] if last else rest[2]
        out_i, *rest_i = stage_call(
            plan, stage, False, scalars, state, chunks, inner_halos, token, older[1], out_o if last else None
        )
        if last:
            return out_i
        outer_edges, dealt = rest[:2], rest[3]
        inner_edges, waited = rest_i[:2], rest_i[2:]
        chunks = (out_o, out_i)
        history.append(chunks)


def solution(mesh):
    return jax.shard_map(
        on_device,
        mesh=mesh,
        in_specs=(P(None, "row", "sector", None), P(), P(), P(), P("row"), P(), P()),
        out_specs=P(None, "row", "sector", None),
        check_vma=False,
    )
```

```python
import functools

import jax
import jax.numpy as jnp
from jax import lax
from jax.experimental import pallas as pl
from jax.experimental.pallas import tpu as pltpu
from jax.sharding import PartitionSpec as P

time_step = 0.4
highest = lax.Precision.HIGHEST
VMEM = pltpu.VMEM
SMEM = pltpu.SMEM
LOW = 8


def whole(space):
    return pl.BlockSpec(memory_space=space)


def held(shape):
    return pltpu.VMEM(tuple(shape), jnp.float32)


def near(value):
    return pltpu.with_memory_space_constraint(value, pltpu.VMEM)


def params():
    return pltpu.CompilerParams(vmem_limit_bytes=16 * 1024 * 1024)


class Plan:
    def __init__(self, state, rows, sectors):
        self.fields, self.axial, self.cycle, self.radial = state.shape
        self.sectors = sectors
        strip = self.axial // 4
        self.outer = ((0, strip), (self.axial - strip, self.axial))
        self.inner = ((strip, self.axial - strip),)
        self.rows = rows
        self.ghost = (self.fields, 2, self.cycle, self.radial)


def count(ranges):
    return sum(high - low for low, high in ranges)


def write_edges(plan, value, field, place, low_ref, high_ref):
    tile, row = place
    low_ref[field, tile, row : row + 2, :] = value[:2]
    high_ref[field, tile, row : row + 2, :] = value[plan.cycle - 2 :]


def planes_kernel(plan, place, state, *refs):
    *sent, planes, sems = refs
    copies = [
        pltpu.make_async_copy(state.at[:, 0:2], planes.at[0], sems.at[0]),
        pltpu.make_async_copy(state.at[:, plan.axial - 2 : plan.axial], planes.at[1], sems.at[1]),
    ]
    for item in copies:
        item.start()
    for item in copies:
        item.wait()
    for interface, out in enumerate(sent):
        out[...] = planes[jnp.where(place[0] == interface, 1, 0)]


def first_planes(plan, place, state):
    return pl.pallas_call(
        functools.partial(planes_kernel, plan),
        in_specs=[whole(SMEM), whole(pl.ANY)],
        out_specs=[whole(VMEM)] * (plan.rows - 1),
        out_shape=[held(plan.ghost)] * (plan.rows - 1),
        scratch_shapes=[held((2, *plan.ghost)), pltpu.SemaphoreType.DMA((2,))],
        compiler_params=params(),
        name="first_planes",
    )(place, state)


def first_kernel(plan, state, lo_o, hi_o, lo_i, hi_i):
    for ranges, low_ref, high_ref in ((plan.outer, lo_o, hi_o), (plan.inner, lo_i, hi_i)):
        start = 0
        for low, high in ranges:

            def body(tile, carry, low=low, start=start, low_ref=low_ref, high_ref=high_ref):
                for field in range(plan.fields):
                    for step in range(4):
                        at = low + tile * 4 + step
                        low_ref[field, start + tile, 2 * step : 2 * step + 2, :] = state[field, at, 0:2, :]
                        high_ref[field, start + tile, 2 * step : 2 * step + 2, :] = state[
                            field, at, plan.cycle - 2 : plan.cycle, :
                        ]
                return carry

            lax.fori_loop(0, (high - low) // 4, body, 0)
            start += (high - low) // 4


def edge_shape(plan, ranges):
    return held((plan.fields, count(ranges) // 4, 8, plan.radial))


def first_edges(plan, state):
    return pl.pallas_call(
        functools.partial(first_kernel, plan),
        in_specs=[whole(VMEM)],
        out_specs=[whole(VMEM)] * 4,
        out_shape=[edge_shape(plan, ranges) for ranges in (plan.outer, plan.outer, plan.inner, plan.inner)],
        compiler_params=params(),
        name="first_edges",
    )(state)


def make_ghosts(plan, section, row, offsets, weights, pairs, ghosts, near_pair, spread):
    full = plan.cycle * plan.sectors
    for side in range(2):
        near_pair[...] = jnp.zeros(near_pair.shape, jnp.float32)
        interface = row - 1 if side == 0 else row
        for number in range(plan.rows - 1):

            @pl.when(interface == number)
            def _(number=number):
                first, second = pairs[2 * number], pairs[2 * number + 1]
                near_pair[:, :, : plan.cycle, :] = first[...]
                near_pair[:, :, plan.cycle :, :] = second[...]

        offset = offsets[section, jnp.clip(interface, 0, plan.rows - 2)]
        if side == 1:
            offset = lax.rem(full - offset, full)
        matrix = weights[lax.rem(offset, plan.cycle)]
        for k in range(2 * plan.cycle):
            spread[k] = jnp.broadcast_to(matrix[:, k : k + 1], (plan.cycle, plan.radial))
        for field in range(plan.fields):
            for plane in range(2):
                total = None
                for k in range(2 * plan.cycle):
                    value = near_pair[field, plane, k : k + 1, :]
                    term = spread[k] * jnp.broadcast_to(value, (plan.cycle, plan.radial))
                    total = term if total is None else total + term
                ghosts[side, field, plane] = total


def coefficients(plan, speed, swirl, diffusion, coupling):
    twelfth = 1.0 / 12.0
    w = swirl[0]
    table = []
    for f in range(plan.fields):
        v, d = speed[f], diffusion[f]
        axial = ((-v - d) * twelfth, (8.0 * v + 16.0 * d) * twelfth, (16.0 * d - 8.0 * v) * twelfth, (v - d) * twelfth)
        cycle = ((-w - d) * twelfth, (8.0 * w + 16.0 * d) * twelfth, (16.0 * d - 8.0 * w) * twelfth, (w - d) * twelfth)
        mix = [coupling[f, e] - 7.0 * d if e == f else coupling[f, e] for e in range(plan.fields)]
        table.append((axial, cycle, d, mix))
    return table


def stage_kernel(plan, stage, outer, speed, swirl, diffusion, coupling, *refs):
    refs = list(refs)
    take = lambda number: [refs.pop(0) for _ in range(number)]
    ranges = plan.outer if outer else plan.inner
    (state,) = take(1)
    chunks = {"state": state} if stage == 0 else dict(zip(("outer", "inner"), take(2)))
    low_in, high_in = take(2)
    if outer:
        place, offsets, weights = take(3)
        pairs = take(2 * (plan.rows - 1))
    else:
        take(1)
    if stage == 3:
        older = take(2)
        if not outer:
            take(1)
        (out_any,) = take(1)
        if outer:
            (token,) = take(1)
        out_buf, sem = take(2)
    else:
        out, low_out, high_out, token = take(4)
        if outer:
            sent = take(plan.rows - 1)
    work, spread = take(2)
    if outer:
        ghosts, near_pair, weight_spread = take(3)
        make_ghosts(plan, stage, place[0], offsets, weights, pairs, ghosts, near_pair, weight_spread)
    cycle, radial = plan.cycle, plan.radial
    terms = plan.fields + 9
    for f, (axial, around, d, mix) in enumerate(coefficients(plan, speed, swirl, diffusion, coupling)):
        for number, factor in enumerate((d, *mix, *axial, *around)):
            spread[f * terms + number] = jnp.full((8, radial), factor, jnp.float32)
    lane = lax.broadcasted_iota(jnp.int32, (8, radial), 1)
    not_first = lane > 0
    not_last = lane < radial - 1

    def source(at):
        if at < 0:
            return ghosts, 0, at + 2
        if at >= plan.axial:
            return ghosts, 1, at - plan.axial
        if stage == 0:
            return state, None, at
        start = 0
        for low, high in plan.outer:
            if low <= at < high:
                return chunks["outer"], None, start + at - low
            start += high - low
        return chunks["inner"], None, at - plan.inner[0][0]

    def fill(field, at, to):
        ref, side, place = source(at)
        if side is not None:
            work[field, to, LOW : LOW + cycle, :] = ref[side, field, place]
        else:
            work[field, to, LOW : LOW + cycle, :] = ref[field, place]

    begin = 0
    for low, high in ranges:
        size = high - low
        for field in range(plan.fields):
            for at, to in ((low - 2, 0), (low - 1, 1), (high, size + 2), (high + 1, size + 3)):
                fill(field, at, to)
        ref, _, first_place = source(low)

        def copy(tile, carry, ref=ref, first_place=first_place, begin=begin):
            for field in range(plan.fields):
                for step in range(4):
                    place = tile * 4 + step
                    work[field, place + 2, LOW : LOW + cycle, :] = ref[field, first_place + place]
                    work[field, place + 2, LOW - 2 : LOW, :] = low_in[field, begin // 4 + tile, 2 * step : 2 * step + 2, :]
                    work[field, place + 2, LOW + cycle : LOW + cycle + 2, :] = high_in[
                        field, begin // 4 + tile, 2 * step : 2 * step + 2, :
                    ]
            return carry

        lax.fori_loop(0, size // 4, copy, 0)

        def compute(tile, carry, low=low, begin=begin):
            for f in range(plan.fields):
                factors = [spread[f * terms + number] for number in range(terms)]
                values = {}
                for step in range(4):
                    at = tile * 4 + step + 2
                    for row in range(0, cycle, 8):
                        here = slice(LOW + row, LOW + row + 8)
                        center = work[f, at, here, :]
                        left = jnp.where(not_first, pltpu.roll(center, 1, 1), 0.0)
                        right = jnp.where(not_last, pltpu.roll(center, radial - 1, 1), 0.0)
                        total = factors[0] * (left + right)
                        for e in range(plan.fields):
                            total += factors[1 + e] * (center if e == f else work[e, at, here, :])
                        for number, by in enumerate((-2, -1, 1, 2)):
                            total += factors[1 + plan.fields + number] * work[f, at + by, here, :]
                            total += factors[5 + plan.fields + number] * work[f, at, LOW + row + by : LOW + row + by + 8, :]
                        place = begin + tile * 4 + step
                        base = state[f, low + tile * 4 + step, row : row + 8, :]
                        if stage == 3:
                            second, third = older
                            kept = second[f, place, row : row + 8, :] + 2.0 * third[f, place, row : row + 8, :]
                            value = (kept + center - base) * (1.0 / 3.0) + (time_step / 6.0) * total
                        else:
                            value = base + (time_step if stage == 2 else 0.5 * time_step) * total
                        values[step, row] = value
                for (step, row), value in values.items():
                    place = begin + tile * 4 + step
                    if stage == 3:
                        out_buf[f, place, row : row + 8, :] = value
                        continue
                    out[f, place, row : row + 8, :] = value
                    if row == 0:
                        low_out[f, begin // 4 + tile, 2 * step : 2 * step + 2, :] = value[:2]
                    if row == cycle - 8:
                        high_out[f, begin // 4 + tile, 2 * step : 2 * step + 2, :] = value[6:]
            return carry

        lax.fori_loop(0, size // 4, compute, 0)
        begin += size

    if stage == 3:
        begin = 0
        copies = []
        for number, (low, high) in enumerate(ranges):
            copies.append(
                pltpu.make_async_copy(
                    out_buf.at[:, begin : begin + high - low], out_any.at[:, low:high], sem.at[number]
                )
            )
            copies[-1].start()
            begin += high - low
        for item in copies:
            item.wait()
    elif outer:
        total = count(ranges)
        for interface, planes in enumerate(sent):

            @pl.when(place[0] == interface)
            def _(planes=planes):
                planes[...] = out[:, total - 2 : total]

            @pl.when(place[0] != interface)
            def _(planes=planes):
                planes[...] = out[:, 0:2]
    if stage < 3 or outer:
        token[...] = jnp.zeros(token.shape, jnp.float32)


def stage_call(plan, stage, outer, scalars, state, chunks, halos, extra, older=(), whole_out=None):
    ranges = plan.outer if outer else plan.inner
    chunk = (plan.fields, count(ranges), plan.cycle, plan.radial)
    longest = max(high - low for low, high in ranges)
    operands, specs = list(scalars), [whole(SMEM)] * len(scalars)

    def add(values):
        operands.extend(map(near, values))
        specs.extend([whole(VMEM)] * len(values))

    add([state, *(chunks or ()), *halos])
    if outer:
        operands += extra[0]
        specs += [whole(SMEM), whole(SMEM), whole(VMEM)]
        add(extra[1])
    else:
        add([extra])
    scratch = [
        held((plan.fields, longest + 4, plan.cycle + 16, plan.radial)),
        held((plan.fields * (plan.fields + 9), 8, plan.radial)),
    ]
    if outer:
        scratch += [
            held((2, *plan.ghost)),
            held((plan.fields, 2, 2 * plan.cycle, plan.radial)),
            held((2 * plan.cycle, plan.cycle, plan.radial)),
        ]
    aliases = {}
    token = held((8, plan.radial))
    if stage == 3:
        add(older)
        if whole_out is not None:
            aliases = {len(operands): 0}
            operands.append(whole_out)
            specs.append(whole(pl.ANY))
        out_shape = [jax.ShapeDtypeStruct(state.shape, jnp.float32)] + [token] * outer
        out_specs = [whole(pl.ANY)] + [whole(VMEM)] * outer
        scratch = [held(chunk), pltpu.SemaphoreType.DMA((len(ranges),))] + scratch
    else:
        out_shape = [held(chunk), edge_shape(plan, ranges), edge_shape(plan, ranges), token]
        if outer:
            out_shape += [held(plan.ghost)] * (plan.rows - 1)
        out_specs = [whole(VMEM)] * len(out_shape)
    return pl.pallas_call(
        functools.partial(stage_kernel, plan, stage, outer),
        in_specs=specs,
        out_specs=out_specs,
        out_shape=out_shape,
        scratch_shapes=scratch,
        input_output_aliases=aliases,
        compiler_params=params(),
        name=f"stage{stage}_{'outer' if outer else 'inner'}",
    )(*operands)


def exchange(edges):
    size = lax.axis_size("sector")
    ahead = [(i, (i + 1) % size) for i in range(size)]
    back = [(i, (i - 1) % size) for i in range(size)]
    low_edges, high_edges = edges
    return lax.ppermute(high_edges, "sector", ahead), lax.ppermute(low_edges, "sector", back)


def over_interface(plan, interface, offset, planes):
    sectors, cycle = plan.sectors, plan.cycle

    def carry(up, down, blocks):
        route = []
        for sector in range(sectors):
            here, there = interface * sectors + sector, (interface + 1) * sectors + sector
            route.append((interface * sectors + (sector + up) % sectors, there))
            route.append(((interface + 1) * sectors + (sector + down) % sectors, here))
        return lax.ppermute(blocks, ("row", "sector"), route)

    def branch(up, down):
        return lambda blocks: (carry(up, down, blocks), carry(up + 1, down + 1, blocks))

    branches = []
    for up in range(sectors):
        branches.append(branch(up, (sectors - up) % sectors))
        branches.append(branch(up, sectors - 1 - up))
    index = 2 * (offset // cycle) + (offset % cycle > 0).astype(jnp.int32)
    return lax.switch(index, branches, planes)


def on_device(state, interp_blocks, rotor_offset, axial_speed, row_swirl, diffusivity, coupling):
    plan = Plan(state, lax.axis_size("row"), lax.axis_size("sector"))
    place = jnp.stack([lax.axis_index("row"), lax.axis_index("sector")]).astype(jnp.int32)
    scalars = (axial_speed, row_swirl, diffusivity, coupling)
    order = [*range(0, plan.rows - 1, 2), *range(1, plan.rows - 1, 2)]

    sent = first_planes(plan, place, state)
    lo_o, hi_o, lo_i, hi_i = first_edges(plan, state)
    outer_edges, inner_edges = (lo_o, hi_o), (lo_i, hi_i)
    chunks = None
    history = []
    for stage in range(4):
        outer_halos = exchange(outer_edges)
        blocks = {}
        for interface in order:
            blocks[interface] = over_interface(plan, interface, rotor_offset[stage, interface], sent[interface])
        pairs = [block for interface in range(plan.rows - 1) for block in blocks[interface]]
        inner_halos = exchange(inner_edges)
        last = stage == 3
        older = [(history[0][i], history[1][i]) if last else () for i in range(2)]
        given = ([place, rotor_offset, interp_blocks], pairs)
        out_o, *rest = stage_call(plan, stage, True, scalars, state, chunks, outer_halos, given, older[0])
        token = rest[0] if last else rest[2]
        out_i, *rest_i = stage_call(
            plan, stage, False, scalars, state, chunks, inner_halos, token, older[1], out_o if last else None
        )
        if last:
            return out_i
        outer_edges, sent = rest[:2], rest[3:]
        inner_edges = rest_i[:2]
        chunks = (out_o, out_i)
        history.append(chunks)


def solution(mesh):
    return jax.shard_map(
        on_device,
        mesh=mesh,
        in_specs=(P(None, "row", "sector", None), P(), P(), P(), P("row"), P(), P()),
        out_specs=P(None, "row", "sector", None),
        check_vma=False,
    )
```

```python
import functools

import jax
import jax.numpy as jnp
from jax import lax
from jax.experimental import pallas as pl
from jax.experimental.pallas import tpu as pltpu
from jax.sharding import PartitionSpec as P

time_step = 0.4
highest = lax.Precision.HIGHEST
VMEM = pltpu.VMEM
SMEM = pltpu.SMEM
LOW = 8


def whole(space):
    return pl.BlockSpec(memory_space=space)


def held(shape):
    return pltpu.VMEM(tuple(shape), jnp.float32)


def near(value):
    return pltpu.with_memory_space_constraint(value, pltpu.VMEM)


def params():
    return pltpu.CompilerParams(vmem_limit_bytes=16 * 1024 * 1024)


class Plan:
    def __init__(self, state, sectors):
        self.fields, self.axial, self.cycle, self.radial = state.shape
        self.sectors = sectors
        strip = self.axial // 4
        self.outer = ((0, strip), (self.axial - strip, self.axial))
        self.inner = ((strip, self.axial - strip),)
        self.half = sectors // 2
        self.per = -(-2 * self.fields // self.half)
        self.high = sectors // 2
        self.dealt = (sectors, self.per, self.cycle, self.radial)
        self.part = (self.high, self.per, self.cycle, self.radial)
        self.pair = (2, self.per, self.cycle, self.radial)

    def combo(self, side, field, plane):
        place = side * self.per * self.half + field * 2 + plane
        return place // self.per, place % self.per


def count(ranges):
    return sum(high - low for low, high in ranges)


def write_edges(plan, value, field, place, low_ref, high_ref):
    tile, row = place
    low_ref[field, tile, row : row + 2, :] = value[:2]
    high_ref[field, tile, row : row + 2, :] = value[plan.cycle - 2 :]


def gather_planes(plan, buffer, upper, lower):
    for field in range(plan.fields):
        for plane in range(2):
            piece, slot = plan.combo(0, field, plane)
            buffer[piece, slot] = upper(field, plane)
            piece, slot = plan.combo(1, field, plane)
            buffer[piece, slot] = lower(field, plane)


def clear_spare(plan, buffer):
    used = {plan.combo(side, field, plane) for side in range(2) for field in range(plan.fields) for plane in range(2)}
    for piece in range(plan.sectors):
        for slot in range(plan.per):
            if (piece, slot) not in used:
                buffer[piece, slot] = jnp.zeros((plan.cycle, plan.radial), jnp.float32)


def split(plan, low, dealt, keep, give):
    for high in range(plan.high):
        keep[high] = dealt[2 * high + low]
        give[high] = dealt[2 * high + 1 - low]


def planes_kernel(plan, place, state, keep, give, dealt, planes, sems):
    copies = [
        pltpu.make_async_copy(state.at[:, plan.axial - 2 : plan.axial], planes.at[0], sems.at[0]),
        pltpu.make_async_copy(state.at[:, 0:2], planes.at[1], sems.at[1]),
    ]
    for item in copies:
        item.start()
    clear_spare(plan, dealt)
    for item in copies:
        item.wait()
    gather_planes(plan, dealt, lambda f, p: planes[0, f, p], lambda f, p: planes[1, f, p])
    split(plan, place[1] % 2, dealt, keep, give)


def first_planes(plan, place, state):
    return pl.pallas_call(
        functools.partial(planes_kernel, plan),
        in_specs=[whole(SMEM), whole(pl.ANY)],
        out_specs=[whole(VMEM)] * 2,
        out_shape=[held(plan.part)] * 2,
        scratch_shapes=[
            held(plan.dealt),
            held((2, plan.fields, 2, plan.cycle, plan.radial)),
            pltpu.SemaphoreType.DMA((2,)),
        ],
        compiler_params=params(),
        name="first_planes",
    )(place, state)


def first_kernel(plan, state, low_ref, high_ref):
    start = 0
    for low, high in plan.outer + plan.inner:

        def body(tile, carry, low=low, start=start):
            for field in range(plan.fields):
                for step in range(4):
                    at = low + tile * 4 + step
                    rows = slice(2 * step, 2 * step + 2)
                    low_ref[field, start + tile, rows, :] = state[field, at, 0:2, :]
                    high_ref[field, start + tile, rows, :] = state[field, at, plan.cycle - 2 : plan.cycle, :]
            return carry

        lax.fori_loop(0, (high - low) // 4, body, 0)
        start += (high - low) // 4


def edge_shape(plan, ranges):
    return held((plan.fields, count(ranges) // 4, 8, plan.radial))


def first_edges(plan, state):
    return pl.pallas_call(
        functools.partial(first_kernel, plan),
        in_specs=[whole(VMEM)],
        out_specs=[whole(VMEM)] * 2,
        out_shape=[edge_shape(plan, plan.outer + plan.inner)] * 2,
        compiler_params=params(),
        name="first_edges",
    )(near(state))


def gather_kernel(plan, place, keep, came, *refs):
    outs = refs[-plan.high :]
    low, high = place[1] % 2, place[1] // 2
    for ahead, out in enumerate(outs):
        target = lax.rem(high + ahead, plan.high)
        out[low] = keep[target]
        out[1 - low] = came[target]


def gather(plan, place, keep, came, after):
    operands = [place, *map(near, (keep, came)), *map(near, after)]
    return pl.pallas_call(
        functools.partial(gather_kernel, plan),
        in_specs=[whole(SMEM)] + [whole(VMEM)] * (len(operands) - 1),
        out_specs=[whole(VMEM)] * plan.high,
        out_shape=[held(plan.pair)] * plan.high,
        compiler_params=params(),
        name="gather_low",
    )(*operands)


def sort_kernel(plan, place, *refs):
    came, (keep, give) = refs[: plan.high], refs[plan.high :]
    low, high = place[1] % 2, place[1] // 2
    for ahead, value in enumerate(came):
        source = lax.rem(high + plan.high - ahead, plan.high)
        keep[source] = value[low]
        give[source] = value[1 - low]


def sort(plan, place, came):
    return pl.pallas_call(
        functools.partial(sort_kernel, plan),
        in_specs=[whole(SMEM)] + [whole(VMEM)] * plan.high,
        out_specs=[whole(VMEM)] * 2,
        out_shape=[held(plan.part)] * 2,
        compiler_params=params(),
        name="sort_low",
    )(place, *map(near, came))


def interp_kernel(plan, section, place, offsets, weights, *refs):
    *refs, ring, spread = refs
    came, outs = refs[: plan.high], refs[plan.high :]
    full = plan.cycle * plan.sectors
    row, sector = place[0], place[1]
    up = sector < plan.half
    at = jnp.where(up, jnp.minimum(row, offsets.shape[1] - 1), jnp.maximum(row - 1, 0))
    offset = offsets[section, at]
    offset = jnp.where(up, offset, lax.rem(full - offset, full))
    turn = offset // plan.cycle
    cell = lax.rem(offset, plan.cycle)
    matrix = weights[cell]
    for k in range(2 * plan.cycle):
        spread[k] = jnp.broadcast_to(matrix[:, k : k + 1], (plan.cycle, plan.radial))
    high = sector // 2
    for ahead, value in enumerate(came):
        source = lax.rem(high + plan.high - ahead, plan.high)
        for low in range(2):
            ring[2 * source + low] = value[low]
    for ahead, out in enumerate(outs):
        for low in range(2):
            target = 2 * lax.rem(high + ahead, plan.high) + low
            here = lax.rem(target + turn, plan.sectors)
            after = lax.rem(here + 1, plan.sectors)
            for slot in range(plan.per):
                total = None
                for k in range(2 * plan.cycle):
                    cell_at = k % plan.cycle
                    row_value = ring[here if k < plan.cycle else after, slot, cell_at : cell_at + 1, :]
                    term = spread[k] * jnp.broadcast_to(row_value, (plan.cycle, plan.radial))
                    total = term if total is None else total + term
                out[low, slot] = total


def interp(plan, section, place, offsets, weights, came):
    return pl.pallas_call(
        functools.partial(interp_kernel, plan, section),
        in_specs=[whole(SMEM), whole(SMEM)] + [whole(VMEM)] * (1 + plan.high),
        out_specs=[whole(VMEM)] * plan.high,
        out_shape=[held(plan.pair)] * plan.high,
        scratch_shapes=[held(plan.dealt), held((2 * plan.cycle, plan.cycle, plan.radial))],
        compiler_params=params(),
        name="interpolate",
    )(place, offsets, weights, *map(near, came))


def coefficients(plan, speed, swirl, diffusion, coupling):
    twelfth = 1.0 / 12.0
    w = swirl[0]
    table = []
    for f in range(plan.fields):
        v, d = speed[f], diffusion[f]
        axial = ((-v - d) * twelfth, (8.0 * v + 16.0 * d) * twelfth, (16.0 * d - 8.0 * v) * twelfth, (v - d) * twelfth)
        cycle = ((-w - d) * twelfth, (8.0 * w + 16.0 * d) * twelfth, (16.0 * d - 8.0 * w) * twelfth, (w - d) * twelfth)
        mix = [coupling[f, e] - 7.0 * d if e == f else coupling[f, e] for e in range(plan.fields)]
        table.append((axial, cycle, d, mix))
    return table


def stage_kernel(plan, stage, outer, speed, swirl, diffusion, coupling, *refs):
    refs = list(refs)
    take = lambda number: [refs.pop(0) for _ in range(number)]
    ranges = plan.outer if outer else plan.inner
    (state,) = take(1)
    chunks = {"state": state} if stage == 0 else dict(zip(("outer", "inner"), take(2)))
    low_in, high_in = take(2)
    if outer:
        place, keep_in, came_in = take(3)
    elif stage < 3:
        outer_edges = take(2)
    else:
        take(1)
    if stage == 3:
        older = take(2)
        if not outer:
            take(1)
        (out_any,) = take(1)
        if outer:
            (token,) = take(1)
        out_buf, sem = take(2)
    else:
        out, low_out, high_out = take(3)
        if outer:
            keep_out, give_out = take(2)
    work, spread = take(2)
    if outer:
        (ghosts,) = take(1)
        low_place = place[1] % 2
        for high in range(plan.high):
            ghosts[2 * high + low_place] = keep_in[high]
            ghosts[2 * high + 1 - low_place] = came_in[high]
    tiles_ahead = 0 if outer else count(plan.outer) // 4
    if not outer and stage < 3:
        low_out[:, :tiles_ahead] = outer_edges[0][...]
        high_out[:, :tiles_ahead] = outer_edges[1][...]
    cycle, radial = plan.cycle, plan.radial
    terms = plan.fields + 9
    for f, (axial, around, d, mix) in enumerate(coefficients(plan, speed, swirl, diffusion, coupling)):
        for number, factor in enumerate((d, *mix, *axial, *around)):
            spread[f * terms + number] = jnp.full((8, radial), factor, jnp.float32)
    lane = lax.broadcasted_iota(jnp.int32, (8, radial), 1)
    not_first = lane > 0
    not_last = lane < radial - 1

    def source(at):
        if at < 0:
            return ghosts, 0, at + 2
        if at >= plan.axial:
            return ghosts, 1, at - plan.axial
        if stage == 0:
            return state, None, at
        start = 0
        for low, high in plan.outer:
            if low <= at < high:
                return chunks["outer"], None, start + at - low
            start += high - low
        return chunks["inner"], None, at - plan.inner[0][0]

    def fill(field, at, to):
        ref, side, place = source(at)
        if side is not None:
            piece, slot = plan.combo(side, field, place)
            work[field, to, LOW : LOW + cycle, :] = ref[piece, slot]
        else:
            work[field, to, LOW : LOW + cycle, :] = ref[field, place]

    begin = 0
    for low, high in ranges:
        size = high - low
        for field in range(plan.fields):
            for at, to in ((low - 2, 0), (low - 1, 1), (high, size + 2), (high + 1, size + 3)):
                fill(field, at, to)
        ref, _, first_place = source(low)

        def copy(tile, carry, ref=ref, first_place=first_place, begin=begin):
            for field in range(plan.fields):
                for step in range(4):
                    place = tile * 4 + step
                    work[field, place + 2, LOW : LOW + cycle, :] = ref[field, first_place + place]
                    work[field, place + 2, LOW - 2 : LOW, :] = low_in[field, tiles_ahead + begin // 4 + tile, 2 * step : 2 * step + 2, :]
                    work[field, place + 2, LOW + cycle : LOW + cycle + 2, :] = high_in[
                        field, tiles_ahead + begin // 4 + tile, 2 * step : 2 * step + 2, :
                    ]
            return carry

        lax.fori_loop(0, size // 4, copy, 0)

        def compute(tile, carry, low=low, begin=begin):
            for f in range(plan.fields):
                factors = [spread[f * terms + number] for number in range(terms)]
                values = {}
                for step in range(4):
                    at = tile * 4 + step + 2
                    for row in range(0, cycle, 8):
                        here = slice(LOW + row, LOW + row + 8)
                        center = work[f, at, here, :]
                        left = jnp.where(not_first, pltpu.roll(center, 1, 1), 0.0)
                        right = jnp.where(not_last, pltpu.roll(center, radial - 1, 1), 0.0)
                        total = factors[0] * (left + right)
                        for e in range(plan.fields):
                            total += factors[1 + e] * (center if e == f else work[e, at, here, :])
                        for number, by in enumerate((-2, -1, 1, 2)):
                            total += factors[1 + plan.fields + number] * work[f, at + by, here, :]
                            total += factors[5 + plan.fields + number] * work[f, at, LOW + row + by : LOW + row + by + 8, :]
                        place = begin + tile * 4 + step
                        base = state[f, low + tile * 4 + step, row : row + 8, :]
                        if stage == 3:
                            second, third = older
                            kept = second[f, place, row : row + 8, :] + 2.0 * third[f, place, row : row + 8, :]
                            value = (kept + center - base) * (1.0 / 3.0) + (time_step / 6.0) * total
                        else:
                            value = base + (time_step if stage == 2 else 0.5 * time_step) * total
                        values[step, row] = value
                for (step, row), value in values.items():
                    place = begin + tile * 4 + step
                    if stage == 3:
                        out_buf[f, place, row : row + 8, :] = value
                        continue
                    out[f, place, row : row + 8, :] = value
                    if row == 0:
                        low_out[f, tiles_ahead + begin // 4 + tile, 2 * step : 2 * step + 2, :] = value[:2]
                    if row == cycle - 8:
                        high_out[f, tiles_ahead + begin // 4 + tile, 2 * step : 2 * step + 2, :] = value[6:]
            return carry

        lax.fori_loop(0, size // 4, compute, 0)
        begin += size

    if stage == 3:
        begin = 0
        copies = []
        for number, (low, high) in enumerate(ranges):
            copies.append(
                pltpu.make_async_copy(
                    out_buf.at[:, begin : begin + high - low], out_any.at[:, low:high], sem.at[number]
                )
            )
            copies[-1].start()
            begin += high - low
        for item in copies:
            item.wait()
    elif outer:
        total = count(ranges)
        clear_spare(plan, ghosts)
        gather_planes(plan, ghosts, lambda f, p: out[f, total - 2 + p], lambda f, p: out[f, p])
        split(plan, low_place, ghosts, keep_out, give_out)
    if stage == 3 and outer:
        token[...] = jnp.zeros(token.shape, jnp.float32)


def stage_call(plan, stage, outer, scalars, state, chunks, halos, extra, older=(), whole_out=None):
    ranges = plan.outer if outer else plan.inner
    chunk = (plan.fields, count(ranges), plan.cycle, plan.radial)
    longest = max(high - low for low, high in ranges)
    operands, specs = list(scalars), [whole(SMEM)] * len(scalars)

    def add(values):
        operands.extend(map(near, values))
        specs.extend([whole(VMEM)] * len(values))

    add([state, *(chunks or ()), *halos])
    if outer:
        operands.append(extra[0])
        specs.append(whole(SMEM))
        extra = extra[1:]
    add(extra)
    scratch = [
        held((plan.fields, longest + 4, plan.cycle + 16, plan.radial)),
        held((plan.fields * (plan.fields + 9), 8, plan.radial)),
    ]
    if outer:
        scratch.append(held(plan.dealt))
    aliases = {}
    token = held((8, plan.radial))
    if stage == 3:
        add(older)
        if whole_out is not None:
            aliases = {len(operands): 0}
            operands.append(whole_out)
            specs.append(whole(pl.ANY))
        out_shape = [jax.ShapeDtypeStruct(state.shape, jnp.float32)] + [token] * outer
        out_specs = [whole(pl.ANY)] + [whole(VMEM)] * outer
        scratch = [held(chunk), pltpu.SemaphoreType.DMA((len(ranges),))] + scratch
    else:
        edges = edge_shape(plan, ranges if outer else plan.outer + plan.inner)
        out_shape = [held(chunk), edges, edges]
        if outer:
            out_shape += [held(plan.part)] * 2
        out_specs = [whole(VMEM)] * len(out_shape)
    return pl.pallas_call(
        functools.partial(stage_kernel, plan, stage, outer),
        in_specs=specs,
        out_specs=out_specs,
        out_shape=out_shape,
        scratch_shapes=scratch,
        input_output_aliases=aliases,
        compiler_params=params(),
        name=f"stage{stage}_{'outer' if outer else 'inner'}",
    )(*operands)


def exchange(edges):
    size = lax.axis_size("sector")
    ahead = [(i, (i + 1) % size) for i in range(size)]
    back = [(i, (i - 1) % size) for i in range(size)]
    low_edges, high_edges = edges
    return lax.ppermute(high_edges, "sector", ahead), lax.ppermute(low_edges, "sector", back)


def swap_low(plan, value):
    return lax.ppermute(value, "sector", [(i, i + 1 - 2 * (i % 2)) for i in range(plan.sectors)])


def along_high(plan, values):
    sent = [values[0]]
    for ahead in range(1, plan.high):
        route = [(i, (i + 2 * ahead) % plan.sectors) for i in range(plan.sectors)]
        sent.append(lax.ppermute(values[ahead], "sector", route))
    return sent


def along_high_to_next_row(plan, values):
    rows, sent = lax.axis_size("row"), []
    for ahead in range(plan.high):
        route = []
        for row in range(rows):
            for sector in range(plan.sectors):
                target = row + 1 if sector < plan.half else row - 1
                if 0 <= target < rows:
                    to = target * plan.sectors + (sector + 2 * ahead) % plan.sectors
                    route.append((row * plan.sectors + sector, to))
        sent.append(lax.ppermute(values[ahead], ("row", "sector"), route))
    return sent


def on_device(state, interp_blocks, rotor_offset, axial_speed, row_swirl, diffusivity, coupling):
    plan = Plan(state, lax.axis_size("sector"))
    place = jnp.stack([lax.axis_index("row"), lax.axis_index("sector")]).astype(jnp.int32)
    scalars = (axial_speed, row_swirl, diffusivity, coupling)

    keep, give = first_planes(plan, place, state)
    edges = first_edges(plan, state)
    chunks, history = None, []
    for stage in range(4):
        last = stage == 3
        gathered = gather(plan, place, keep, swap_low(plan, give), edges[:1])
        *edges, _ = lax.optimization_barrier((*edges, gathered[0]))
        came = along_high(plan, gathered)
        halos = exchange(edges)
        made = interp(plan, stage, place, rotor_offset, interp_blocks, came)
        keep, give = sort(plan, place, along_high_to_next_row(plan, made))
        older = [(history[0][i], history[1][i]) if last else () for i in range(2)]
        ghosts = (place, keep, swap_low(plan, give))
        out_o, *rest = stage_call(plan, stage, True, scalars, state, chunks, halos, ghosts, older[0])
        after = rest if last else rest[:2]
        out_i, *edges = stage_call(
            plan, stage, False, scalars, state, chunks, halos, after, older[1], out_o if last else None
        )
        if last:
            return out_i
        keep, give = rest[2:]
        chunks = (out_o, out_i)
        history.append(chunks)


def solution(mesh):
    return jax.shard_map(
        on_device,
        mesh=mesh,
        in_specs=(P(None, "row", "sector", None), P(), P(), P(), P("row"), P(), P()),
        out_specs=P(None, "row", "sector", None),
        check_vma=False,
    )
```

```python
import functools

import jax
import jax.numpy as jnp
from jax import lax
from jax.experimental import pallas as pl
from jax.experimental.pallas import tpu as pltpu
from jax.sharding import PartitionSpec as P

time_step = 0.4
highest = lax.Precision.HIGHEST
VMEM = pltpu.VMEM
SMEM = pltpu.SMEM
EXTRA = 4
LOW = 8


def whole(space):
    return pl.BlockSpec(memory_space=space)


def held(shape):
    return pltpu.VMEM(tuple(shape), jnp.float32)


def near(value):
    return pltpu.with_memory_space_constraint(value, pltpu.VMEM)


def params():
    return pltpu.CompilerParams(vmem_limit_bytes=16 * 1024 * 1024)


class Plan:
    def __init__(self, state, sectors):
        self.fields, self.axial, self.cycle, self.radial = state.shape
        self.sectors = sectors
        strip = self.axial // 4
        self.outer = ((0, strip), (self.axial - strip, self.axial))
        self.inner = ((strip, self.axial - strip),)
        self.ghost = (2, self.fields, 2, self.cycle, self.radial)
        self.deep = 8
        self.full = self.cycle * sectors
        self.mine = self.radial // sectors
        self.wide = self.mine + 2 * EXTRA
        self.packed = self.deep * self.cycle


def count(ranges):
    return sum(high - low for low, high in ranges)


def write_edges(plan, value, field, place, low_ref, high_ref):
    tile, row = place
    low_ref[field, tile, row : row + 2, :] = value[:2]
    high_ref[field, tile, row : row + 2, :] = value[plan.cycle - 2 :]


def pack_kernel(plan, state, below, out, planes, tall, sem):
    copy = pltpu.make_async_copy(state.at[:, plan.axial - plan.deep : plan.axial], planes, sem.at[0])
    copy.start()
    tall[...] = jnp.zeros(tall.shape, jnp.float32)
    copy.wait()
    for side, source in enumerate((planes, below)):
        for field in range(plan.fields):
            flat = source[field].reshape(plan.packed, plan.radial)
            tall[EXTRA : EXTRA + plan.radial, :] = flat.T
            for sector in range(plan.sectors):
                out[sector, side * plan.fields + field] = tall[sector * plan.mine : sector * plan.mine + plan.wide, :]


def pack(plan, state, below):
    return pl.pallas_call(
        functools.partial(pack_kernel, plan),
        in_specs=[whole(pl.ANY), whole(VMEM)],
        out_specs=whole(VMEM),
        out_shape=jax.ShapeDtypeStruct((plan.sectors, 2 * plan.fields, plan.wide, plan.packed), jnp.float32),
        scratch_shapes=[
            held((plan.fields, plan.deep, plan.cycle, plan.radial)),
            held((plan.radial + 2 * EXTRA, plan.packed)),
            pltpu.SemaphoreType.DMA((1,)),
        ],
        compiler_params=params(),
        name="pack_zone",
    )(state, below)


def zone_kernel(plan, place, offsets, speed, swirl, next_swirl, diffusion, coupling, weights, got, *refs):
    to_here, to_next, base, now, later, spread, matrix, made = refs
    fields, deep, cycle, full, wide = plan.fields, plan.deep, plan.cycle, plan.full, plan.wide
    sections = offsets.shape[0]
    row, sector = place[0], place[1]
    terms = fields + 9
    rows = slice(LOW, LOW + wide)
    lane = lax.broadcasted_iota(jnp.int32, (wide, plan.packed), 1) // cycle
    own_lane = lax.broadcasted_iota(jnp.int32, (plan.mine, plan.packed), 1) // cycle
    at_radius = lax.broadcasted_iota(jnp.int32, (wide, full), 0) + sector * plan.mine - EXTRA
    inside = (at_radius >= 0) & (at_radius < plan.radial)
    block = plan.packed // cycle

    for side, w in enumerate((swirl, next_swirl)):
        for f, (axial, around, d, mix) in enumerate(coefficients(plan, speed, w, diffusion, coupling)):
            for number, factor in enumerate((d, *mix, *axial, *around)):
                spread[side * fields * terms + f * terms + number] = jnp.full((wide, full), factor, jnp.float32)

    for buffer in (base, now, later):
        for side in range(2):
            def clear(field, carry, buffer=buffer, side=side):
                buffer[side, field] = jnp.zeros(buffer.shape[2:], jnp.float32)
                return carry

            lax.fori_loop(0, fields, clear, 0)

    for side in range(2):
        def spread_out(field, carry, side=side):
            for plane in range(deep):
                parts = []
                for first in range(0, plan.sectors, block):
                    total = jnp.zeros((wide, plan.packed), jnp.float32)
                    for number in range(min(block, plan.sectors - first)):
                        turned = got[first + number, side * fields + field]
                        turn = (number - plane) * cycle % plan.packed
                        if turn:
                            turned = pltpu.roll(turned, turn, 1)
                        total = jnp.where(lane == number, turned, total)
                    parts.append(total)
                value = parts[0] if len(parts) == 1 else jnp.concatenate(parts, axis=1)
                base[side, field, 2 + plane, rows, :] = value
                now[side, field, 2 + plane, rows, :] = value
            return carry

        lax.fori_loop(0, fields, spread_out, 0)

    for section in range(sections):
        offset = offsets[section, jnp.minimum(row, offsets.shape[1] - 1)]
        for side in range(2):
            here = lax.rem(full - offset, full) if side == 0 else offset
            shift, cell = here // cycle, lax.rem(here, cycle)
            for target in range(plan.sectors):
                matrix[target * cycle : (target + 1) * cycle, :] = pltpu.roll(
                    weights[cell], lax.rem(target + shift, plan.sectors) * cycle, 1
                )
            other = 1 - side
            first = 2 if other == 1 else deep
            to = deep + 2 if side == 0 else 0
            pairs = [(field, plane) for field in range(fields) for plane in range(2)]
            values = [now[other, field, first + plane, rows, :] for field, plane in pairs]
            turn = matrix[...]
            together = wide % 8 == 0
            if together:
                values = [jnp.concatenate(values, axis=0)]
            results = [
                lax.dot_general(
                    value, turn, (((1,), (1,)), ((), ())), precision=highest, preferred_element_type=jnp.float32
                )
                for value in values
            ]
            for number, (field, plane) in enumerate(pairs):
                if together:
                    value = results[0][number * wide : (number + 1) * wide]
                else:
                    value = results[number]
                now[side, field, to + plane, rows, :] = value
                made[side, field, 2 * section + plane] = now[side, field, to + plane, LOW + EXTRA : LOW + EXTRA + plan.mine, :]
        if section == sections - 1:
            break
        size = deep - 2 * (section + 1)
        step_size = time_step if section == sections - 2 else 0.5 * time_step
        for side in range(2):
            begin = 2 + (deep - size if side == 0 else 0)

            def advance(number, carry, side=side, begin=begin, now=now, later=later, step_size=step_size):
                plane = begin + number
                center = [now[side, e, plane, rows, :] for e in range(fields)]
                for f in range(fields):
                    factor = lambda k: spread[side * fields * terms + f * terms + k]
                    total = factor(0) * (
                        now[side, f, plane, LOW - 1 : LOW - 1 + wide, :] + now[side, f, plane, LOW + 1 : LOW + 1 + wide, :]
                    )
                    for e in range(fields):
                        total += factor(1 + e) * center[e]
                    for place_at, by in enumerate((-2, -1, 1, 2)):
                        total += factor(1 + fields + place_at) * now[side, f, plane + by, rows, :]
                        total += factor(5 + fields + place_at) * pltpu.roll(center[f], -by % full, 1)
                    value = base[side, f, plane, rows, :] + step_size * total
                    later[side, f, plane, rows, :] = jnp.where(inside, value, 0.0)
                return carry

            lax.fori_loop(0, size, advance, 0)
        now, later = later, now

    has_next = (row < offsets.shape[1]).astype(jnp.float32)
    for side, out in enumerate((to_here, to_next)):
        def hand_out(field, carry, side=side, out=out):
            for target in range(plan.sectors):
                total = jnp.zeros((plan.mine, plan.packed), jnp.float32)
                first = target // block * plan.packed
                for number in range(2 * sections):
                    turned = made[side, field, number, :, first : first + plan.packed]
                    turn = (number - target % block) * cycle % plan.packed
                    if turn:
                        turned = pltpu.roll(turned, turn, 1)
                    total = jnp.where(own_lane == number, turned, total)
                out[target, field] = total * has_next if side == 0 else total
            return carry

        lax.fori_loop(0, fields, hand_out, 0)


def zone(plan, place, offsets, scalars, next_swirl, weights, got):
    speed, swirl, diffusion, coupling = scalars
    buffer = held((2, plan.fields, plan.deep + 4, LOW + plan.wide + 8, plan.full))
    sent = jax.ShapeDtypeStruct((plan.sectors, plan.fields, plan.mine, plan.packed), jnp.float32)
    return pl.pallas_call(
        functools.partial(zone_kernel, plan),
        in_specs=[whole(SMEM)] * 7 + [whole(VMEM)] * 2,
        out_specs=[whole(VMEM)] * 2,
        out_shape=[sent] * 2,
        scratch_shapes=[
            buffer,
            buffer,
            buffer,
            held((2 * plan.fields * (plan.fields + 9), plan.wide, plan.full)),
            held((plan.full, plan.full)),
            held((2, plan.fields, 2 * offsets.shape[0], plan.mine, plan.full)),
        ],
        compiler_params=pltpu.CompilerParams(vmem_limit_bytes=48 * 1024 * 1024),
        name="step_zone",
    )(place, offsets, speed, swirl, next_swirl, diffusion, coupling, weights, got)


def unpack_kernel(plan, got, *refs):
    *outs, tall = refs
    for side in range(2):
        for field in range(plan.fields):
            for sector in range(plan.sectors):
                tall[sector * plan.mine : (sector + 1) * plan.mine, :] = got[sector, side * plan.fields + field]
            flat = tall[...].T
            for section, out in enumerate(outs):
                for plane in range(2):
                    start = (2 * section + plane) * plan.cycle
                    out[side, field, plane] = flat[start : start + plan.cycle]


def unpack(plan, got, sections):
    return pl.pallas_call(
        functools.partial(unpack_kernel, plan),
        in_specs=[whole(VMEM)],
        out_specs=[whole(VMEM)] * sections,
        out_shape=[held(plan.ghost)] * sections,
        scratch_shapes=[held((plan.radial, plan.packed))],
        compiler_params=params(),
        name="unpack_ghosts",
    )(got)


def first_kernel(plan, state, lo_o, hi_o, lo_i, hi_i):
    for ranges, low_ref, high_ref in ((plan.outer, lo_o, hi_o), (plan.inner, lo_i, hi_i)):
        start = 0
        for low, high in ranges:

            def body(tile, carry, low=low, start=start, low_ref=low_ref, high_ref=high_ref):
                for field in range(plan.fields):
                    for step in range(4):
                        at = low + tile * 4 + step
                        low_ref[field, start + tile, 2 * step : 2 * step + 2, :] = state[field, at, 0:2, :]
                        high_ref[field, start + tile, 2 * step : 2 * step + 2, :] = state[
                            field, at, plan.cycle - 2 : plan.cycle, :
                        ]
                return carry

            lax.fori_loop(0, (high - low) // 4, body, 0)
            start += (high - low) // 4


def edge_shape(plan, ranges):
    return held((plan.fields, count(ranges) // 4, 8, plan.radial))


def first(plan, state):
    return pl.pallas_call(
        functools.partial(first_kernel, plan),
        in_specs=[whole(VMEM)],
        out_specs=[whole(VMEM)] * 4,
        out_shape=[edge_shape(plan, ranges) for ranges in (plan.outer, plan.outer, plan.inner, plan.inner)],
        compiler_params=params(),
        name="first_edges",
    )(state)


def coefficients(plan, speed, swirl, diffusion, coupling):
    twelfth = 1.0 / 12.0
    w = swirl[0]
    table = []
    for f in range(plan.fields):
        v, d = speed[f], diffusion[f]
        axial = ((-v - d) * twelfth, (8.0 * v + 16.0 * d) * twelfth, (16.0 * d - 8.0 * v) * twelfth, (v - d) * twelfth)
        cycle = ((-w - d) * twelfth, (8.0 * w + 16.0 * d) * twelfth, (16.0 * d - 8.0 * w) * twelfth, (w - d) * twelfth)
        mix = [coupling[f, e] - 7.0 * d if e == f else coupling[f, e] for e in range(plan.fields)]
        table.append((axial, cycle, d, mix))
    return table


def stage_kernel(plan, stage, outer, speed, swirl, diffusion, coupling, *refs):
    refs = list(refs)
    take = lambda number: [refs.pop(0) for _ in range(number)]
    ranges = plan.outer if outer else plan.inner
    (state,) = take(1)
    chunks = {"state": state} if stage == 0 else dict(zip(("outer", "inner"), take(2)))
    low_in, high_in = take(2)
    if outer:
        (ghosts,) = take(1)
    else:
        take(1)
    if stage == 3:
        older = take(2)
        if not outer:
            take(1)
        (out_any,) = take(1)
        if outer:
            (token,) = take(1)
        out_buf, sem = take(2)
    else:
        out, low_out, high_out, token = take(4)
    work, spread = take(2)
    cycle, radial = plan.cycle, plan.radial
    terms = plan.fields + 9
    for f, (axial, around, d, mix) in enumerate(coefficients(plan, speed, swirl, diffusion, coupling)):
        for number, factor in enumerate((d, *mix, *axial, *around)):
            spread[f * terms + number] = jnp.full((8, radial), factor, jnp.float32)
    lane = lax.broadcasted_iota(jnp.int32, (8, radial), 1)
    not_first = lane > 0
    not_last = lane < radial - 1

    def source(at):
        if at < 0:
            return ghosts, 0, at + 2
        if at >= plan.axial:
            return ghosts, 1, at - plan.axial
        if stage == 0:
            return state, None, at
        start = 0
        for low, high in plan.outer:
            if low <= at < high:
                return chunks["outer"], None, start + at - low
            start += high - low
        return chunks["inner"], None, at - plan.inner[0][0]

    def fill(field, at, to):
        ref, side, place = source(at)
        if side is not None:
            work[field, to, LOW : LOW + cycle, :] = ref[side, field, place]
        else:
            work[field, to, LOW : LOW + cycle, :] = ref[field, place]

    begin = 0
    for low, high in ranges:
        size = high - low
        for field in range(plan.fields):
            for at, to in ((low - 2, 0), (low - 1, 1), (high, size + 2), (high + 1, size + 3)):
                fill(field, at, to)
        ref, _, first_place = source(low)

        def copy(tile, carry, ref=ref, first_place=first_place, begin=begin):
            for field in range(plan.fields):
                for step in range(4):
                    place = tile * 4 + step
                    work[field, place + 2, LOW : LOW + cycle, :] = ref[field, first_place + place]
                    work[field, place + 2, LOW - 2 : LOW, :] = low_in[field, begin // 4 + tile, 2 * step : 2 * step + 2, :]
                    work[field, place + 2, LOW + cycle : LOW + cycle + 2, :] = high_in[
                        field, begin // 4 + tile, 2 * step : 2 * step + 2, :
                    ]
            return carry

        lax.fori_loop(0, size // 4, copy, 0)

        def compute(tile, carry, low=low, begin=begin):
            for f in range(plan.fields):
                factors = [spread[f * terms + number] for number in range(terms)]
                values = {}
                for step in range(4):
                    at = tile * 4 + step + 2
                    for row in range(0, cycle, 8):
                        here = slice(LOW + row, LOW + row + 8)
                        center = work[f, at, here, :]
                        left = jnp.where(not_first, pltpu.roll(center, 1, 1), 0.0)
                        right = jnp.where(not_last, pltpu.roll(center, radial - 1, 1), 0.0)
                        total = factors[0] * (left + right)
                        for e in range(plan.fields):
                            total += factors[1 + e] * (center if e == f else work[e, at, here, :])
                        for number, by in enumerate((-2, -1, 1, 2)):
                            total += factors[1 + plan.fields + number] * work[f, at + by, here, :]
                            total += factors[5 + plan.fields + number] * work[f, at, LOW + row + by : LOW + row + by + 8, :]
                        place = begin + tile * 4 + step
                        base = state[f, low + tile * 4 + step, row : row + 8, :]
                        if stage == 3:
                            second, third = older
                            kept = second[f, place, row : row + 8, :] + 2.0 * third[f, place, row : row + 8, :]
                            value = (kept + center - base) * (1.0 / 3.0) + (time_step / 6.0) * total
                        else:
                            value = base + (time_step if stage == 2 else 0.5 * time_step) * total
                        values[step, row] = value
                for (step, row), value in values.items():
                    place = begin + tile * 4 + step
                    if stage == 3:
                        out_buf[f, place, row : row + 8, :] = value
                        continue
                    out[f, place, row : row + 8, :] = value
                    if row == 0:
                        low_out[f, begin // 4 + tile, 2 * step : 2 * step + 2, :] = value[:2]
                    if row == cycle - 8:
                        high_out[f, begin // 4 + tile, 2 * step : 2 * step + 2, :] = value[6:]
            return carry

        lax.fori_loop(0, size // 4, compute, 0)
        begin += size

    if stage == 3:
        begin = 0
        copies = []
        for number, (low, high) in enumerate(ranges):
            copies.append(
                pltpu.make_async_copy(
                    out_buf.at[:, begin : begin + high - low], out_any.at[:, low:high], sem.at[number]
                )
            )
            copies[-1].start()
            begin += high - low
        for item in copies:
            item.wait()
    if stage < 3 or outer:
        token[...] = jnp.zeros(token.shape, jnp.float32)


def stage_call(plan, stage, outer, scalars, state, chunks, halos, extra, older=(), whole_out=None):
    ranges = plan.outer if outer else plan.inner
    chunk = (plan.fields, count(ranges), plan.cycle, plan.radial)
    longest = max(high - low for low, high in ranges)
    operands, specs = list(scalars), [whole(SMEM)] * len(scalars)

    def add(values):
        operands.extend(map(near, values))
        specs.extend([whole(VMEM)] * len(values))

    add([state, *(chunks or ()), *halos, extra])
    scratch = [
        held((plan.fields, longest + 4, plan.cycle + 16, plan.radial)),
        held((plan.fields * (plan.fields + 9), 8, plan.radial)),
    ]
    aliases = {}
    token = held((8, plan.radial))
    if stage == 3:
        add(older)
        if whole_out is not None:
            aliases = {len(operands): 0}
            operands.append(whole_out)
            specs.append(whole(pl.ANY))
        out_shape = [jax.ShapeDtypeStruct(state.shape, jnp.float32)] + [token] * outer
        out_specs = [whole(pl.ANY)] + [whole(VMEM)] * outer
        scratch = [held(chunk), pltpu.SemaphoreType.DMA((len(ranges),))] + scratch
    else:
        out_shape = [held(chunk), edge_shape(plan, ranges), edge_shape(plan, ranges), token]
        out_specs = [whole(VMEM)] * len(out_shape)
    return pl.pallas_call(
        functools.partial(stage_kernel, plan, stage, outer),
        in_specs=specs,
        out_specs=out_specs,
        out_shape=out_shape,
        scratch_shapes=scratch,
        input_output_aliases=aliases,
        compiler_params=params(),
        name=f"stage{stage}_{'outer' if outer else 'inner'}",
    )(*operands)


def exchange(edges):
    size = lax.axis_size("sector")
    ahead = [(i, (i + 1) % size) for i in range(size)]
    back = [(i, (i - 1) % size) for i in range(size)]
    low_edges, high_edges = edges
    return lax.ppermute(high_edges, "sector", ahead), lax.ppermute(low_edges, "sector", back)


def on_device(state, interp_blocks, rotor_offset, axial_speed, row_swirl, diffusivity, coupling):
    plan = Plan(state, lax.axis_size("sector"))
    rows = lax.axis_size("row")
    sections = rotor_offset.shape[0]
    place = jnp.stack([lax.axis_index("row"), lax.axis_index("sector")]).astype(jnp.int32)
    scalars = (axial_speed, row_swirl, diffusivity, coupling)
    back = [(row + 1, row) for row in range(rows - 1)]
    ahead = [(row, row + 1) for row in range(rows - 1)]

    below = lax.ppermute(state[:, : plan.deep], "row", back)
    next_swirl = lax.ppermute(row_swirl, "row", back)
    got = lax.all_to_all(pack(plan, state, below), "sector", 0, 0, tiled=True)
    weights = jnp.pad(interp_blocks, ((0, 0), (0, 0), (0, plan.full - interp_blocks.shape[2])))
    downstream, to_next = zone(plan, place, rotor_offset, scalars, next_swirl, weights, got)
    upstream = lax.ppermute(to_next, "row", ahead)
    returned = lax.all_to_all(jnp.concatenate([upstream, downstream], axis=1), "sector", 0, 0, tiled=True)
    ghosts = unpack(plan, returned, sections)

    lo_o, hi_o, lo_i, hi_i = first(plan, state)
    outer_edges, inner_edges = (lo_o, hi_o), (lo_i, hi_i)
    chunks, history = None, []
    for stage in range(4):
        outer_halos, inner_halos = exchange(outer_edges), exchange(inner_edges)
        last = stage == 3
        older = [(history[0][i], history[1][i]) if last else () for i in range(2)]
        out_o, *rest = stage_call(plan, stage, True, scalars, state, chunks, outer_halos, ghosts[stage], older[0])
        token = rest[0] if last else rest[2]
        out_i, *rest_i = stage_call(
            plan, stage, False, scalars, state, chunks, inner_halos, token, older[1], out_o if last else None
        )
        if last:
            return out_i
        outer_edges, inner_edges = rest[:2], rest_i[:2]
        chunks = (out_o, out_i)
        history.append(chunks)


def solution(mesh):
    return jax.shard_map(
        on_device,
        mesh=mesh,
        in_specs=(P(None, "row", "sector", None), P(), P(), P(), P("row"), P(), P()),
        out_specs=P(None, "row", "sector", None),
        check_vma=False,
    )
```

```python
import functools

import jax
import jax.numpy as jnp
from jax import lax
from jax.experimental import pallas as pl
from jax.experimental.pallas import tpu as pltpu
from jax.sharding import PartitionSpec as P

time_step = 0.4
highest = lax.Precision.HIGHEST
VMEM = pltpu.VMEM
SMEM = pltpu.SMEM
EXTRA = 4
LOW = 8


def whole(space):
    return pl.BlockSpec(memory_space=space)


def held(shape):
    return pltpu.VMEM(tuple(shape), jnp.float32)


def near(value):
    return pltpu.with_memory_space_constraint(value, pltpu.VMEM)


def params():
    return pltpu.CompilerParams(vmem_limit_bytes=16 * 1024 * 1024)


class Plan:
    def __init__(self, state, sectors):
        self.fields, self.axial, self.cycle, self.radial = state.shape
        self.sectors = sectors
        self.middle = self.axial // 8 * 4
        self.ghost = (2, self.fields, 2, self.cycle, self.radial)
        self.ends = 8
        self.deep = 8
        self.full = self.cycle * sectors
        self.mine = self.radial // sectors
        self.wide = self.mine + 2 * EXTRA
        self.packed = self.deep * self.cycle


    def ranges(self, kind, stage):
        reach = 2 * (stage + 1)
        if kind == "low":
            return ((reach, self.middle),)
        if kind == "high":
            return ((self.middle, self.axial - reach),)
        return ((0, reach), (self.axial - reach, self.axial))

    def kept(self, kind):
        return {"low": self.middle, "high": self.axial - self.middle, "ends": 2 * self.ends}[kind]

    def owner(self, plane, stage):
        reach = 2 * stage
        if plane < reach:
            return "ends", plane
        if plane >= self.axial - reach:
            return "ends", plane - self.axial + 2 * self.ends
        return ("low", plane) if plane < self.middle else ("high", plane - self.middle)

    def place(self, kind, plane):
        if kind == "ends":
            return plane if plane < self.middle else plane - self.axial + 2 * self.ends
        return plane if kind == "low" else plane - self.middle


def pack_kernel(plan, state, below, out, planes, tall, sem):
    copy = pltpu.make_async_copy(state.at[:, plan.axial - plan.deep : plan.axial], planes, sem.at[0])
    copy.start()
    tall[...] = jnp.zeros(tall.shape, jnp.float32)
    copy.wait()
    for side, source in enumerate((planes, below)):
        for field in range(plan.fields):
            flat = source[field].reshape(plan.packed, plan.radial)
            tall[EXTRA : EXTRA + plan.radial, :] = flat.T
            for sector in range(plan.sectors):
                out[sector, side * plan.fields + field] = tall[sector * plan.mine : sector * plan.mine + plan.wide, :]


def pack(plan, state, below):
    return pl.pallas_call(
        functools.partial(pack_kernel, plan),
        in_specs=[whole(pl.ANY), whole(VMEM)],
        out_specs=whole(VMEM),
        out_shape=jax.ShapeDtypeStruct((plan.sectors, 2 * plan.fields, plan.wide, plan.packed), jnp.float32),
        scratch_shapes=[
            held((plan.fields, plan.deep, plan.cycle, plan.radial)),
            held((plan.radial + 2 * EXTRA, plan.packed)),
            pltpu.SemaphoreType.DMA((1,)),
        ],
        compiler_params=params(),
        name="pack_zone",
    )(state, below)


def zone_kernel(plan, place, offsets, speed, swirl, next_swirl, diffusion, coupling, weights, got, *refs):
    _, to_here, to_next, token, base, now, later, spread, matrix, made = refs
    token[...] = jnp.zeros(token.shape, jnp.float32)
    fields, deep, cycle, full, wide = plan.fields, plan.deep, plan.cycle, plan.full, plan.wide
    sections = offsets.shape[0]
    row, sector = place[0], place[1]
    terms = fields + 9
    rows = slice(LOW, LOW + wide)
    lane = lax.broadcasted_iota(jnp.int32, (wide, plan.packed), 1) // cycle
    own_lane = lax.broadcasted_iota(jnp.int32, (plan.mine, plan.packed), 1) // cycle
    at_radius = lax.broadcasted_iota(jnp.int32, (wide, full), 0) + sector * plan.mine - EXTRA
    inside = (at_radius >= 0) & (at_radius < plan.radial)
    block = plan.packed // cycle

    for side, w in enumerate((swirl, next_swirl)):
        for f, (axial, around, d, mix) in enumerate(coefficients(plan, speed, w, diffusion, coupling)):
            for number, factor in enumerate((d, *mix, *axial, *around)):
                spread[side * fields * terms + f * terms + number] = jnp.full((wide, full), factor, jnp.float32)

    for buffer in (base, now, later):
        for side in range(2):
            def clear(field, carry, buffer=buffer, side=side):
                buffer[side, field] = jnp.zeros(buffer.shape[2:], jnp.float32)
                return carry

            lax.fori_loop(0, fields, clear, 0)

    for side in range(2):
        def spread_out(field, carry, side=side):
            for plane in range(deep):
                parts = []
                for first in range(0, plan.sectors, block):
                    total = jnp.zeros((wide, plan.packed), jnp.float32)
                    for number in range(min(block, plan.sectors - first)):
                        turned = got[first + number, side * fields + field]
                        turn = (number - plane) * cycle % plan.packed
                        if turn:
                            turned = pltpu.roll(turned, turn, 1)
                        total = jnp.where(lane == number, turned, total)
                    parts.append(total)
                value = parts[0] if len(parts) == 1 else jnp.concatenate(parts, axis=1)
                base[side, field, 2 + plane, rows, :] = value
                now[side, field, 2 + plane, rows, :] = value
            return carry

        lax.fori_loop(0, fields, spread_out, 0)

    for section in range(sections):
        offset = offsets[section, jnp.minimum(row, offsets.shape[1] - 1)]
        for side in range(2):
            here = lax.rem(full - offset, full) if side == 0 else offset
            shift, cell = here // cycle, lax.rem(here, cycle)
            for target in range(plan.sectors):
                matrix[target * cycle : (target + 1) * cycle, :] = pltpu.roll(
                    weights[cell], lax.rem(target + shift, plan.sectors) * cycle, 1
                )
            other = 1 - side
            first = 2 if other == 1 else deep
            to = deep + 2 if side == 0 else 0
            pairs = [(field, plane) for field in range(fields) for plane in range(2)]
            values = [now[other, field, first + plane, rows, :] for field, plane in pairs]
            turn = matrix[...]
            together = wide % 8 == 0
            if together:
                values = [jnp.concatenate(values, axis=0)]
            results = [
                lax.dot_general(
                    value, turn, (((1,), (1,)), ((), ())), precision=highest, preferred_element_type=jnp.float32
                )
                for value in values
            ]
            for number, (field, plane) in enumerate(pairs):
                if together:
                    value = results[0][number * wide : (number + 1) * wide]
                else:
                    value = results[number]
                now[side, field, to + plane, rows, :] = value
                made[side, field, 2 * section + plane] = now[side, field, to + plane, LOW + EXTRA : LOW + EXTRA + plan.mine, :]
        if section == sections - 1:
            break
        size = deep - 2 * (section + 1)
        step_size = time_step if section == sections - 2 else 0.5 * time_step
        for side in range(2):
            begin = 2 + (deep - size if side == 0 else 0)

            def advance(number, carry, side=side, begin=begin, now=now, later=later, step_size=step_size):
                plane = begin + number
                center = [now[side, e, plane, rows, :] for e in range(fields)]
                for f in range(fields):
                    factor = lambda k: spread[side * fields * terms + f * terms + k]
                    total = factor(0) * (
                        now[side, f, plane, LOW - 1 : LOW - 1 + wide, :] + now[side, f, plane, LOW + 1 : LOW + 1 + wide, :]
                    )
                    for e in range(fields):
                        total += factor(1 + e) * center[e]
                    for place_at, by in enumerate((-2, -1, 1, 2)):
                        total += factor(1 + fields + place_at) * now[side, f, plane + by, rows, :]
                        total += factor(5 + fields + place_at) * pltpu.roll(center[f], -by % full, 1)
                    value = base[side, f, plane, rows, :] + step_size * total
                    later[side, f, plane, rows, :] = jnp.where(inside, value, 0.0)
                return carry

            lax.fori_loop(0, size, advance, 0)
        now, later = later, now

    has_next = (row < offsets.shape[1]).astype(jnp.float32)
    for side, out in enumerate((to_here, to_next)):
        def hand_out(field, carry, side=side, out=out):
            for target in range(plan.sectors):
                total = jnp.zeros((plan.mine, plan.packed), jnp.float32)
                first = target // block * plan.packed
                for number in range(2 * sections):
                    turned = made[side, field, number, :, first : first + plan.packed]
                    turn = (number - target % block) * cycle % plan.packed
                    if turn:
                        turned = pltpu.roll(turned, turn, 1)
                    total = jnp.where(own_lane == number, turned, total)
                out[target, field] = total * has_next if side == 0 else total
            return carry

        lax.fori_loop(0, fields, hand_out, 0)


def zone(plan, place, offsets, scalars, next_swirl, weights, got, after):
    speed, swirl, diffusion, coupling = scalars
    buffer = held((2, plan.fields, plan.deep + 4, LOW + plan.wide + 8, plan.full))
    rows = -(-(LOW + plan.wide + 8) // 8) * 8
    need = (3 * 2 * plan.fields * (plan.deep + 4) + 2 * plan.fields * (plan.fields + 9)) * rows * plan.full * 4
    sent = jax.ShapeDtypeStruct((plan.sectors, plan.fields, plan.mine, plan.packed), jnp.float32)
    return pl.pallas_call(
        functools.partial(zone_kernel, plan),
        in_specs=[whole(SMEM)] * 7 + [whole(VMEM)] * 3,
        out_specs=[whole(VMEM)] * 3,
        out_shape=[sent, sent, held((8, plan.radial))],
        scratch_shapes=[
            buffer,
            buffer,
            buffer,
            held((2 * plan.fields * (plan.fields + 9), plan.wide, plan.full)),
            held((plan.full, plan.full)),
            held((2, plan.fields, 2 * offsets.shape[0], plan.mine, plan.full)),
        ],
        compiler_params=pltpu.CompilerParams(vmem_limit_bytes=need + 6 * 1024 * 1024),
        name="step_zone",
    )(place, offsets, speed, swirl, next_swirl, diffusion, coupling, weights, got, near(after[0]))


def unpack_kernel(plan, got, _, *refs):
    *outs, token, tall = refs
    token[...] = jnp.zeros(token.shape, jnp.float32)
    for side in range(2):
        for field in range(plan.fields):
            for sector in range(plan.sectors):
                tall[sector * plan.mine : (sector + 1) * plan.mine, :] = got[sector, side * plan.fields + field]
            flat = tall[...].T
            for section, out in enumerate(outs):
                for plane in range(2):
                    start = (2 * section + plane) * plan.cycle
                    out[side, field, plane] = flat[start : start + plan.cycle]


def unpack(plan, got, sections, after):
    return pl.pallas_call(
        functools.partial(unpack_kernel, plan),
        in_specs=[whole(VMEM)] * 2,
        out_specs=[whole(VMEM)] * (sections + 1),
        out_shape=[held(plan.ghost)] * sections + [held((8, plan.radial))],
        scratch_shapes=[held((plan.radial, plan.packed))],
        compiler_params=params(),
        name="unpack_ghosts",
    )(got, near(after[0]))


def edge_shape(plan, kind):
    return held((plan.fields, plan.kept(kind) // 4, 8, plan.radial))


def first_kernel(plan, state, *refs):
    for at, (first, low_ref, high_ref) in enumerate(((0, *refs[:2]), (plan.middle, *refs[2:]))):

        def body(tile, carry, first=first, low_ref=low_ref, high_ref=high_ref):
            for field in range(plan.fields):
                for step in range(4):
                    plane = first + tile * 4 + step
                    rows = slice(2 * step, 2 * step + 2)
                    low_ref[field, tile, rows, :] = state[field, plane, 0:2, :]
                    high_ref[field, tile, rows, :] = state[field, plane, plan.cycle - 2 : plan.cycle, :]
            return carry

        lax.fori_loop(0, low_ref.shape[1], body, 0)


def first_edges(plan, state):
    low, high = edge_shape(plan, "low"), edge_shape(plan, "high")
    results = pl.pallas_call(
        functools.partial(first_kernel, plan),
        in_specs=[whole(VMEM)],
        out_specs=[whole(VMEM)] * 4,
        out_shape=[low, low, high, high],
        compiler_params=params(),
        name="first_edges",
    )(near(state))
    return results[:2], results[2:]


def coefficients(plan, speed, swirl, diffusion, coupling):
    twelfth = 1.0 / 12.0
    w = swirl[0]
    table = []
    for f in range(plan.fields):
        v, d = speed[f], diffusion[f]
        axial = ((-v - d) * twelfth, (8.0 * v + 16.0 * d) * twelfth, (16.0 * d - 8.0 * v) * twelfth, (v - d) * twelfth)
        cycle = ((-w - d) * twelfth, (8.0 * w + 16.0 * d) * twelfth, (16.0 * d - 8.0 * w) * twelfth, (w - d) * twelfth)
        mix = [coupling[f, e] - 7.0 * d if e == f else coupling[f, e] for e in range(plan.fields)]
        table.append((axial, cycle, d, mix))
    return table


def stage_kernel(plan, stage, kind, names, speed, swirl, diffusion, coupling, *refs):
    ref = dict(zip(names, refs))
    ranges = plan.ranges(kind, stage)
    cycle, radial, last = plan.cycle, plan.radial, stage == 3
    state, work, spread = ref["state"], ref["work"], ref["spread"]
    terms = plan.fields + 9
    for f, (axial, around, d, mix) in enumerate(coefficients(plan, speed, swirl, diffusion, coupling)):
        for number, factor in enumerate((d, *mix, *axial, *around)):
            spread[f * terms + number] = jnp.full((8, radial), factor, jnp.float32)
    lane = lax.broadcasted_iota(jnp.int32, (8, radial), 1)
    not_first = lane > 0
    not_last = lane < radial - 1

    def cells(plane, level):
        if plane < 0:
            return ref["ghosts"][0, :, plane + 2]
        if plane >= plan.axial:
            return ref["ghosts"][1, :, plane - plan.axial]
        if level == 0:
            return state[:, plane]
        owner, at = plan.owner(plane, level)
        return ref["cells", level, owner][:, at]

    copies = []
    for number, (low, high) in enumerate(ranges):
        size = high - low
        for plane in range(low - 2, high + 2):
            work[:, plane - low + 2, LOW : LOW + cycle, :] = cells(plane, stage)
        for plane in range(low, high):
            owner, at = plan.owner(plane, stage)
            rows = slice(2 * (at % 4), 2 * (at % 4) + 2)
            work[:, plane - low + 2, LOW - 2 : LOW, :] = ref["low halo", owner][:, at // 4, rows, :]
            work[:, plane - low + 2, LOW + cycle : LOW + cycle + 2, :] = ref["high halo", owner][:, at // 4, rows, :]
            if last:
                ref["earlier"][:, plane - low] = cells(plane, 1) + 2.0 * cells(plane, 2)
        start = plan.place(kind, low)

        def compute(tile, steps, low=low, start=start, number=number):
            for f in range(plan.fields):
                factors = [spread[f * terms + number] for number in range(terms)]
                values = {}
                for step in steps:
                    at = tile * 4 + step - start % 4
                    for row in range(0, cycle, 8):
                        here = slice(LOW + row, LOW + row + 8)
                        center = work[f, at + 2, here, :]
                        left = jnp.where(not_first, pltpu.roll(center, 1, 1), 0.0)
                        right = jnp.where(not_last, pltpu.roll(center, radial - 1, 1), 0.0)
                        total = factors[0] * (left + right)
                        for e in range(plan.fields):
                            total += factors[1 + e] * (center if e == f else work[e, at + 2, here, :])
                        for place, by in enumerate((-2, -1, 1, 2)):
                            total += factors[1 + plan.fields + place] * work[f, at + 2 + by, here, :]
                            beside = slice(LOW + row + by, LOW + row + by + 8)
                            total += factors[5 + plan.fields + place] * work[f, at + 2, beside, :]
                        base = state[f, low + at, row : row + 8, :]
                        if last:
                            value = (ref["earlier"][f, at, row : row + 8, :] + center - base) * (1.0 / 3.0)
                            value += (time_step / 6.0) * total
                        else:
                            value = base + (time_step if stage == 2 else 0.5 * time_step) * total
                        values[step, row] = value
                for (step, row), value in values.items():
                    at = tile * 4 + step - start % 4
                    if last:
                        ref["made"][number, f, at, row : row + 8, :] = value
                        continue
                    ref["out"][f, start + at, row : row + 8, :] = value
                    rows = slice(2 * step, 2 * step + 2)
                    if row == 0:
                        ref["low edge"][f, start // 4 + tile, rows, :] = value[:2]
                    if row == cycle - 8:
                        ref["high edge"][f, start // 4 + tile, rows, :] = value[6:]

        head = start % 4
        tiles = (head + size) // 4
        if head:
            compute(0, range(head, min(4, head + size)))
        first = 1 if head else 0

        def whole_tile(tile, carry, compute=compute):
            compute(tile, range(4))
            return carry

        if tiles > first:
            lax.fori_loop(first, tiles, whole_tile, 0)
        tail = (head + size) % 4
        if tail and tiles >= first:
            compute(tiles, range(tail))
        if last:
            copies.append(
                pltpu.make_async_copy(
                    ref["made"].at[number, :, 0:size], ref["result"].at[:, low:high], ref["sem"].at[number]
                )
            )
            copies[-1].start()
    for item in copies:
        item.wait()
    ref["token"][...] = jnp.zeros(ref["token"].shape, jnp.float32)


def stage_call(plan, stage, kind, scalars, state, levels, halos, ghosts, after, result=None):
    ranges = plan.ranges(kind, stage)
    last = stage == 3
    longest = max(high - low for low, high in ranges)
    operands = {"state": near(state)}
    specs = [whole(VMEM)]

    def add(name, value):
        operands[name] = near(value)
        specs.append(whole(VMEM))

    kinds = {plan.owner(plane, stage)[0] for low, high in ranges for plane in range(low, high)}
    for owner in sorted(kinds):
        add(("low halo", owner), halos[owner][0])
        add(("high halo", owner), halos[owner][1])
    for level in (1, 2, stage) if last else (stage,) if stage else ():
        edge = 2 if level == stage else 0
        planes = [plane for low, high in ranges for plane in range(max(0, low - edge), min(plan.axial, high + edge))]
        for owner in sorted({plan.owner(plane, level)[0] for plane in planes}):
            add(("cells", level, owner), levels[level][owner])
    if kind == "ends":
        add("ghosts", ghosts)
    for number, token in enumerate(after):
        add(("after", number), token)
    aliases = {}
    if result is not None:
        aliases = {len(scalars) + len(operands): 0}
        operands["earlier result"] = result
        specs.append(whole(pl.ANY))
    token = held((8, plan.radial))
    if last:
        outs = {"result": jax.ShapeDtypeStruct(state.shape, jnp.float32), "token": token}
    else:
        edges = edge_shape(plan, kind)
        cells = held((plan.fields, plan.kept(kind), plan.cycle, plan.radial))
        outs = {"out": cells, "low edge": edges, "high edge": edges, "token": token}
    scratch = {
        "work": held((plan.fields, longest + 4, plan.cycle + 16, plan.radial)),
        "spread": held((plan.fields * (plan.fields + 9), 8, plan.radial)),
    }
    if last:
        scratch["earlier"] = held((plan.fields, longest, plan.cycle, plan.radial))
        scratch["made"] = held((len(ranges), plan.fields, longest, plan.cycle, plan.radial))
        scratch["sem"] = pltpu.SemaphoreType.DMA((len(ranges),))
    names = (*operands, *outs, *scratch)
    return pl.pallas_call(
        functools.partial(stage_kernel, plan, stage, kind, names),
        in_specs=[whole(SMEM)] * len(scalars) + specs,
        out_specs=[whole(pl.ANY if name == "result" else VMEM) for name in outs],
        out_shape=list(outs.values()),
        scratch_shapes=list(scratch.values()),
        input_output_aliases=aliases,
        compiler_params=params(),
        name=f"stage{stage}_{kind}",
    )(*scalars, *operands.values())


def exchange(edges):
    size = lax.axis_size("sector")
    ahead = [(i, (i + 1) % size) for i in range(size)]
    back = [(i, (i - 1) % size) for i in range(size)]
    low_edges, high_edges = edges
    return lax.ppermute(high_edges, "sector", ahead), lax.ppermute(low_edges, "sector", back)


def on_device(state, interp_blocks, rotor_offset, axial_speed, row_swirl, diffusivity, coupling):
    plan = Plan(state, lax.axis_size("sector"))
    rows = lax.axis_size("row")
    sections = rotor_offset.shape[0]
    place = jnp.stack([lax.axis_index("row"), lax.axis_index("sector")]).astype(jnp.int32)
    scalars = (axial_speed, row_swirl, diffusivity, coupling)
    back = [(row + 1, row) for row in range(rows - 1)]
    ahead = [(row, row + 1) for row in range(rows - 1)]

    below = lax.ppermute(state[:, : plan.deep], "row", back)
    next_swirl = lax.ppermute(row_swirl, "row", back)
    weights = jnp.pad(interp_blocks, ((0, 0), (0, 0), (0, plan.full - interp_blocks.shape[2])))
    packed = pack(plan, state, below)
    got = lax.all_to_all(packed, "sector", 0, 0, tiled=True)

    levels, halos = [None], [{}]
    edges = dict(zip(("low", "high"), first_edges(plan, state)))
    halos[0] = {kind: exchange(edges[kind]) for kind in ("low", "high")}
    token, result, ghosts = (), None, None

    def step(stage, kind):
        nonlocal token, result
        ghost = ghosts[stage] if kind == "ends" else None
        outs = stage_call(plan, stage, kind, scalars, state, levels, halos[stage], ghost, token, result)
        token = outs[-1:]
        if stage == sections - 1:
            result = outs[0]
            return
        if len(levels) == stage + 1:
            levels.append({})
            halos.append({})
        levels[stage + 1][kind] = outs[0]
        halos[stage + 1][kind] = exchange(outs[1:3])

    step(0, "low")
    step(0, "high")
    downstream, to_next, *token = zone(plan, place, rotor_offset, scalars, next_swirl, weights, got, token)
    upstream = lax.ppermute(to_next, "row", ahead)
    returned = lax.all_to_all(jnp.concatenate([upstream, downstream], axis=1), "sector", 0, 0, tiled=True)
    step(1, "low")
    step(1, "high")
    *ghosts, last_token = unpack(plan, returned, sections, token)
    token = (last_token,)
    step(0, "ends")
    step(2, "low")
    step(1, "ends")
    step(2, "high")
    step(2, "ends")
    step(3, "low")
    step(3, "high")
    step(3, "ends")
    return result


def solution(mesh):
    return jax.shard_map(
        on_device,
        mesh=mesh,
        in_specs=(P(None, "row", "sector", None), P(), P(), P(), P("row"), P(), P()),
        out_specs=P(None, "row", "sector", None),
        check_vma=False,
    )
```

```python
import functools

import jax
import jax.numpy as jnp
from jax import lax
from jax.experimental import pallas as pl
from jax.experimental.pallas import tpu as pltpu
from jax.sharding import PartitionSpec as P

time_step = 0.4
highest = lax.Precision.HIGHEST
VMEM = pltpu.VMEM
SMEM = pltpu.SMEM
EXTRA = 4
LOW = 8


def whole(space):
    return pl.BlockSpec(memory_space=space)


def held(shape):
    return pltpu.VMEM(tuple(shape), jnp.float32)


def near(value):
    return pltpu.with_memory_space_constraint(value, pltpu.VMEM)


def params():
    return pltpu.CompilerParams(vmem_limit_bytes=16 * 1024 * 1024)


class Plan:
    def __init__(self, state, sectors):
        self.fields, self.axial, self.cycle, self.radial = state.shape
        self.sectors = sectors
        self.middle = self.axial // 8 * 4
        self.ghost = (2, self.fields, 2, self.cycle, self.radial)
        self.ends = 8
        self.deep = 8
        self.full = self.cycle * sectors
        self.mine = self.radial // sectors
        self.wide = self.mine + 2 * EXTRA
        self.packed = self.deep * self.cycle


    def ranges(self, kind, stage):
        reach = 2 * (stage + 1)
        if kind == "low":
            return ((reach, self.middle),)
        if kind == "high":
            return ((self.middle, self.axial - reach),)
        return ((0, reach), (self.axial - reach, self.axial))

    def kept(self, kind):
        return {"low": self.middle, "high": self.axial - self.middle, "ends": 2 * self.ends}[kind]

    def owner(self, plane, stage):
        reach = 2 * stage
        if plane < reach:
            return "ends", plane
        if plane >= self.axial - reach:
            return "ends", plane - self.axial + 2 * self.ends
        return ("low", plane) if plane < self.middle else ("high", plane - self.middle)

    def place(self, kind, plane):
        if kind == "ends":
            return plane if plane < self.middle else plane - self.axial + 2 * self.ends
        return plane if kind == "low" else plane - self.middle


def pack_kernel(plan, state, below, out, planes, tall, sem):
    copy = pltpu.make_async_copy(state.at[:, plan.axial - plan.deep : plan.axial], planes, sem.at[0])
    copy.start()
    tall[...] = jnp.zeros(tall.shape, jnp.float32)
    copy.wait()
    for side, source in enumerate((planes, below)):
        for field in range(plan.fields):
            flat = source[field].reshape(plan.packed, plan.radial)
            tall[EXTRA : EXTRA + plan.radial, :] = flat.T
            for sector in range(plan.sectors):
                out[sector, side * plan.fields + field] = tall[sector * plan.mine : sector * plan.mine + plan.wide, :]


def pack(plan, state, below):
    return pl.pallas_call(
        functools.partial(pack_kernel, plan),
        in_specs=[whole(pl.ANY), whole(VMEM)],
        out_specs=whole(VMEM),
        out_shape=jax.ShapeDtypeStruct((plan.sectors, 2 * plan.fields, plan.wide, plan.packed), jnp.float32),
        scratch_shapes=[
            held((plan.fields, plan.deep, plan.cycle, plan.radial)),
            held((plan.radial + 2 * EXTRA, plan.packed)),
            pltpu.SemaphoreType.DMA((1,)),
        ],
        cost_estimate=pl.CostEstimate(flops=10000000000, transcendentals=0, bytes_accessed=10000000),
        compiler_params=params(),
        name="pack_zone",
    )(state, below)


def zone_kernel(plan, place, offsets, speed, swirl, next_swirl, diffusion, coupling, weights, got, *refs):
    _, to_here, to_next, token, base, now, later, spread, matrix, made = refs
    token[...] = jnp.zeros(token.shape, jnp.float32)
    fields, deep, cycle, full, wide = plan.fields, plan.deep, plan.cycle, plan.full, plan.wide
    sections = offsets.shape[0]
    row, sector = place[0], place[1]
    terms = fields + 9
    rows = slice(LOW, LOW + wide)
    lane = lax.broadcasted_iota(jnp.int32, (wide, plan.packed), 1) // cycle
    own_lane = lax.broadcasted_iota(jnp.int32, (plan.mine, plan.packed), 1) // cycle
    at_radius = lax.broadcasted_iota(jnp.int32, (wide, full), 0) + sector * plan.mine - EXTRA
    inside = (at_radius >= 0) & (at_radius < plan.radial)
    block = plan.packed // cycle

    for side, w in enumerate((swirl, next_swirl)):
        for f, (axial, around, d, mix) in enumerate(coefficients(plan, speed, w, diffusion, coupling)):
            for number, factor in enumerate((d, *mix, *axial, *around)):
                spread[side * fields * terms + f * terms + number] = jnp.full((wide, full), factor, jnp.float32)

    for buffer in (base, now, later):
        for side in range(2):
            def clear(field, carry, buffer=buffer, side=side):
                buffer[side, field] = jnp.zeros(buffer.shape[2:], jnp.float32)
                return carry

            lax.fori_loop(0, fields, clear, 0)

    for side in range(2):
        def spread_out(field, carry, side=side):
            for plane in range(deep):
                parts = []
                for first in range(0, plan.sectors, block):
                    total = jnp.zeros((wide, plan.packed), jnp.float32)
                    for number in range(min(block, plan.sectors - first)):
                        turned = got[first + number, side * fields + field]
                        turn = (number - plane) * cycle % plan.packed
                        if turn:
                            turned = pltpu.roll(turned, turn, 1)
                        total = jnp.where(lane == number, turned, total)
                    parts.append(total)
                value = parts[0] if len(parts) == 1 else jnp.concatenate(parts, axis=1)
                base[side, field, 2 + plane, rows, :] = value
                now[side, field, 2 + plane, rows, :] = value
            return carry

        lax.fori_loop(0, fields, spread_out, 0)

    for section in range(sections):
        offset = offsets[section, jnp.minimum(row, offsets.shape[1] - 1)]
        for side in range(2):
            here = lax.rem(full - offset, full) if side == 0 else offset
            shift, cell = here // cycle, lax.rem(here, cycle)
            for target in range(plan.sectors):
                matrix[target * cycle : (target + 1) * cycle, :] = pltpu.roll(
                    weights[cell], lax.rem(target + shift, plan.sectors) * cycle, 1
                )
            other = 1 - side
            first = 2 if other == 1 else deep
            to = deep + 2 if side == 0 else 0
            pairs = [(field, plane) for field in range(fields) for plane in range(2)]
            values = [now[other, field, first + plane, rows, :] for field, plane in pairs]
            turn = matrix[...]
            together = wide % 8 == 0
            if together:
                values = [jnp.concatenate(values, axis=0)]
            results = [
                lax.dot_general(
                    value, turn, (((1,), (1,)), ((), ())), precision=highest, preferred_element_type=jnp.float32
                )
                for value in values
            ]
            for number, (field, plane) in enumerate(pairs):
                if together:
                    value = results[0][number * wide : (number + 1) * wide]
                else:
                    value = results[number]
                now[side, field, to + plane, rows, :] = value
                made[side, field, 2 * section + plane] = now[side, field, to + plane, LOW + EXTRA : LOW + EXTRA + plan.mine, :]
        if section == sections - 1:
            break
        size = deep - 2 * (section + 1)
        step_size = time_step if section == sections - 2 else 0.5 * time_step
        for side in range(2):
            begin = 2 + (deep - size if side == 0 else 0)

            def advance(number, carry, side=side, begin=begin, now=now, later=later, step_size=step_size):
                plane = begin + number
                center = [now[side, e, plane, rows, :] for e in range(fields)]
                for f in range(fields):
                    factor = lambda k: spread[side * fields * terms + f * terms + k]
                    total = factor(0) * (
                        now[side, f, plane, LOW - 1 : LOW - 1 + wide, :] + now[side, f, plane, LOW + 1 : LOW + 1 + wide, :]
                    )
                    for e in range(fields):
                        total += factor(1 + e) * center[e]
                    for place_at, by in enumerate((-2, -1, 1, 2)):
                        total += factor(1 + fields + place_at) * now[side, f, plane + by, rows, :]
                        total += factor(5 + fields + place_at) * pltpu.roll(center[f], -by % full, 1)
                    value = base[side, f, plane, rows, :] + step_size * total
                    later[side, f, plane, rows, :] = jnp.where(inside, value, 0.0)
                return carry

            lax.fori_loop(0, size, advance, 0)
        now, later = later, now

    has_next = (row < offsets.shape[1]).astype(jnp.float32)
    for side, out in enumerate((to_here, to_next)):
        def hand_out(field, carry, side=side, out=out):
            for target in range(plan.sectors):
                total = jnp.zeros((plan.mine, plan.packed), jnp.float32)
                first = target // block * plan.packed
                for number in range(2 * sections):
                    turned = made[side, field, number, :, first : first + plan.packed]
                    turn = (number - target % block) * cycle % plan.packed
                    if turn:
                        turned = pltpu.roll(turned, turn, 1)
                    total = jnp.where(own_lane == number, turned, total)
                out[target, field] = total * has_next if side == 0 else total
            return carry

        lax.fori_loop(0, fields, hand_out, 0)


def zone(plan, place, offsets, scalars, next_swirl, weights, got, after):
    speed, swirl, diffusion, coupling = scalars
    buffer = held((2, plan.fields, plan.deep + 4, LOW + plan.wide + 8, plan.full))
    rows = -(-(LOW + plan.wide + 8) // 8) * 8
    need = (3 * 2 * plan.fields * (plan.deep + 4) + 2 * plan.fields * (plan.fields + 9)) * rows * plan.full * 4
    sent = jax.ShapeDtypeStruct((plan.sectors, plan.fields, plan.mine, plan.packed), jnp.float32)
    return pl.pallas_call(
        functools.partial(zone_kernel, plan),
        in_specs=[whole(SMEM)] * 7 + [whole(VMEM)] * 3,
        out_specs=[whole(VMEM)] * 3,
        out_shape=[sent, sent, held((8, plan.radial))],
        scratch_shapes=[
            buffer,
            buffer,
            buffer,
            held((2 * plan.fields * (plan.fields + 9), plan.wide, plan.full)),
            held((plan.full, plan.full)),
            held((2, plan.fields, 2 * offsets.shape[0], plan.mine, plan.full)),
        ],
        cost_estimate=pl.CostEstimate(flops=10000000000, transcendentals=0, bytes_accessed=10000000),
        compiler_params=pltpu.CompilerParams(vmem_limit_bytes=need + 6 * 1024 * 1024),
        name="step_zone",
    )(place, offsets, speed, swirl, next_swirl, diffusion, coupling, weights, got, near(after[0]))


def unpack_kernel(plan, got, _, *refs):
    *outs, token, tall = refs
    token[...] = jnp.zeros(token.shape, jnp.float32)
    for side in range(2):
        for field in range(plan.fields):
            for sector in range(plan.sectors):
                tall[sector * plan.mine : (sector + 1) * plan.mine, :] = got[sector, side * plan.fields + field]
            flat = tall[...].T
            for section, out in enumerate(outs):
                for plane in range(2):
                    start = (2 * section + plane) * plan.cycle
                    out[side, field, plane] = flat[start : start + plan.cycle]


def unpack(plan, got, sections, after):
    return pl.pallas_call(
        functools.partial(unpack_kernel, plan),
        in_specs=[whole(VMEM)] * 2,
        out_specs=[whole(VMEM)] * (sections + 1),
        out_shape=[held(plan.ghost)] * sections + [held((8, plan.radial))],
        scratch_shapes=[held((plan.radial, plan.packed))],
        cost_estimate=pl.CostEstimate(flops=10000000000, transcendentals=0, bytes_accessed=10000000),
        compiler_params=params(),
        name="unpack_ghosts",
    )(got, near(after[0]))


def edge_shape(plan, kind):
    return held((plan.fields, plan.kept(kind) // 4, 8, plan.radial))


def first_kernel(plan, state, *refs):
    for at, (first, low_ref, high_ref) in enumerate(((0, *refs[:2]), (plan.middle, *refs[2:]))):

        def body(tile, carry, first=first, low_ref=low_ref, high_ref=high_ref):
            for field in range(plan.fields):
                for step in range(4):
                    plane = first + tile * 4 + step
                    rows = slice(2 * step, 2 * step + 2)
                    low_ref[field, tile, rows, :] = state[field, plane, 0:2, :]
                    high_ref[field, tile, rows, :] = state[field, plane, plan.cycle - 2 : plan.cycle, :]
            return carry

        lax.fori_loop(0, low_ref.shape[1], body, 0)


def first_edges(plan, state):
    low, high = edge_shape(plan, "low"), edge_shape(plan, "high")
    results = pl.pallas_call(
        functools.partial(first_kernel, plan),
        in_specs=[whole(VMEM)],
        out_specs=[whole(VMEM)] * 4,
        out_shape=[low, low, high, high],
        cost_estimate=pl.CostEstimate(flops=10000000000, transcendentals=0, bytes_accessed=10000000),
        compiler_params=params(),
        name="first_edges",
    )(near(state))
    return results[:2], results[2:]


def coefficients(plan, speed, swirl, diffusion, coupling):
    twelfth = 1.0 / 12.0
    w = swirl[0]
    table = []
    for f in range(plan.fields):
        v, d = speed[f], diffusion[f]
        axial = ((-v - d) * twelfth, (8.0 * v + 16.0 * d) * twelfth, (16.0 * d - 8.0 * v) * twelfth, (v - d) * twelfth)
        cycle = ((-w - d) * twelfth, (8.0 * w + 16.0 * d) * twelfth, (16.0 * d - 8.0 * w) * twelfth, (w - d) * twelfth)
        mix = [coupling[f, e] - 7.0 * d if e == f else coupling[f, e] for e in range(plan.fields)]
        table.append((axial, cycle, d, mix))
    return table


def stage_kernel(plan, stage, kind, names, speed, swirl, diffusion, coupling, *refs):
    ref = dict(zip(names, refs))
    ranges = plan.ranges(kind, stage)
    cycle, radial, last = plan.cycle, plan.radial, stage == 3
    state, work, spread = ref["state"], ref["work"], ref["spread"]
    terms = plan.fields + 9
    for f, (axial, around, d, mix) in enumerate(coefficients(plan, speed, swirl, diffusion, coupling)):
        for number, factor in enumerate((d, *mix, *axial, *around)):
            spread[f * terms + number] = jnp.full((8, radial), factor, jnp.float32)
    lane = lax.broadcasted_iota(jnp.int32, (8, radial), 1)
    not_first = lane > 0
    not_last = lane < radial - 1

    def cells(plane, level):
        if plane < 0:
            return ref["ghosts"][0, :, plane + 2]
        if plane >= plan.axial:
            return ref["ghosts"][1, :, plane - plan.axial]
        if level == 0:
            return state[:, plane]
        owner, at = plan.owner(plane, level)
        return ref["cells", level, owner][:, at]

    copies = []
    for number, (low, high) in enumerate(ranges):
        size = high - low
        for plane in range(low - 2, high + 2):
            work[:, plane - low + 2, LOW : LOW + cycle, :] = cells(plane, stage)
        for plane in range(low, high):
            owner, at = plan.owner(plane, stage)
            rows = slice(2 * (at % 4), 2 * (at % 4) + 2)
            work[:, plane - low + 2, LOW - 2 : LOW, :] = ref["low halo", owner][:, at // 4, rows, :]
            work[:, plane - low + 2, LOW + cycle : LOW + cycle + 2, :] = ref["high halo", owner][:, at // 4, rows, :]
            if last:
                ref["earlier"][:, plane - low] = cells(plane, 1) + 2.0 * cells(plane, 2)
        start = plan.place(kind, low)

        def compute(tile, steps, low=low, start=start, number=number):
            for f in range(plan.fields):
                factors = [spread[f * terms + number] for number in range(terms)]
                values = {}
                for step in steps:
                    at = tile * 4 + step - start % 4
                    for row in range(0, cycle, 8):
                        here = slice(LOW + row, LOW + row + 8)
                        center = work[f, at + 2, here, :]
                        left = jnp.where(not_first, pltpu.roll(center, 1, 1), 0.0)
                        right = jnp.where(not_last, pltpu.roll(center, radial - 1, 1), 0.0)
                        total = factors[0] * (left + right)
                        for e in range(plan.fields):
                            total += factors[1 + e] * (center if e == f else work[e, at + 2, here, :])
                        for place, by in enumerate((-2, -1, 1, 2)):
                            total += factors[1 + plan.fields + place] * work[f, at + 2 + by, here, :]
                            beside = slice(LOW + row + by, LOW + row + by + 8)
                            total += factors[5 + plan.fields + place] * work[f, at + 2, beside, :]
                        base = state[f, low + at, row : row + 8, :]
                        if last:
                            value = (ref["earlier"][f, at, row : row + 8, :] + center - base) * (1.0 / 3.0)
                            value += (time_step / 6.0) * total
                        else:
                            value = base + (time_step if stage == 2 else 0.5 * time_step) * total
                        values[step, row] = value
                for (step, row), value in values.items():
                    at = tile * 4 + step - start % 4
                    if last:
                        ref["made"][number, f, at, row : row + 8, :] = value
                        continue
                    ref["out"][f, start + at, row : row + 8, :] = value
                    rows = slice(2 * step, 2 * step + 2)
                    if row == 0:
                        ref["low edge"][f, start // 4 + tile, rows, :] = value[:2]
                    if row == cycle - 8:
                        ref["high edge"][f, start // 4 + tile, rows, :] = value[6:]

        head = start % 4
        tiles = (head + size) // 4
        if head:
            compute(0, range(head, min(4, head + size)))
        first = 1 if head else 0

        def whole_tile(tile, carry, compute=compute):
            compute(tile, range(4))
            return carry

        if tiles > first:
            lax.fori_loop(first, tiles, whole_tile, 0)
        tail = (head + size) % 4
        if tail and tiles >= first:
            compute(tiles, range(tail))
        if last:
            copies.append(
                pltpu.make_async_copy(
                    ref["made"].at[number, :, 0:size], ref["result"].at[:, low:high], ref["sem"].at[number]
                )
            )
            copies[-1].start()
    for item in copies:
        item.wait()
    ref["token"][...] = jnp.zeros(ref["token"].shape, jnp.float32)


def stage_call(plan, stage, kind, scalars, state, levels, halos, ghosts, after, result=None):
    ranges = plan.ranges(kind, stage)
    last = stage == 3
    longest = max(high - low for low, high in ranges)
    operands = {"state": near(state)}
    specs = [whole(VMEM)]

    def add(name, value):
        operands[name] = near(value)
        specs.append(whole(VMEM))

    kinds = {plan.owner(plane, stage)[0] for low, high in ranges for plane in range(low, high)}
    for owner in sorted(kinds):
        add(("low halo", owner), halos[owner][0])
        add(("high halo", owner), halos[owner][1])
    for level in (1, 2, stage) if last else (stage,) if stage else ():
        edge = 2 if level == stage else 0
        planes = [plane for low, high in ranges for plane in range(max(0, low - edge), min(plan.axial, high + edge))]
        for owner in sorted({plan.owner(plane, level)[0] for plane in planes}):
            add(("cells", level, owner), levels[level][owner])
    if kind == "ends":
        add("ghosts", ghosts)
    for number, token in enumerate(after):
        add(("after", number), token)
    aliases = {}
    if result is not None:
        aliases = {len(scalars) + len(operands): 0}
        operands["earlier result"] = result
        specs.append(whole(pl.ANY))
    token = held((8, plan.radial))
    if last:
        outs = {"result": jax.ShapeDtypeStruct(state.shape, jnp.float32), "token": token}
    else:
        edges = edge_shape(plan, kind)
        cells = held((plan.fields, plan.kept(kind), plan.cycle, plan.radial))
        outs = {"out": cells, "low edge": edges, "high edge": edges, "token": token}
    scratch = {
        "work": held((plan.fields, longest + 4, plan.cycle + 16, plan.radial)),
        "spread": held((plan.fields * (plan.fields + 9), 8, plan.radial)),
    }
    if last:
        scratch["earlier"] = held((plan.fields, longest, plan.cycle, plan.radial))
        scratch["made"] = held((len(ranges), plan.fields, longest, plan.cycle, plan.radial))
        scratch["sem"] = pltpu.SemaphoreType.DMA((len(ranges),))
    names = (*operands, *outs, *scratch)
    return pl.pallas_call(
        functools.partial(stage_kernel, plan, stage, kind, names),
        in_specs=[whole(SMEM)] * len(scalars) + specs,
        out_specs=[whole(pl.ANY if name == "result" else VMEM) for name in outs],
        out_shape=list(outs.values()),
        scratch_shapes=list(scratch.values()),
        input_output_aliases=aliases,
        cost_estimate=pl.CostEstimate(flops=10000000000, transcendentals=0, bytes_accessed=10000000),
        compiler_params=params(),
        name=f"stage{stage}_{kind}",
    )(*scalars, *operands.values())


def exchange(edges):
    size = lax.axis_size("sector")
    ahead = [(i, (i + 1) % size) for i in range(size)]
    back = [(i, (i - 1) % size) for i in range(size)]
    low_edges, high_edges = edges
    return lax.ppermute(high_edges, "sector", ahead), lax.ppermute(low_edges, "sector", back)


def on_device(state, interp_blocks, rotor_offset, axial_speed, row_swirl, diffusivity, coupling):
    plan = Plan(state, lax.axis_size("sector"))
    rows = lax.axis_size("row")
    sections = rotor_offset.shape[0]
    place = jnp.stack([lax.axis_index("row"), lax.axis_index("sector")]).astype(jnp.int32)
    scalars = (axial_speed, row_swirl, diffusivity, coupling)
    back = [(row + 1, row) for row in range(rows - 1)]
    ahead = [(row, row + 1) for row in range(rows - 1)]

    below = lax.ppermute(state[:, : plan.deep], "row", back)
    next_swirl = lax.ppermute(row_swirl, "row", back)
    weights = jnp.pad(interp_blocks, ((0, 0), (0, 0), (0, plan.full - interp_blocks.shape[2])))
    packed = pack(plan, state, below)
    levels, halos = [None], [{}]
    edges = dict(zip(("low", "high"), first_edges(plan, state)))
    halos[0] = {"low": exchange(edges["low"])}
    packed, *halos[0]["low"] = lax.optimization_barrier((packed, *halos[0]["low"]))
    got = lax.all_to_all(packed, "sector", 0, 0, tiled=True)
    token, result, ghosts = (), None, None

    def step(stage, kind):
        nonlocal token, result
        ghost = ghosts[stage] if kind == "ends" else None
        outs = stage_call(plan, stage, kind, scalars, state, levels, halos[stage], ghost, token, result)
        token = outs[-1:]
        if stage == sections - 1:
            result = outs[0]
            return
        if len(levels) == stage + 1:
            levels.append({})
            halos.append({})
        levels[stage + 1][kind] = outs[0]
        halos[stage + 1][kind] = exchange(outs[1:3])

    step(0, "low")
    *high_edges, first_token = lax.optimization_barrier((*edges["high"], *token))
    halos[0]["high"] = exchange(high_edges)
    token = (first_token,)
    downstream, to_next, *token = zone(plan, place, rotor_offset, scalars, next_swirl, weights, got, token)
    upstream = lax.ppermute(to_next, "row", ahead)
    step(0, "high")
    joined, *token = lax.optimization_barrier((jnp.concatenate([upstream, downstream], axis=1), *token))
    returned = lax.all_to_all(joined, "sector", 0, 0, tiled=True)
    step(1, "low")
    step(1, "high")
    *ghosts, last_token = unpack(plan, returned, sections, token)
    token = (last_token,)
    step(0, "ends")
    step(2, "low")
    step(1, "ends")
    step(2, "high")
    step(2, "ends")
    step(3, "low")
    step(3, "high")
    step(3, "ends")
    return result


def solution(mesh):
    return jax.shard_map(
        on_device,
        mesh=mesh,
        in_specs=(P(None, "row", "sector", None), P(), P(), P(), P("row"), P(), P()),
        out_specs=P(None, "row", "sector", None),
        check_vma=False,
    )
```

```python
import functools

import jax
import jax.numpy as jnp
from jax import lax
from jax.experimental import pallas as pl
from jax.experimental.pallas import tpu as pltpu
from jax.sharding import PartitionSpec as P

time_step = 0.4
highest = lax.Precision.HIGHEST
VMEM = pltpu.VMEM
SMEM = pltpu.SMEM
EXTRA = 4
LOW = 8


def whole(space):
    return pl.BlockSpec(memory_space=space)


def held(shape):
    return pltpu.VMEM(tuple(shape), jnp.float32)


def near(value):
    return pltpu.with_memory_space_constraint(value, pltpu.VMEM)


def params():
    return pltpu.CompilerParams(vmem_limit_bytes=16 * 1024 * 1024)


class Plan:
    def __init__(self, state, sectors):
        self.fields, self.axial, self.cycle, self.radial = state.shape
        self.sectors = sectors
        self.middle = self.axial // 8 * 4
        self.ghost = (2, self.fields, 2, self.cycle, self.radial)
        self.ends = 8
        self.deep = 8
        self.full = self.cycle * sectors
        self.mine = self.radial // sectors
        self.wide = self.mine + 2 * EXTRA
        self.packed = self.deep * self.cycle


    def ranges(self, kind, stage):
        reach = 2 * (stage + 1)
        if kind == "low":
            return ((reach, self.middle),)
        if kind == "high":
            return ((self.middle, self.axial - reach),)
        return ((0, reach), (self.axial - reach, self.axial))

    def kept(self, kind):
        return {"low": self.middle, "high": self.axial - self.middle, "ends": 2 * self.ends}[kind]

    def owner(self, plane, stage):
        reach = 2 * stage
        if plane < reach:
            return "ends", plane
        if plane >= self.axial - reach:
            return "ends", plane - self.axial + 2 * self.ends
        return ("low", plane) if plane < self.middle else ("high", plane - self.middle)

    def place(self, kind, plane):
        if kind == "ends":
            return plane if plane < self.middle else plane - self.axial + 2 * self.ends
        return plane if kind == "low" else plane - self.middle


def pack_kernel(plan, state, below, out, planes, tall, sem):
    copy = pltpu.make_async_copy(state.at[:, plan.axial - plan.deep : plan.axial], planes, sem.at[0])
    copy.start()
    tall[...] = jnp.zeros(tall.shape, jnp.float32)
    copy.wait()
    for side, source in enumerate((planes, below)):
        for field in range(plan.fields):
            flat = source[field].reshape(plan.packed, plan.radial)
            tall[EXTRA : EXTRA + plan.radial, :] = flat.T
            for sector in range(plan.sectors):
                out[sector, side * plan.fields + field] = tall[sector * plan.mine : sector * plan.mine + plan.wide, :]


def pack(plan, state, below):
    return pl.pallas_call(
        functools.partial(pack_kernel, plan),
        in_specs=[whole(pl.ANY), whole(VMEM)],
        out_specs=whole(VMEM),
        out_shape=jax.ShapeDtypeStruct((plan.sectors, 2 * plan.fields, plan.wide, plan.packed), jnp.float32),
        scratch_shapes=[
            held((plan.fields, plan.deep, plan.cycle, plan.radial)),
            held((plan.radial + 2 * EXTRA, plan.packed)),
            pltpu.SemaphoreType.DMA((1,)),
        ],
        cost_estimate=pl.CostEstimate(flops=10000000000, transcendentals=0, bytes_accessed=10000000),
        compiler_params=params(),
        name="pack_zone",
    )(state, below)


def zone_kernel(plan, place, offsets, speed, swirl, next_swirl, diffusion, coupling, weights, got, *refs):
    _, to_here, to_next, token, base, now, later, spread, matrix, made = refs
    token[...] = jnp.zeros(token.shape, jnp.float32)
    fields, deep, cycle, full, wide = plan.fields, plan.deep, plan.cycle, plan.full, plan.wide
    sections = offsets.shape[0]
    row, sector = place[0], place[1]
    terms = fields + 9
    rows = slice(LOW, LOW + wide)
    lane = lax.broadcasted_iota(jnp.int32, (wide, plan.packed), 1) // cycle
    own_lane = lax.broadcasted_iota(jnp.int32, (plan.mine, plan.packed), 1) // cycle
    at_radius = lax.broadcasted_iota(jnp.int32, (wide, full), 0) + sector * plan.mine - EXTRA
    inside = (at_radius >= 0) & (at_radius < plan.radial)
    block = plan.packed // cycle

    for side, w in enumerate((swirl, next_swirl)):
        for f, (axial, around, d, mix) in enumerate(coefficients(plan, speed, w, diffusion, coupling)):
            for number, factor in enumerate((d, *mix, *axial, *around)):
                spread[side * fields * terms + f * terms + number] = jnp.full((8, full), factor, jnp.float32)

    for buffer in (now, later):
        for side in range(2):
            def clear(field, carry, buffer=buffer, side=side):
                for first, after in ((0, LOW), (LOW + wide, buffer.shape[3])):
                    empty = jnp.zeros((buffer.shape[2], after - first, full), jnp.float32)
                    buffer[side, field, :, first:after, :] = empty
                return carry

            lax.fori_loop(0, fields, clear, 0)

    for side in range(2):
        def spread_out(field, carry, side=side):
            for plane in range(deep):
                parts = []
                for first in range(0, plan.sectors, block):
                    total = jnp.zeros((wide, plan.packed), jnp.float32)
                    for number in range(min(block, plan.sectors - first)):
                        turned = got[first + number, side * fields + field]
                        turn = (number - plane) * cycle % plan.packed
                        if turn:
                            turned = pltpu.roll(turned, turn, 1)
                        total = jnp.where(lane == number, turned, total)
                    parts.append(total)
                value = parts[0] if len(parts) == 1 else jnp.concatenate(parts, axis=1)
                base[side, field, 2 + plane, rows, :] = value
                now[side, field, 2 + plane, rows, :] = value
            return carry

        lax.fori_loop(0, fields, spread_out, 0)

    for section in range(sections):
        offset = offsets[section, jnp.minimum(row, offsets.shape[1] - 1)]
        for side in range(2):
            here = lax.rem(full - offset, full) if side == 0 else offset
            shift, cell = here // cycle, lax.rem(here, cycle)
            for target in range(plan.sectors):
                matrix[target * cycle : (target + 1) * cycle, :] = pltpu.roll(
                    weights[cell], lax.rem(target + shift, plan.sectors) * cycle, 1
                )
            other = 1 - side
            first = 2 if other == 1 else deep
            to = deep + 2 if side == 0 else 0
            pairs = [(field, plane) for field in range(fields) for plane in range(2)]
            values = [now[other, field, first + plane, rows, :] for field, plane in pairs]
            turn = matrix[...]
            together = wide % 8 == 0
            if together:
                values = [jnp.concatenate(values, axis=0)]
            results = [
                lax.dot_general(
                    value, turn, (((1,), (1,)), ((), ())), precision=highest, preferred_element_type=jnp.float32
                )
                for value in values
            ]
            for number, (field, plane) in enumerate(pairs):
                if together:
                    value = results[0][number * wide : (number + 1) * wide]
                else:
                    value = results[number]
                now[side, field, to + plane, rows, :] = value
                made[side, field, 2 * section + plane] = now[side, field, to + plane, LOW + EXTRA : LOW + EXTRA + plan.mine, :]
        if section == sections - 1:
            break
        size = deep - 2 * (section + 1)
        step_size = time_step if section == sections - 2 else 0.5 * time_step
        for side in range(2):
            begin = 2 + (deep - size if side == 0 else 0)

            def advance(number, carry, side=side, begin=begin, now=now, later=later, step_size=step_size):
                plane = begin + number
                for f in range(fields):
                    start = side * fields * terms + f * terms
                    factors = [spread[start + number] for number in range(terms)]
                    for first in range(0, wide, 8):
                        tall = min(8, wide - first)
                        factor = lambda k: factors[k] if tall == 8 else factors[k][:tall]
                        here = slice(LOW + first, LOW + first + tall)
                        center = now[side, f, plane, here, :]
                        total = factor(0) * (
                            now[side, f, plane, LOW + first - 1 : LOW + first - 1 + tall, :]
                            + now[side, f, plane, LOW + first + 1 : LOW + first + 1 + tall, :]
                        )
                        for e in range(fields):
                            total += factor(1 + e) * (center if e == f else now[side, e, plane, here, :])
                        for place_at, by in enumerate((-2, -1, 1, 2)):
                            total += factor(1 + fields + place_at) * now[side, f, plane + by, here, :]
                            total += factor(5 + fields + place_at) * pltpu.roll(center, -by % full, 1)
                        value = base[side, f, plane, here, :] + step_size * total
                        later[side, f, plane, here, :] = jnp.where(inside[first : first + tall], value, 0.0)
                return carry

            lax.fori_loop(0, size, advance, 0)
        now, later = later, now

    has_next = (row < offsets.shape[1]).astype(jnp.float32)
    for side, out in enumerate((to_here, to_next)):
        def hand_out(field, carry, side=side, out=out):
            for target in range(plan.sectors):
                total = jnp.zeros((plan.mine, plan.packed), jnp.float32)
                first = target // block * plan.packed
                for number in range(2 * sections):
                    turned = made[side, field, number, :, first : first + plan.packed]
                    turn = (number - target % block) * cycle % plan.packed
                    if turn:
                        turned = pltpu.roll(turned, turn, 1)
                    total = jnp.where(own_lane == number, turned, total)
                out[target, field] = total * has_next if side == 0 else total
            return carry

        lax.fori_loop(0, fields, hand_out, 0)


def zone(plan, place, offsets, scalars, next_swirl, weights, got, after):
    speed, swirl, diffusion, coupling = scalars
    buffer = held((2, plan.fields, plan.deep + 4, LOW + plan.wide + 8, plan.full))
    rows = -(-(LOW + plan.wide + 8) // 8) * 8
    need = (3 * 2 * plan.fields * (plan.deep + 4) + 2 * plan.fields * (plan.fields + 9)) * rows * plan.full * 4
    sent = jax.ShapeDtypeStruct((plan.sectors, plan.fields, plan.mine, plan.packed), jnp.float32)
    return pl.pallas_call(
        functools.partial(zone_kernel, plan),
        in_specs=[whole(SMEM)] * 7 + [whole(VMEM)] * 3,
        out_specs=[whole(VMEM)] * 3,
        out_shape=[sent, sent, held((8, plan.radial))],
        scratch_shapes=[
            buffer,
            buffer,
            buffer,
            held((2 * plan.fields * (plan.fields + 9), 8, plan.full)),
            held((plan.full, plan.full)),
            held((2, plan.fields, 2 * offsets.shape[0], plan.mine, plan.full)),
        ],
        cost_estimate=pl.CostEstimate(flops=10000000000, transcendentals=0, bytes_accessed=10000000),
        compiler_params=pltpu.CompilerParams(vmem_limit_bytes=need + 6 * 1024 * 1024),
        name="step_zone",
    )(place, offsets, speed, swirl, next_swirl, diffusion, coupling, weights, got, near(after[0]))


def unpack_kernel(plan, got, _, *refs):
    *outs, token, tall = refs
    token[...] = jnp.zeros(token.shape, jnp.float32)
    for side in range(2):
        for field in range(plan.fields):
            for sector in range(plan.sectors):
                tall[sector * plan.mine : (sector + 1) * plan.mine, :] = got[sector, side * plan.fields + field]
            flat = tall[...].T
            for section, out in enumerate(outs):
                for plane in range(2):
                    start = (2 * section + plane) * plan.cycle
                    out[side, field, plane] = flat[start : start + plan.cycle]


def unpack(plan, got, sections, after):
    return pl.pallas_call(
        functools.partial(unpack_kernel, plan),
        in_specs=[whole(VMEM)] * 2,
        out_specs=[whole(VMEM)] * (sections + 1),
        out_shape=[held(plan.ghost)] * sections + [held((8, plan.radial))],
        scratch_shapes=[held((plan.radial, plan.packed))],
        cost_estimate=pl.CostEstimate(flops=10000000000, transcendentals=0, bytes_accessed=10000000),
        compiler_params=params(),
        name="unpack_ghosts",
    )(got, near(after[0]))


def edge_shape(plan, kind):
    return held((plan.fields, plan.kept(kind) // 4, 8, plan.radial))


def first_kernel(plan, state, *refs):
    for at, (first, low_ref, high_ref) in enumerate(((0, *refs[:2]), (plan.middle, *refs[2:]))):

        def body(tile, carry, first=first, low_ref=low_ref, high_ref=high_ref):
            for field in range(plan.fields):
                for step in range(4):
                    plane = first + tile * 4 + step
                    rows = slice(2 * step, 2 * step + 2)
                    low_ref[field, tile, rows, :] = state[field, plane, 0:2, :]
                    high_ref[field, tile, rows, :] = state[field, plane, plan.cycle - 2 : plan.cycle, :]
            return carry

        lax.fori_loop(0, low_ref.shape[1], body, 0)


def first_edges(plan, state):
    low, high = edge_shape(plan, "low"), edge_shape(plan, "high")
    results = pl.pallas_call(
        functools.partial(first_kernel, plan),
        in_specs=[whole(VMEM)],
        out_specs=[whole(VMEM)] * 4,
        out_shape=[low, low, high, high],
        cost_estimate=pl.CostEstimate(flops=10000000000, transcendentals=0, bytes_accessed=10000000),
        compiler_params=params(),
        name="first_edges",
    )(near(state))
    return results[:2], results[2:]


def coefficients(plan, speed, swirl, diffusion, coupling):
    twelfth = 1.0 / 12.0
    w = swirl[0]
    table = []
    for f in range(plan.fields):
        v, d = speed[f], diffusion[f]
        axial = ((-v - d) * twelfth, (8.0 * v + 16.0 * d) * twelfth, (16.0 * d - 8.0 * v) * twelfth, (v - d) * twelfth)
        cycle = ((-w - d) * twelfth, (8.0 * w + 16.0 * d) * twelfth, (16.0 * d - 8.0 * w) * twelfth, (w - d) * twelfth)
        mix = [coupling[f, e] - 7.0 * d if e == f else coupling[f, e] for e in range(plan.fields)]
        table.append((axial, cycle, d, mix))
    return table


def stage_kernel(plan, stage, kind, names, speed, swirl, diffusion, coupling, *refs):
    ref = dict(zip(names, refs))
    ranges = plan.ranges(kind, stage)
    cycle, radial, last = plan.cycle, plan.radial, stage == 3
    state, work, spread = ref["state"], ref["work"], ref["spread"]
    terms = plan.fields + 9
    for f, (axial, around, d, mix) in enumerate(coefficients(plan, speed, swirl, diffusion, coupling)):
        for number, factor in enumerate((d, *mix, *axial, *around)):
            spread[f * terms + number] = jnp.full((8, radial), factor, jnp.float32)
    lane = lax.broadcasted_iota(jnp.int32, (8, radial), 1)
    not_first = lane > 0
    not_last = lane < radial - 1

    def cells(plane, level):
        if plane < 0:
            return ref["ghosts"][0, :, plane + 2]
        if plane >= plan.axial:
            return ref["ghosts"][1, :, plane - plan.axial]
        if level == 0:
            return state[:, plane]
        owner, at = plan.owner(plane, level)
        return ref["cells", level, owner][:, at]

    copies = []
    for number, (low, high) in enumerate(ranges):
        size = high - low
        for plane in range(low - 2, high + 2):
            work[:, plane - low + 2, LOW : LOW + cycle, :] = cells(plane, stage)
        for plane in range(low, high):
            owner, at = plan.owner(plane, stage)
            rows = slice(2 * (at % 4), 2 * (at % 4) + 2)
            work[:, plane - low + 2, LOW - 2 : LOW, :] = ref["low halo", owner][:, at // 4, rows, :]
            work[:, plane - low + 2, LOW + cycle : LOW + cycle + 2, :] = ref["high halo", owner][:, at // 4, rows, :]
            if last:
                ref["earlier"][:, plane - low] = cells(plane, 1) + 2.0 * cells(plane, 2)
        start = plan.place(kind, low)

        def compute(tile, steps, low=low, start=start, number=number):
            for f in range(plan.fields):
                factors = [spread[f * terms + number] for number in range(terms)]
                values = {}
                for step in steps:
                    at = tile * 4 + step - start % 4
                    for row in range(0, cycle, 8):
                        here = slice(LOW + row, LOW + row + 8)
                        center = work[f, at + 2, here, :]
                        left = jnp.where(not_first, pltpu.roll(center, 1, 1), 0.0)
                        right = jnp.where(not_last, pltpu.roll(center, radial - 1, 1), 0.0)
                        total = factors[0] * (left + right)
                        for e in range(plan.fields):
                            total += factors[1 + e] * (center if e == f else work[e, at + 2, here, :])
                        for place, by in enumerate((-2, -1, 1, 2)):
                            total += factors[1 + plan.fields + place] * work[f, at + 2 + by, here, :]
                            beside = slice(LOW + row + by, LOW + row + by + 8)
                            total += factors[5 + plan.fields + place] * work[f, at + 2, beside, :]
                        base = state[f, low + at, row : row + 8, :]
                        if last:
                            value = (ref["earlier"][f, at, row : row + 8, :] + center - base) * (1.0 / 3.0)
                            value += (time_step / 6.0) * total
                        else:
                            value = base + (time_step if stage == 2 else 0.5 * time_step) * total
                        values[step, row] = value
                for (step, row), value in values.items():
                    at = tile * 4 + step - start % 4
                    if last:
                        ref["made"][number, f, at, row : row + 8, :] = value
                        continue
                    ref["out"][f, start + at, row : row + 8, :] = value
                    rows = slice(2 * step, 2 * step + 2)
                    if row == 0:
                        ref["low edge"][f, start // 4 + tile, rows, :] = value[:2]
                    if row == cycle - 8:
                        ref["high edge"][f, start // 4 + tile, rows, :] = value[6:]

        head = start % 4
        tiles = (head + size) // 4
        if head:
            compute(0, range(head, min(4, head + size)))
        first = 1 if head else 0

        def whole_tile(tile, carry, compute=compute):
            compute(tile, range(4))
            return carry

        if tiles > first:
            lax.fori_loop(first, tiles, whole_tile, 0)
        tail = (head + size) % 4
        if tail and tiles >= first:
            compute(tiles, range(tail))
        if last:
            copies.append(
                pltpu.make_async_copy(
                    ref["made"].at[number, :, 0:size], ref["result"].at[:, low:high], ref["sem"].at[number]
                )
            )
            copies[-1].start()
    for item in copies:
        item.wait()
    ref["token"][...] = jnp.zeros(ref["token"].shape, jnp.float32)


def stage_call(plan, stage, kind, scalars, state, levels, halos, ghosts, after, result=None):
    ranges = plan.ranges(kind, stage)
    last = stage == 3
    longest = max(high - low for low, high in ranges)
    operands = {"state": near(state)}
    specs = [whole(VMEM)]

    def add(name, value):
        operands[name] = near(value)
        specs.append(whole(VMEM))

    kinds = {plan.owner(plane, stage)[0] for low, high in ranges for plane in range(low, high)}
    for owner in sorted(kinds):
        add(("low halo", owner), halos[owner][0])
        add(("high halo", owner), halos[owner][1])
    for level in (1, 2, stage) if last else (stage,) if stage else ():
        edge = 2 if level == stage else 0
        planes = [plane for low, high in ranges for plane in range(max(0, low - edge), min(plan.axial, high + edge))]
        for owner in sorted({plan.owner(plane, level)[0] for plane in planes}):
            add(("cells", level, owner), levels[level][owner])
    if kind == "ends":
        add("ghosts", ghosts)
    for number, token in enumerate(after):
        add(("after", number), token)
    aliases = {}
    if result is not None:
        aliases = {len(scalars) + len(operands): 0}
        operands["earlier result"] = result
        specs.append(whole(pl.ANY))
    token = held((8, plan.radial))
    if last:
        outs = {"result": jax.ShapeDtypeStruct(state.shape, jnp.float32), "token": token}
    else:
        edges = edge_shape(plan, kind)
        cells = held((plan.fields, plan.kept(kind), plan.cycle, plan.radial))
        outs = {"out": cells, "low edge": edges, "high edge": edges, "token": token}
    scratch = {
        "work": held((plan.fields, longest + 4, plan.cycle + 16, plan.radial)),
        "spread": held((plan.fields * (plan.fields + 9), 8, plan.radial)),
    }
    if last:
        scratch["earlier"] = held((plan.fields, longest, plan.cycle, plan.radial))
        scratch["made"] = held((len(ranges), plan.fields, longest, plan.cycle, plan.radial))
        scratch["sem"] = pltpu.SemaphoreType.DMA((len(ranges),))
    names = (*operands, *outs, *scratch)
    return pl.pallas_call(
        functools.partial(stage_kernel, plan, stage, kind, names),
        in_specs=[whole(SMEM)] * len(scalars) + specs,
        out_specs=[whole(pl.ANY if name == "result" else VMEM) for name in outs],
        out_shape=list(outs.values()),
        scratch_shapes=list(scratch.values()),
        input_output_aliases=aliases,
        cost_estimate=pl.CostEstimate(flops=10000000000, transcendentals=0, bytes_accessed=10000000),
        compiler_params=params(),
        name=f"stage{stage}_{kind}",
    )(*scalars, *operands.values())


def exchange(edges):
    size = lax.axis_size("sector")
    ahead = [(i, (i + 1) % size) for i in range(size)]
    back = [(i, (i - 1) % size) for i in range(size)]
    low_edges, high_edges = edges
    return lax.ppermute(high_edges, "sector", ahead), lax.ppermute(low_edges, "sector", back)


def on_device(state, interp_blocks, rotor_offset, axial_speed, row_swirl, diffusivity, coupling):
    plan = Plan(state, lax.axis_size("sector"))
    rows = lax.axis_size("row")
    sections = rotor_offset.shape[0]
    place = jnp.stack([lax.axis_index("row"), lax.axis_index("sector")]).astype(jnp.int32)
    scalars = (axial_speed, row_swirl, diffusivity, coupling)
    back = [(row + 1, row) for row in range(rows - 1)]
    ahead = [(row, row + 1) for row in range(rows - 1)]

    below = lax.ppermute(state[:, : plan.deep], "row", back)
    next_swirl = lax.ppermute(row_swirl, "row", back)
    weights = jnp.pad(interp_blocks, ((0, 0), (0, 0), (0, plan.full - interp_blocks.shape[2])))
    packed = pack(plan, state, below)
    levels, halos = [None], [{}]
    edges = dict(zip(("low", "high"), first_edges(plan, state)))
    packed, *edges["high"] = lax.optimization_barrier((packed, *edges["high"]))
    halos[0] = {kind: exchange(edges[kind]) for kind in ("low", "high")}
    packed, *halos[0]["low"] = lax.optimization_barrier((packed, *halos[0]["low"]))
    got = lax.all_to_all(packed, "sector", 0, 0, tiled=True)
    token, result, ghosts = (), None, None

    def step(stage, kind):
        nonlocal token, result
        ghost = ghosts[stage] if kind == "ends" else None
        outs = stage_call(plan, stage, kind, scalars, state, levels, halos[stage], ghost, token, result if stage == sections - 1 else None)
        token = outs[-1:]
        if stage == sections - 1:
            result = outs[0]
            return None
        if len(levels) == stage + 1:
            levels.append({})
            halos.append({})
        levels[stage + 1][kind] = outs[0]
        return outs[1:3]

    def send(stage, kind, edges):
        halos[stage + 1][kind] = exchange(edges)

    def go(stage, kind):
        edges = step(stage, kind)
        if edges is not None:
            send(stage, kind, edges)

    go(0, "low")
    go(0, "high")
    downstream, to_next, *token = zone(plan, place, rotor_offset, scalars, next_swirl, weights, got, token)
    upstream = lax.ppermute(to_next, "row", ahead)
    low_edges = step(1, "low")
    joined = jnp.concatenate([upstream, downstream], axis=1)
    joined, *rest = lax.optimization_barrier((joined, *token, *low_edges))
    token, low_edges = rest[:1], rest[1:]
    returned = lax.all_to_all(joined, "sector", 0, 0, tiled=True)
    send(1, "low", low_edges)
    go(1, "high")
    *ghosts, last_token = unpack(plan, returned, sections, token)
    token = (last_token,)
    go(0, "ends")
    go(2, "low")
    go(2, "high")
    go(1, "ends")
    go(3, "low")
    go(2, "ends")
    go(3, "high")
    go(3, "ends")
    return result


def solution(mesh):
    return jax.shard_map(
        on_device,
        mesh=mesh,
        in_specs=(P(None, "row", "sector", None), P(), P(), P(), P("row"), P(), P()),
        out_specs=P(None, "row", "sector", None),
        check_vma=False,
    )
```

```python
import functools

import jax
import jax.numpy as jnp
from jax import lax
from jax.experimental import pallas as pl
from jax.experimental.pallas import tpu as pltpu
from jax.sharding import PartitionSpec as P

time_step = 0.4
highest = lax.Precision.HIGHEST
VMEM = pltpu.VMEM
SMEM = pltpu.SMEM
EXTRA = 4
LOW = 8


def whole(space):
    return pl.BlockSpec(memory_space=space)


def held(shape):
    return pltpu.VMEM(tuple(shape), jnp.float32)


def near(value):
    return pltpu.with_memory_space_constraint(value, pltpu.VMEM)


def params():
    return pltpu.CompilerParams(vmem_limit_bytes=16 * 1024 * 1024)


class Plan:
    def __init__(self, state, sectors):
        self.fields, self.axial, self.cycle, self.radial = state.shape
        self.sectors = sectors
        self.base = 4
        self.ends = self.base + 8
        self.ghost = (2, self.fields, 2, self.cycle, self.radial)
        self.deep = 8
        self.full = self.cycle * sectors
        self.mine = self.radial // sectors
        self.wide = self.mine + 2 * EXTRA
        self.packed = self.deep * self.cycle


    def ranges(self, kind, stage):
        reach = self.base + 2 * (stage + 1)
        if kind == "mid":
            return ((reach, self.axial - reach),)
        return ((0, reach), (self.axial - reach, self.axial))

    def kept(self, kind):
        return self.axial - 2 * self.base if kind == "mid" else 2 * self.ends

    def owner(self, plane, stage):
        reach = self.base + 2 * stage
        kind = "mid" if reach <= plane < self.axial - reach else "ends"
        return kind, self.place(kind, plane)

    def place(self, kind, plane):
        if kind == "mid":
            return plane - self.base
        return plane if plane < self.axial // 2 else plane - self.axial + 2 * self.ends


def pack_kernel(plan, state, below, out, planes, tall, sem):
    copy = pltpu.make_async_copy(state.at[:, plan.axial - plan.deep : plan.axial], planes, sem.at[0])
    copy.start()
    tall[...] = jnp.zeros(tall.shape, jnp.float32)
    copy.wait()
    for side, source in enumerate((planes, below)):
        for field in range(plan.fields):
            flat = source[field].reshape(plan.packed, plan.radial)
            tall[EXTRA : EXTRA + plan.radial, :] = flat.T
            for sector in range(plan.sectors):
                out[sector, side * plan.fields + field] = tall[sector * plan.mine : sector * plan.mine + plan.wide, :]


def pack(plan, state, below):
    return pl.pallas_call(
        functools.partial(pack_kernel, plan),
        in_specs=[whole(pl.ANY), whole(VMEM)],
        out_specs=whole(VMEM),
        out_shape=jax.ShapeDtypeStruct((plan.sectors, 2 * plan.fields, plan.wide, plan.packed), jnp.float32),
        scratch_shapes=[
            held((plan.fields, plan.deep, plan.cycle, plan.radial)),
            held((plan.radial + 2 * EXTRA, plan.packed)),
            pltpu.SemaphoreType.DMA((1,)),
        ],
        cost_estimate=pl.CostEstimate(flops=10000000000, transcendentals=0, bytes_accessed=10000000),
        compiler_params=params(),
        name="pack_zone",
    )(state, below)


def zone_kernel(plan, place, offsets, speed, swirl, next_swirl, diffusion, coupling, weights, got, *refs):
    _, to_here, to_next, token, base, now, later, spread, matrix, made = refs
    token[...] = jnp.zeros(token.shape, jnp.float32)
    fields, deep, cycle, full, wide = plan.fields, plan.deep, plan.cycle, plan.full, plan.wide
    sections = offsets.shape[0]
    row, sector = place[0], place[1]
    terms = fields + 9
    rows = slice(LOW, LOW + wide)
    lane = lax.broadcasted_iota(jnp.int32, (wide, plan.packed), 1) // cycle
    own_lane = lax.broadcasted_iota(jnp.int32, (plan.mine, plan.packed), 1) // cycle
    at_radius = lax.broadcasted_iota(jnp.int32, (wide, full), 0) + sector * plan.mine - EXTRA
    inside = (at_radius >= 0) & (at_radius < plan.radial)
    block = plan.packed // cycle

    for side, w in enumerate((swirl, next_swirl)):
        for f, (axial, around, d, mix) in enumerate(coefficients(plan, speed, w, diffusion, coupling)):
            for number, factor in enumerate((d, *mix, *axial, *around)):
                spread[side * fields * terms + f * terms + number] = jnp.full((8, full), factor, jnp.float32)

    for buffer in (now, later):
        for side in range(2):
            def clear(field, carry, buffer=buffer, side=side):
                for first, after in ((0, LOW), (LOW + wide, buffer.shape[3])):
                    empty = jnp.zeros((buffer.shape[2], after - first, full), jnp.float32)
                    buffer[side, field, :, first:after, :] = empty
                return carry

            lax.fori_loop(0, fields, clear, 0)

    for side in range(2):
        def spread_out(field, carry, side=side):
            for plane in range(deep):
                parts = []
                for first in range(0, plan.sectors, block):
                    total = jnp.zeros((wide, plan.packed), jnp.float32)
                    for number in range(min(block, plan.sectors - first)):
                        turned = got[first + number, side * fields + field]
                        turn = (number - plane) * cycle % plan.packed
                        if turn:
                            turned = pltpu.roll(turned, turn, 1)
                        total = jnp.where(lane == number, turned, total)
                    parts.append(total)
                value = parts[0] if len(parts) == 1 else jnp.concatenate(parts, axis=1)
                base[side, field, 2 + plane, rows, :] = value
                now[side, field, 2 + plane, rows, :] = value
            return carry

        lax.fori_loop(0, fields, spread_out, 0)

    for section in range(sections):
        offset = offsets[section, jnp.minimum(row, offsets.shape[1] - 1)]
        for side in range(2):
            here = lax.rem(full - offset, full) if side == 0 else offset
            shift, cell = here // cycle, lax.rem(here, cycle)
            for target in range(plan.sectors):
                matrix[target * cycle : (target + 1) * cycle, :] = pltpu.roll(
                    weights[cell], lax.rem(target + shift, plan.sectors) * cycle, 1
                )
            other = 1 - side
            first = 2 if other == 1 else deep
            to = deep + 2 if side == 0 else 0
            pairs = [(field, plane) for field in range(fields) for plane in range(2)]
            values = [now[other, field, first + plane, rows, :] for field, plane in pairs]
            turn = matrix[...]
            together = wide % 8 == 0
            if together:
                values = [jnp.concatenate(values, axis=0)]
            results = [
                lax.dot_general(
                    value, turn, (((1,), (1,)), ((), ())), precision=highest, preferred_element_type=jnp.float32
                )
                for value in values
            ]
            for number, (field, plane) in enumerate(pairs):
                if together:
                    value = results[0][number * wide : (number + 1) * wide]
                else:
                    value = results[number]
                now[side, field, to + plane, rows, :] = value
                made[side, field, 2 * section + plane] = now[side, field, to + plane, LOW + EXTRA : LOW + EXTRA + plan.mine, :]
        if section == sections - 1:
            break
        size = deep - 2 * (section + 1)
        step_size = time_step if section == sections - 2 else 0.5 * time_step
        for side in range(2):
            begin = 2 + (deep - size if side == 0 else 0)

            def advance(number, carry, side=side, begin=begin, now=now, later=later, step_size=step_size):
                plane = begin + number
                for f in range(fields):
                    start = side * fields * terms + f * terms
                    factors = [spread[start + number] for number in range(terms)]
                    for first in range(0, wide, 8):
                        tall = min(8, wide - first)
                        factor = lambda k: factors[k] if tall == 8 else factors[k][:tall]
                        here = slice(LOW + first, LOW + first + tall)
                        center = now[side, f, plane, here, :]
                        total = factor(0) * (
                            now[side, f, plane, LOW + first - 1 : LOW + first - 1 + tall, :]
                            + now[side, f, plane, LOW + first + 1 : LOW + first + 1 + tall, :]
                        )
                        for e in range(fields):
                            total += factor(1 + e) * (center if e == f else now[side, e, plane, here, :])
                        for place_at, by in enumerate((-2, -1, 1, 2)):
                            total += factor(1 + fields + place_at) * now[side, f, plane + by, here, :]
                            total += factor(5 + fields + place_at) * pltpu.roll(center, -by % full, 1)
                        value = base[side, f, plane, here, :] + step_size * total
                        later[side, f, plane, here, :] = jnp.where(inside[first : first + tall], value, 0.0)
                return carry

            lax.fori_loop(0, size, advance, 0)
        now, later = later, now

    has_next = (row < offsets.shape[1]).astype(jnp.float32)
    for side, out in enumerate((to_here, to_next)):
        def hand_out(field, carry, side=side, out=out):
            for target in range(plan.sectors):
                total = jnp.zeros((plan.mine, plan.packed), jnp.float32)
                first = target // block * plan.packed
                for number in range(2 * sections):
                    turned = made[side, field, number, :, first : first + plan.packed]
                    turn = (number - target % block) * cycle % plan.packed
                    if turn:
                        turned = pltpu.roll(turned, turn, 1)
                    total = jnp.where(own_lane == number, turned, total)
                out[target, field] = total * has_next if side == 0 else total
            return carry

        lax.fori_loop(0, fields, hand_out, 0)


def zone(plan, place, offsets, scalars, next_swirl, weights, got, after):
    speed, swirl, diffusion, coupling = scalars
    buffer = held((2, plan.fields, plan.deep + 4, LOW + plan.wide + 8, plan.full))
    rows = -(-(LOW + plan.wide + 8) // 8) * 8
    need = (3 * 2 * plan.fields * (plan.deep + 4) + 2 * plan.fields * (plan.fields + 9)) * rows * plan.full * 4
    sent = jax.ShapeDtypeStruct((plan.sectors, plan.fields, plan.mine, plan.packed), jnp.float32)
    return pl.pallas_call(
        functools.partial(zone_kernel, plan),
        in_specs=[whole(SMEM)] * 7 + [whole(VMEM)] * 3,
        out_specs=[whole(VMEM)] * 3,
        out_shape=[sent, sent, held((8, plan.radial))],
        scratch_shapes=[
            buffer,
            buffer,
            buffer,
            held((2 * plan.fields * (plan.fields + 9), 8, plan.full)),
            held((plan.full, plan.full)),
            held((2, plan.fields, 2 * offsets.shape[0], plan.mine, plan.full)),
        ],
        cost_estimate=pl.CostEstimate(flops=10000000000, transcendentals=0, bytes_accessed=10000000),
        compiler_params=pltpu.CompilerParams(vmem_limit_bytes=need + 6 * 1024 * 1024),
        name="step_zone",
    )(place, offsets, speed, swirl, next_swirl, diffusion, coupling, weights, got, near(after[0]))


def unpack_kernel(plan, got, _, *refs):
    *outs, token, tall = refs
    token[...] = jnp.zeros(token.shape, jnp.float32)
    for side in range(2):
        for field in range(plan.fields):
            for sector in range(plan.sectors):
                tall[sector * plan.mine : (sector + 1) * plan.mine, :] = got[sector, side * plan.fields + field]
            flat = tall[...].T
            for section, out in enumerate(outs):
                for plane in range(2):
                    start = (2 * section + plane) * plan.cycle
                    out[side, field, plane] = flat[start : start + plan.cycle]


def unpack(plan, got, sections, after):
    return pl.pallas_call(
        functools.partial(unpack_kernel, plan),
        in_specs=[whole(VMEM)] * 2,
        out_specs=[whole(VMEM)] * (sections + 1),
        out_shape=[held(plan.ghost)] * sections + [held((8, plan.radial))],
        scratch_shapes=[held((plan.radial, plan.packed))],
        cost_estimate=pl.CostEstimate(flops=10000000000, transcendentals=0, bytes_accessed=10000000),
        compiler_params=params(),
        name="unpack_ghosts",
    )(got, near(after[0]))


def edge_shape(plan, kind):
    return held((plan.fields, plan.kept(kind) // 4, 8, plan.radial))


def first_kernel(plan, ranges, kind, state, low_ref, high_ref):
    for first, after in ranges:
        start = plan.place(kind, first) // 4

        def body(tile, carry, first=first, start=start):
            for field in range(plan.fields):
                for step in range(4):
                    plane = first + tile * 4 + step
                    rows = slice(2 * step, 2 * step + 2)
                    low_ref[field, start + tile, rows, :] = state[field, plane, 0:2, :]
                    high_ref[field, start + tile, rows, :] = state[field, plane, plan.cycle - 2 : plan.cycle, :]
            return carry

        lax.fori_loop(0, (after - first) // 4, body, 0)


def first_edges(plan, kind, state):
    base = plan.base
    ranges = ((base, plan.axial - base),) if kind == "mid" else ((0, base), (plan.axial - base, plan.axial))
    return pl.pallas_call(
        functools.partial(first_kernel, plan, ranges, kind),
        in_specs=[whole(VMEM)],
        out_specs=[whole(VMEM)] * 2,
        out_shape=[edge_shape(plan, kind)] * 2,
        cost_estimate=pl.CostEstimate(flops=10000000000, transcendentals=0, bytes_accessed=10000000),
        compiler_params=params(),
        name=f"first_edges_{kind}",
    )(near(state))


def coefficients(plan, speed, swirl, diffusion, coupling):
    twelfth = 1.0 / 12.0
    w = swirl[0]
    table = []
    for f in range(plan.fields):
        v, d = speed[f], diffusion[f]
        axial = ((-v - d) * twelfth, (8.0 * v + 16.0 * d) * twelfth, (16.0 * d - 8.0 * v) * twelfth, (v - d) * twelfth)
        cycle = ((-w - d) * twelfth, (8.0 * w + 16.0 * d) * twelfth, (16.0 * d - 8.0 * w) * twelfth, (w - d) * twelfth)
        mix = [coupling[f, e] - 7.0 * d if e == f else coupling[f, e] for e in range(plan.fields)]
        table.append((axial, cycle, d, mix))
    return table


def stage_kernel(plan, stage, kind, names, speed, swirl, diffusion, coupling, *refs):
    ref = dict(zip(names, refs))
    ranges = plan.ranges(kind, stage)
    cycle, radial, last = plan.cycle, plan.radial, stage == 3
    state, work, spread = ref["state"], ref["work"], ref["spread"]
    terms = plan.fields + 9
    for f, (axial, around, d, mix) in enumerate(coefficients(plan, speed, swirl, diffusion, coupling)):
        for number, factor in enumerate((d, *mix, *axial, *around)):
            spread[f * terms + number] = jnp.full((8, radial), factor, jnp.float32)
    lane = lax.broadcasted_iota(jnp.int32, (8, radial), 1)
    not_first = lane > 0
    not_last = lane < radial - 1

    def cells(plane, level):
        if plane < 0:
            return ref["ghosts"][0, :, plane + 2]
        if plane >= plan.axial:
            return ref["ghosts"][1, :, plane - plan.axial]
        if level == 0:
            return state[:, plane]
        owner, at = plan.owner(plane, level)
        return ref["cells", level, owner][:, at]

    copies = []
    for number, (low, high) in enumerate(ranges):
        size = high - low
        for plane in range(low - 2, high + 2):
            work[:, plane - low + 2, LOW : LOW + cycle, :] = cells(plane, stage)
        for plane in range(low, high):
            owner, at = plan.owner(plane, stage)
            rows = slice(2 * (at % 4), 2 * (at % 4) + 2)
            work[:, plane - low + 2, LOW - 2 : LOW, :] = ref["low halo", owner][:, at // 4, rows, :]
            work[:, plane - low + 2, LOW + cycle : LOW + cycle + 2, :] = ref["high halo", owner][:, at // 4, rows, :]
            if last:
                ref["earlier"][:, plane - low] = cells(plane, 1) + 2.0 * cells(plane, 2)
        start = plan.place(kind, low)

        def compute(tile, steps, low=low, start=start, number=number):
            for f in range(plan.fields):
                factors = [spread[f * terms + number] for number in range(terms)]
                values = {}
                for step in steps:
                    at = tile * 4 + step - start % 4
                    for row in range(0, cycle, 8):
                        here = slice(LOW + row, LOW + row + 8)
                        center = work[f, at + 2, here, :]
                        left = jnp.where(not_first, pltpu.roll(center, 1, 1), 0.0)
                        right = jnp.where(not_last, pltpu.roll(center, radial - 1, 1), 0.0)
                        total = factors[0] * (left + right)
                        for e in range(plan.fields):
                            total += factors[1 + e] * (center if e == f else work[e, at + 2, here, :])
                        for place, by in enumerate((-2, -1, 1, 2)):
                            total += factors[1 + plan.fields + place] * work[f, at + 2 + by, here, :]
                            beside = slice(LOW + row + by, LOW + row + by + 8)
                            total += factors[5 + plan.fields + place] * work[f, at + 2, beside, :]
                        base = state[f, low + at, row : row + 8, :]
                        if last:
                            value = (ref["earlier"][f, at, row : row + 8, :] + center - base) * (1.0 / 3.0)
                            value += (time_step / 6.0) * total
                        else:
                            value = base + (time_step if stage == 2 else 0.5 * time_step) * total
                        values[step, row] = value
                for (step, row), value in values.items():
                    at = tile * 4 + step - start % 4
                    if last:
                        ref["made"][number, f, at, row : row + 8, :] = value
                        continue
                    ref["out"][f, start + at, row : row + 8, :] = value
                    rows = slice(2 * step, 2 * step + 2)
                    if row == 0:
                        ref["low edge"][f, start // 4 + tile, rows, :] = value[:2]
                    if row == cycle - 8:
                        ref["high edge"][f, start // 4 + tile, rows, :] = value[6:]

        head = start % 4
        tiles = (head + size) // 4
        if head:
            compute(0, range(head, min(4, head + size)))
        first = 1 if head else 0

        def whole_tile(tile, carry, compute=compute):
            compute(tile, range(4))
            return carry

        if tiles > first:
            lax.fori_loop(first, tiles, whole_tile, 0)
        tail = (head + size) % 4
        if tail and tiles >= first:
            compute(tiles, range(tail))
        if last:
            copies.append(
                pltpu.make_async_copy(
                    ref["made"].at[number, :, 0:size], ref["result"].at[:, low:high], ref["sem"].at[number]
                )
            )
            copies[-1].start()
    for item in copies:
        item.wait()
    ref["token"][...] = jnp.zeros(ref["token"].shape, jnp.float32)


def stage_call(plan, stage, kind, scalars, state, levels, halos, ghosts, after, result=None):
    ranges = plan.ranges(kind, stage)
    last = stage == 3
    longest = max(high - low for low, high in ranges)
    operands = {"state": near(state)}
    specs = [whole(VMEM)]

    def add(name, value):
        operands[name] = near(value)
        specs.append(whole(VMEM))

    kinds = {plan.owner(plane, stage)[0] for low, high in ranges for plane in range(low, high)}
    for owner in sorted(kinds):
        add(("low halo", owner), halos[owner][0])
        add(("high halo", owner), halos[owner][1])
    for level in (1, 2, stage) if last else (stage,) if stage else ():
        edge = 2 if level == stage else 0
        planes = [plane for low, high in ranges for plane in range(max(0, low - edge), min(plan.axial, high + edge))]
        for owner in sorted({plan.owner(plane, level)[0] for plane in planes}):
            add(("cells", level, owner), levels[level][owner])
    if kind == "ends":
        add("ghosts", ghosts)
    for number, token in enumerate(after):
        add(("after", number), token)
    aliases = {}
    if result is not None:
        aliases = {len(scalars) + len(operands): 0}
        operands["earlier result"] = result
        specs.append(whole(pl.ANY))
    token = held((8, plan.radial))
    if last:
        outs = {"result": jax.ShapeDtypeStruct(state.shape, jnp.float32), "token": token}
    else:
        edges = edge_shape(plan, kind)
        cells = held((plan.fields, plan.kept(kind), plan.cycle, plan.radial))
        outs = {"out": cells, "low edge": edges, "high edge": edges, "token": token}
    scratch = {
        "work": held((plan.fields, longest + 4, plan.cycle + 16, plan.radial)),
        "spread": held((plan.fields * (plan.fields + 9), 8, plan.radial)),
    }
    if last:
        scratch["earlier"] = held((plan.fields, longest, plan.cycle, plan.radial))
        scratch["made"] = held((len(ranges), plan.fields, longest, plan.cycle, plan.radial))
        scratch["sem"] = pltpu.SemaphoreType.DMA((len(ranges),))
    names = (*operands, *outs, *scratch)
    return pl.pallas_call(
        functools.partial(stage_kernel, plan, stage, kind, names),
        in_specs=[whole(SMEM)] * len(scalars) + specs,
        out_specs=[whole(pl.ANY if name == "result" else VMEM) for name in outs],
        out_shape=list(outs.values()),
        scratch_shapes=list(scratch.values()),
        input_output_aliases=aliases,
        cost_estimate=pl.CostEstimate(flops=10000000000, transcendentals=0, bytes_accessed=10000000),
        compiler_params=params(),
        name=f"stage{stage}_{kind}",
    )(*scalars, *operands.values())


def exchange(edges):
    size = lax.axis_size("sector")
    ahead = [(i, (i + 1) % size) for i in range(size)]
    back = [(i, (i - 1) % size) for i in range(size)]
    low_edges, high_edges = edges
    return lax.ppermute(high_edges, "sector", ahead), lax.ppermute(low_edges, "sector", back)


def on_device(state, interp_blocks, rotor_offset, axial_speed, row_swirl, diffusivity, coupling):
    plan = Plan(state, lax.axis_size("sector"))
    rows = lax.axis_size("row")
    sections = rotor_offset.shape[0]
    place = jnp.stack([lax.axis_index("row"), lax.axis_index("sector")]).astype(jnp.int32)
    scalars = (axial_speed, row_swirl, diffusivity, coupling)
    back = [(row + 1, row) for row in range(rows - 1)]
    ahead = [(row, row + 1) for row in range(rows - 1)]

    below = lax.ppermute(state[:, : plan.deep], "row", back)
    next_swirl = lax.ppermute(row_swirl, "row", back)
    weights = jnp.pad(interp_blocks, ((0, 0), (0, 0), (0, plan.full - interp_blocks.shape[2])))
    packed = pack(plan, state, below)
    levels, halos = [None], [{}]
    halos[0]["mid"] = exchange(first_edges(plan, "mid", state))
    packed, *halos[0]["mid"] = lax.optimization_barrier((packed, *halos[0]["mid"]))
    got = lax.all_to_all(packed, "sector", 0, 0, tiled=True)
    token, result, ghosts = (), None, None

    def step(stage, kind):
        nonlocal token, result
        ghost = ghosts[stage] if kind == "ends" else None
        outs = stage_call(plan, stage, kind, scalars, state, levels, halos[stage], ghost, token, result if stage == sections - 1 else None)
        token = outs[-1:]
        if stage == sections - 1:
            result = outs[0]
            return None
        if len(levels) == stage + 1:
            levels.append({})
            halos.append({})
        levels[stage + 1][kind] = outs[0]
        return outs[1:3]

    def send(stage, kind, edges):
        halos[stage + 1][kind] = exchange(edges)

    def go(stage, kind):
        edges = step(stage, kind)
        if edges is not None:
            send(stage, kind, edges)

    go(0, "mid")
    end_edges, first_token = lax.optimization_barrier((first_edges(plan, "ends", state), token[0]))
    halos[0]["ends"] = exchange(end_edges)
    token = (first_token,)
    downstream, to_next, *token = zone(plan, place, rotor_offset, scalars, next_swirl, weights, got, token)
    upstream = lax.ppermute(to_next, "row", ahead)
    mid_edges = step(1, "mid")
    joined = jnp.concatenate([upstream, downstream], axis=1)
    joined, *rest = lax.optimization_barrier((joined, *token, *mid_edges))
    token, mid_edges = rest[:1], rest[1:]
    returned = lax.all_to_all(joined, "sector", 0, 0, tiled=True)
    send(1, "mid", mid_edges)
    *ghosts, last_token = unpack(plan, returned, sections, token)
    token = (last_token,)
    go(0, "ends")
    go(2, "mid")
    go(1, "ends")
    go(2, "ends")
    go(3, "mid")
    go(3, "ends")
    return result


def solution(mesh):
    return jax.shard_map(
        on_device,
        mesh=mesh,
        in_specs=(P(None, "row", "sector", None), P(), P(), P(), P("row"), P(), P()),
        out_specs=P(None, "row", "sector", None),
        check_vma=False,
    )
```

```python
import functools

import jax
import jax.numpy as jnp
from jax import lax
from jax.experimental import pallas as pl
from jax.experimental.pallas import tpu as pltpu
from jax.sharding import PartitionSpec as P

time_step = 0.4
highest = lax.Precision.HIGHEST
VMEM = pltpu.VMEM
SMEM = pltpu.SMEM
EXTRA = 4
LOW = 8


def whole(space):
    return pl.BlockSpec(memory_space=space)


def held(shape):
    return pltpu.VMEM(tuple(shape), jnp.float32)


def near(value):
    return pltpu.with_memory_space_constraint(value, pltpu.VMEM)


def params():
    return pltpu.CompilerParams(vmem_limit_bytes=16 * 1024 * 1024)


class Plan:
    def __init__(self, state, sectors):
        self.fields, self.axial, self.cycle, self.radial = state.shape
        self.sectors = sectors
        self.base = self.axial // 4
        self.ghost = (2, self.fields, 2, self.cycle, self.radial)
        self.deep = 8
        self.full = self.cycle * sectors
        self.mine = self.radial // sectors
        self.wide = self.mine + 2 * EXTRA
        self.packed = self.deep * self.cycle


    def ranges(self, kind):
        if kind == "mid":
            return ((self.base, self.axial - self.base),)
        return ((0, self.base), (self.axial - self.base, self.axial))

    def kept(self, kind):
        return self.axial - 2 * self.base if kind == "mid" else 2 * self.base

    def owner(self, plane):
        kind = "mid" if self.base <= plane < self.axial - self.base else "ends"
        return kind, self.place(kind, plane)

    def place(self, kind, plane):
        if kind == "mid":
            return plane - self.base
        return plane if plane < self.axial // 2 else plane - self.axial + 2 * self.base


def pack_kernel(plan, state, below, out, planes, tall, sem):
    copy = pltpu.make_async_copy(state.at[:, plan.axial - plan.deep : plan.axial], planes, sem.at[0])
    copy.start()
    tall[...] = jnp.zeros(tall.shape, jnp.float32)
    copy.wait()
    for side, source in enumerate((planes, below)):
        for field in range(plan.fields):
            flat = source[field].reshape(plan.packed, plan.radial)
            tall[EXTRA : EXTRA + plan.radial, :] = flat.T
            for sector in range(plan.sectors):
                out[sector, side * plan.fields + field] = tall[sector * plan.mine : sector * plan.mine + plan.wide, :]


def pack(plan, state, below):
    return pl.pallas_call(
        functools.partial(pack_kernel, plan),
        in_specs=[whole(pl.ANY), whole(VMEM)],
        out_specs=whole(VMEM),
        out_shape=jax.ShapeDtypeStruct((plan.sectors, 2 * plan.fields, plan.wide, plan.packed), jnp.float32),
        scratch_shapes=[
            held((plan.fields, plan.deep, plan.cycle, plan.radial)),
            held((plan.radial + 2 * EXTRA, plan.packed)),
            pltpu.SemaphoreType.DMA((1,)),
        ],
        cost_estimate=pl.CostEstimate(flops=10000000000, transcendentals=0, bytes_accessed=10000000),
        compiler_params=params(),
        name="pack_zone",
    )(state, below)


def zone_kernel(plan, place, offsets, speed, swirl, next_swirl, diffusion, coupling, weights, got, *refs):
    to_here, to_next, token, base, now, later, spread, matrix, made = refs
    token[...] = jnp.zeros(token.shape, jnp.float32)
    fields, deep, cycle, full, wide = plan.fields, plan.deep, plan.cycle, plan.full, plan.wide
    sections = offsets.shape[0]
    row, sector = place[0], place[1]
    terms = fields + 9
    rows = slice(LOW, LOW + wide)
    lane = lax.broadcasted_iota(jnp.int32, (wide, plan.packed), 1) // cycle
    own_lane = lax.broadcasted_iota(jnp.int32, (plan.mine, plan.packed), 1) // cycle
    at_radius = lax.broadcasted_iota(jnp.int32, (wide, full), 0) + sector * plan.mine - EXTRA
    inside = (at_radius >= 0) & (at_radius < plan.radial)
    block = plan.packed // cycle

    for side, w in enumerate((swirl, next_swirl)):
        for f, (axial, around, d, mix) in enumerate(coefficients(plan, speed, w, diffusion, coupling)):
            for number, factor in enumerate((d, *mix, *axial, *around)):
                spread[side * fields * terms + f * terms + number] = jnp.full((8, full), factor, jnp.float32)

    for buffer in (now, later):
        for side in range(2):
            def clear(field, carry, buffer=buffer, side=side):
                for first, after in ((0, LOW), (LOW + wide, buffer.shape[3])):
                    empty = jnp.zeros((buffer.shape[2], after - first, full), jnp.float32)
                    buffer[side, field, :, first:after, :] = empty
                return carry

            lax.fori_loop(0, fields, clear, 0)

    for side in range(2):
        def spread_out(field, carry, side=side):
            for plane in range(deep):
                parts = []
                for first in range(0, plan.sectors, block):
                    total = jnp.zeros((wide, plan.packed), jnp.float32)
                    for number in range(min(block, plan.sectors - first)):
                        turned = got[first + number, side * fields + field]
                        turn = (number - plane) * cycle % plan.packed
                        if turn:
                            turned = pltpu.roll(turned, turn, 1)
                        total = jnp.where(lane == number, turned, total)
                    parts.append(total)
                value = parts[0] if len(parts) == 1 else jnp.concatenate(parts, axis=1)
                base[side, field, 2 + plane, rows, :] = value
                now[side, field, 2 + plane, rows, :] = value
            return carry

        lax.fori_loop(0, fields, spread_out, 0)

    for section in range(sections):
        offset = offsets[section, jnp.minimum(row, offsets.shape[1] - 1)]
        for side in range(2):
            here = lax.rem(full - offset, full) if side == 0 else offset
            shift, cell = here // cycle, lax.rem(here, cycle)
            for target in range(plan.sectors):
                matrix[target * cycle : (target + 1) * cycle, :] = pltpu.roll(
                    weights[cell], lax.rem(target + shift, plan.sectors) * cycle, 1
                )
            other = 1 - side
            first = 2 if other == 1 else deep
            to = deep + 2 if side == 0 else 0
            pairs = [(field, plane) for field in range(fields) for plane in range(2)]
            values = [now[other, field, first + plane, rows, :] for field, plane in pairs]
            turn = matrix[...]
            together = wide % 8 == 0
            if together:
                values = [jnp.concatenate(values, axis=0)]
            results = [
                lax.dot_general(
                    value, turn, (((1,), (1,)), ((), ())), precision=highest, preferred_element_type=jnp.float32
                )
                for value in values
            ]
            for number, (field, plane) in enumerate(pairs):
                if together:
                    value = results[0][number * wide : (number + 1) * wide]
                else:
                    value = results[number]
                now[side, field, to + plane, rows, :] = value
                made[side, field, 2 * section + plane] = now[side, field, to + plane, LOW + EXTRA : LOW + EXTRA + plan.mine, :]
        if section == sections - 1:
            break
        size = deep - 2 * (section + 1)
        step_size = time_step if section == sections - 2 else 0.5 * time_step
        for side in range(2):
            begin = 2 + (deep - size if side == 0 else 0)

            def advance(number, carry, side=side, begin=begin, now=now, later=later, step_size=step_size):
                plane = begin + number
                for f in range(fields):
                    start = side * fields * terms + f * terms
                    factors = [spread[start + number] for number in range(terms)]
                    for first in range(0, wide, 8):
                        tall = min(8, wide - first)
                        factor = lambda k: factors[k] if tall == 8 else factors[k][:tall]
                        here = slice(LOW + first, LOW + first + tall)
                        center = now[side, f, plane, here, :]
                        total = factor(0) * (
                            now[side, f, plane, LOW + first - 1 : LOW + first - 1 + tall, :]
                            + now[side, f, plane, LOW + first + 1 : LOW + first + 1 + tall, :]
                        )
                        for e in range(fields):
                            total += factor(1 + e) * (center if e == f else now[side, e, plane, here, :])
                        for place_at, by in enumerate((-2, -1, 1, 2)):
                            total += factor(1 + fields + place_at) * now[side, f, plane + by, here, :]
                            total += factor(5 + fields + place_at) * pltpu.roll(center, -by % full, 1)
                        value = base[side, f, plane, here, :] + step_size * total
                        later[side, f, plane, here, :] = jnp.where(inside[first : first + tall], value, 0.0)
                return carry

            lax.fori_loop(0, size, advance, 0)
        now, later = later, now

    has_next = (row < offsets.shape[1]).astype(jnp.float32)
    for side, out in enumerate((to_here, to_next)):
        def hand_out(field, carry, side=side, out=out):
            for target in range(plan.sectors):
                total = jnp.zeros((plan.mine, plan.packed), jnp.float32)
                first = target // block * plan.packed
                for number in range(2 * sections):
                    turned = made[side, field, number, :, first : first + plan.packed]
                    turn = (number - target % block) * cycle % plan.packed
                    if turn:
                        turned = pltpu.roll(turned, turn, 1)
                    total = jnp.where(own_lane == number, turned, total)
                out[target, field] = total * has_next if side == 0 else total
            return carry

        lax.fori_loop(0, fields, hand_out, 0)


def zone(plan, place, offsets, scalars, next_swirl, weights, got):
    speed, swirl, diffusion, coupling = scalars
    buffer = held((2, plan.fields, plan.deep + 4, LOW + plan.wide + 8, plan.full))
    rows = -(-(LOW + plan.wide + 8) // 8) * 8
    need = (3 * 2 * plan.fields * (plan.deep + 4) + 2 * plan.fields * (plan.fields + 9)) * rows * plan.full * 4
    sent = jax.ShapeDtypeStruct((plan.sectors, plan.fields, plan.mine, plan.packed), jnp.float32)
    return pl.pallas_call(
        functools.partial(zone_kernel, plan),
        in_specs=[whole(SMEM)] * 7 + [whole(VMEM)] * 2,
        out_specs=[whole(VMEM)] * 3,
        out_shape=[sent, sent, held((8, plan.radial))],
        scratch_shapes=[
            buffer,
            buffer,
            buffer,
            held((2 * plan.fields * (plan.fields + 9), 8, plan.full)),
            held((plan.full, plan.full)),
            held((2, plan.fields, 2 * offsets.shape[0], plan.mine, plan.full)),
        ],
        cost_estimate=pl.CostEstimate(flops=10000000000, transcendentals=0, bytes_accessed=10000000),
        compiler_params=pltpu.CompilerParams(vmem_limit_bytes=need + 6 * 1024 * 1024),
        name="step_zone",
    )(place, offsets, speed, swirl, next_swirl, diffusion, coupling, weights, got)


def unpack_kernel(plan, got, _, *refs):
    *outs, token, tall = refs
    token[...] = jnp.zeros(token.shape, jnp.float32)
    for side in range(2):
        for field in range(plan.fields):
            for sector in range(plan.sectors):
                tall[sector * plan.mine : (sector + 1) * plan.mine, :] = got[sector, side * plan.fields + field]
            flat = tall[...].T
            for section, out in enumerate(outs):
                for plane in range(2):
                    start = (2 * section + plane) * plan.cycle
                    out[side, field, plane] = flat[start : start + plan.cycle]


def unpack(plan, got, sections, after):
    return pl.pallas_call(
        functools.partial(unpack_kernel, plan),
        in_specs=[whole(VMEM)] * 2,
        out_specs=[whole(VMEM)] * (sections + 1),
        out_shape=[held(plan.ghost)] * sections + [held((8, plan.radial))],
        scratch_shapes=[held((plan.radial, plan.packed))],
        cost_estimate=pl.CostEstimate(flops=10000000000, transcendentals=0, bytes_accessed=10000000),
        compiler_params=params(),
        name="unpack_ghosts",
    )(got, near(after[0]))


def edge_shape(plan, kind):
    return held((plan.fields, plan.kept(kind) // 4, 8, plan.radial))


def first_kernel(plan, ranges, kind, state, _, low_ref, high_ref):
    for first, after in ranges:
        start = plan.place(kind, first) // 4

        def body(tile, carry, first=first, start=start):
            for field in range(plan.fields):
                for step in range(4):
                    plane = first + tile * 4 + step
                    rows = slice(2 * step, 2 * step + 2)
                    low_ref[field, start + tile, rows, :] = state[field, plane, 0:2, :]
                    high_ref[field, start + tile, rows, :] = state[field, plane, plan.cycle - 2 : plan.cycle, :]
            return carry

        lax.fori_loop(0, (after - first) // 4, body, 0)


def first_edges(plan, kind, state, after):
    ranges = plan.ranges(kind)
    return pl.pallas_call(
        functools.partial(first_kernel, plan, ranges, kind),
        in_specs=[whole(VMEM), whole(pl.ANY)],
        out_specs=[whole(VMEM)] * 2,
        out_shape=[edge_shape(plan, kind)] * 2,
        cost_estimate=pl.CostEstimate(flops=10000000000, transcendentals=0, bytes_accessed=10000000),
        compiler_params=params(),
        name=f"first_edges_{kind}",
    )(near(state), after)


def coefficients(plan, speed, swirl, diffusion, coupling):
    twelfth = 1.0 / 12.0
    w = swirl[0]
    table = []
    for f in range(plan.fields):
        v, d = speed[f], diffusion[f]
        axial = ((-v - d) * twelfth, (8.0 * v + 16.0 * d) * twelfth, (16.0 * d - 8.0 * v) * twelfth, (v - d) * twelfth)
        cycle = ((-w - d) * twelfth, (8.0 * w + 16.0 * d) * twelfth, (16.0 * d - 8.0 * w) * twelfth, (w - d) * twelfth)
        mix = [coupling[f, e] - 7.0 * d if e == f else coupling[f, e] for e in range(plan.fields)]
        table.append((axial, cycle, d, mix))
    return table


def stage_kernel(plan, stage, kind, names, speed, swirl, diffusion, coupling, *refs):
    ref = dict(zip(names, refs))
    ranges = plan.ranges(kind)
    cycle, radial, last = plan.cycle, plan.radial, stage == 3
    state, work, spread = ref["state"], ref["work"], ref["spread"]
    terms = plan.fields + 9
    for f, (axial, around, d, mix) in enumerate(coefficients(plan, speed, swirl, diffusion, coupling)):
        for number, factor in enumerate((d, *mix, *axial, *around)):
            spread[f * terms + number] = jnp.full((8, radial), factor, jnp.float32)
    lane = lax.broadcasted_iota(jnp.int32, (8, radial), 1)
    not_first = lane > 0
    not_last = lane < radial - 1

    def cells(plane, level):
        if plane < 0:
            return ref["ghosts"][0, :, plane + 2]
        if plane >= plan.axial:
            return ref["ghosts"][1, :, plane - plan.axial]
        if level == 0:
            return state[:, plane]
        owner, at = plan.owner(plane)
        return ref["cells", level, owner][:, at]

    copies = []
    for number, (low, high) in enumerate(ranges):
        size = high - low
        for plane in range(low - 2, high + 2):
            work[:, plane - low + 2, LOW : LOW + cycle, :] = cells(plane, stage)
        for plane in range(low, high):
            owner, at = plan.owner(plane)
            rows = slice(2 * (at % 4), 2 * (at % 4) + 2)
            work[:, plane - low + 2, LOW - 2 : LOW, :] = ref["low halo", owner][:, at // 4, rows, :]
            work[:, plane - low + 2, LOW + cycle : LOW + cycle + 2, :] = ref["high halo", owner][:, at // 4, rows, :]
            if last:
                ref["earlier"][:, plane - low] = cells(plane, 1) + 2.0 * cells(plane, 2)
        start = plan.place(kind, low)

        def compute(tile, steps, low=low, start=start, number=number):
            for f in range(plan.fields):
                factors = [spread[f * terms + number] for number in range(terms)]
                values = {}
                for step in steps:
                    at = tile * 4 + step - start % 4
                    for row in range(0, cycle, 8):
                        here = slice(LOW + row, LOW + row + 8)
                        center = work[f, at + 2, here, :]
                        left = jnp.where(not_first, pltpu.roll(center, 1, 1), 0.0)
                        right = jnp.where(not_last, pltpu.roll(center, radial - 1, 1), 0.0)
                        total = factors[0] * (left + right)
                        for e in range(plan.fields):
                            total += factors[1 + e] * (center if e == f else work[e, at + 2, here, :])
                        for place, by in enumerate((-2, -1, 1, 2)):
                            total += factors[1 + plan.fields + place] * work[f, at + 2 + by, here, :]
                            beside = slice(LOW + row + by, LOW + row + by + 8)
                            total += factors[5 + plan.fields + place] * work[f, at + 2, beside, :]
                        base = state[f, low + at, row : row + 8, :]
                        if last:
                            value = (ref["earlier"][f, at, row : row + 8, :] + center - base) * (1.0 / 3.0)
                            value += (time_step / 6.0) * total
                        else:
                            value = base + (time_step if stage == 2 else 0.5 * time_step) * total
                        values[step, row] = value
                for (step, row), value in values.items():
                    at = tile * 4 + step - start % 4
                    if last:
                        ref["made"][number, f, at, row : row + 8, :] = value
                        continue
                    ref["out"][f, start + at, row : row + 8, :] = value
                    rows = slice(2 * step, 2 * step + 2)
                    if row == 0:
                        ref["low edge"][f, start // 4 + tile, rows, :] = value[:2]
                    if row == cycle - 8:
                        ref["high edge"][f, start // 4 + tile, rows, :] = value[6:]

        head = start % 4
        tiles = (head + size) // 4
        if head:
            compute(0, range(head, min(4, head + size)))
        first = 1 if head else 0

        def whole_tile(tile, carry, compute=compute):
            compute(tile, range(4))
            return carry

        if tiles > first:
            lax.fori_loop(first, tiles, whole_tile, 0)
        tail = (head + size) % 4
        if tail and tiles >= first:
            compute(tiles, range(tail))
        if last:
            copies.append(
                pltpu.make_async_copy(
                    ref["made"].at[number, :, 0:size], ref["result"].at[:, low:high], ref["sem"].at[number]
                )
            )
            copies[-1].start()
    for item in copies:
        item.wait()
    ref["token"][...] = jnp.zeros(ref["token"].shape, jnp.float32)


def stage_call(plan, stage, kind, scalars, state, levels, halos, ghosts, after, result=None):
    ranges = plan.ranges(kind)
    last = stage == 3
    longest = max(high - low for low, high in ranges)
    operands = {"state": near(state)}
    specs = [whole(VMEM)]

    def add(name, value):
        operands[name] = near(value)
        specs.append(whole(VMEM))

    kinds = {plan.owner(plane)[0] for low, high in ranges for plane in range(low, high)}
    for owner in sorted(kinds):
        add(("low halo", owner), halos[owner][0])
        add(("high halo", owner), halos[owner][1])
    for level in (1, 2, stage) if last else (stage,) if stage else ():
        edge = 2 if level == stage else 0
        planes = [plane for low, high in ranges for plane in range(max(0, low - edge), min(plan.axial, high + edge))]
        for owner in sorted({plan.owner(plane)[0] for plane in planes}):
            add(("cells", level, owner), levels[level][owner])
    if kind == "ends":
        add("ghosts", ghosts)
    for number, token in enumerate(after):
        add(("after", number), token)
    aliases = {}
    if result is not None:
        aliases = {len(scalars) + len(operands): 0}
        operands["earlier result"] = result
        specs.append(whole(pl.ANY))
    token = held((8, plan.radial))
    if last:
        outs = {"result": jax.ShapeDtypeStruct(state.shape, jnp.float32), "token": token}
    else:
        edges = edge_shape(plan, kind)
        cells = held((plan.fields, plan.kept(kind), plan.cycle, plan.radial))
        outs = {"out": cells, "low edge": edges, "high edge": edges, "token": token}
    scratch = {
        "work": held((plan.fields, longest + 4, plan.cycle + 16, plan.radial)),
        "spread": held((plan.fields * (plan.fields + 9), 8, plan.radial)),
    }
    if last:
        scratch["earlier"] = held((plan.fields, longest, plan.cycle, plan.radial))
        scratch["made"] = held((len(ranges), plan.fields, longest, plan.cycle, plan.radial))
        scratch["sem"] = pltpu.SemaphoreType.DMA((len(ranges),))
    names = (*operands, *outs, *scratch)
    return pl.pallas_call(
        functools.partial(stage_kernel, plan, stage, kind, names),
        in_specs=[whole(SMEM)] * len(scalars) + specs,
        out_specs=[whole(pl.ANY if name == "result" else VMEM) for name in outs],
        out_shape=list(outs.values()),
        scratch_shapes=list(scratch.values()),
        input_output_aliases=aliases,
        cost_estimate=pl.CostEstimate(flops=10000000000, transcendentals=0, bytes_accessed=10000000),
        compiler_params=params(),
        name=f"stage{stage}_{kind}",
    )(*scalars, *operands.values())


def exchange(edges):
    size = lax.axis_size("sector")
    ahead = [(i, (i + 1) % size) for i in range(size)]
    back = [(i, (i - 1) % size) for i in range(size)]
    low_edges, high_edges = edges
    return lax.ppermute(high_edges, "sector", ahead), lax.ppermute(low_edges, "sector", back)


def on_device(state, interp_blocks, rotor_offset, axial_speed, row_swirl, diffusivity, coupling):
    plan = Plan(state, lax.axis_size("sector"))
    rows = lax.axis_size("row")
    sections = rotor_offset.shape[0]
    place = jnp.stack([lax.axis_index("row"), lax.axis_index("sector")]).astype(jnp.int32)
    scalars = (axial_speed, row_swirl, diffusivity, coupling)
    back = [(row + 1, row) for row in range(rows - 1)]
    ahead = [(row, row + 1) for row in range(rows - 1)]

    below = lax.ppermute(state[:, : plan.deep], "row", back)
    next_swirl = lax.ppermute(row_swirl, "row", back)
    weights = jnp.pad(interp_blocks, ((0, 0), (0, 0), (0, plan.full - interp_blocks.shape[2])))
    packed = pack(plan, state, below)
    levels, halos = [None], [{}]
    got = lax.all_to_all(packed, "sector", 0, 0, tiled=True)
    for kind in ("mid", "ends"):
        halos[0][kind] = exchange(first_edges(plan, kind, state, packed))
    token, result, ghosts = (), None, None

    def step(stage, kind):
        nonlocal token, result
        ghost = ghosts[stage] if kind == "ends" else None
        outs = stage_call(plan, stage, kind, scalars, state, levels, halos[stage], ghost, token, result if stage == sections - 1 else None)
        token = outs[-1:]
        if stage == sections - 1:
            result = outs[0]
            return None
        if len(levels) == stage + 1:
            levels.append({})
            halos.append({})
        levels[stage + 1][kind] = outs[0]
        return outs[1:3]

    def send(stage, kind, edges):
        halos[stage + 1][kind] = exchange(edges)

    def go(stage, kind):
        edges = step(stage, kind)
        if edges is not None:
            send(stage, kind, edges)

    downstream, to_next, *token = zone(plan, place, rotor_offset, scalars, next_swirl, weights, got)
    upstream = lax.ppermute(to_next, "row", ahead)
    mid_edges = step(0, "mid")
    joined = jnp.concatenate([upstream, downstream], axis=1)
    joined, *rest = lax.optimization_barrier((joined, *token, *mid_edges))
    token, mid_edges = rest[:1], rest[1:]
    returned = lax.all_to_all(joined, "sector", 0, 0, tiled=True)
    send(0, "mid", mid_edges)
    *ghosts, last_token = unpack(plan, returned, sections, token)
    token = (last_token,)
    go(0, "ends")
    for stage in range(1, sections):
        go(stage, "mid")
        go(stage, "ends")
    return result


def solution(mesh):
    return jax.shard_map(
        on_device,
        mesh=mesh,
        in_specs=(P(None, "row", "sector", None), P(), P(), P(), P("row"), P(), P()),
        out_specs=P(None, "row", "sector", None),
        check_vma=False,
    )
```

```python
import functools

import jax
import jax.numpy as jnp
from jax import lax
from jax.experimental import pallas as pl
from jax.experimental.pallas import tpu as pltpu
from jax.sharding import PartitionSpec as P

time_step = 0.4
highest = lax.Precision.HIGHEST
VMEM = pltpu.VMEM
SMEM = pltpu.SMEM
EXTRA = 4
BLOCK = 8
LOW = 8


def whole(space):
    return pl.BlockSpec(memory_space=space)


def held(shape):
    return pltpu.VMEM(tuple(shape), jnp.float32)


def near(value):
    return pltpu.with_memory_space_constraint(value, pltpu.VMEM)


def params():
    return pltpu.CompilerParams(vmem_limit_bytes=16 * 1024 * 1024)


class Plan:
    def __init__(self, state, sectors):
        self.fields, self.axial, self.cycle, self.radial = state.shape
        self.sectors = sectors
        self.base = self.axial // 4
        self.ghost = (2, self.fields, 2, self.cycle, self.radial)
        self.deep = 8
        self.full = self.cycle * sectors
        self.mine = self.radial // sectors
        self.wide = self.mine + 2 * EXTRA
        self.packed = self.deep * self.cycle


    def ranges(self, kind):
        if kind == "mid":
            return ((self.base, self.axial - self.base),)
        return ((0, self.base), (self.axial - self.base, self.axial))

    def kept(self, kind):
        return self.axial - 2 * self.base if kind == "mid" else 2 * self.base

    def owner(self, plane):
        kind = "mid" if self.base <= plane < self.axial - self.base else "ends"
        return kind, self.place(kind, plane)

    def place(self, kind, plane):
        if kind == "mid":
            return plane - self.base
        return plane if plane < self.axial // 2 else plane - self.axial + 2 * self.base


def pack_kernel(plan, state, below, out, planes, tall, sem):
    copy = pltpu.make_async_copy(state.at[:, plan.axial - plan.deep : plan.axial], planes, sem.at[0])
    copy.start()
    tall[...] = jnp.zeros(tall.shape, jnp.float32)
    copy.wait()
    for side, source in enumerate((planes, below)):
        for field in range(plan.fields):
            flat = source[field].reshape(plan.packed, plan.radial)
            tall[EXTRA : EXTRA + plan.radial, :] = flat.T
            for sector in range(plan.sectors):
                out[sector, side * plan.fields + field] = tall[sector * plan.mine : sector * plan.mine + plan.wide, :]


def pack(plan, state, below):
    return pl.pallas_call(
        functools.partial(pack_kernel, plan),
        in_specs=[whole(pl.ANY), whole(VMEM)],
        out_specs=whole(VMEM),
        out_shape=jax.ShapeDtypeStruct((plan.sectors, 2 * plan.fields, plan.wide, plan.packed), jnp.float32),
        scratch_shapes=[
            held((plan.fields, plan.deep, plan.cycle, plan.radial)),
            held((plan.radial + 2 * EXTRA, plan.packed)),
            pltpu.SemaphoreType.DMA((1,)),
        ],
        cost_estimate=pl.CostEstimate(flops=10000000000, transcendentals=0, bytes_accessed=10000000),
        compiler_params=params(),
        name="pack_zone",
    )(state, below)


def zone_kernel(plan, place, offsets, speed, swirl, next_swirl, diffusion, coupling, weights, got, *refs):
    to_here, to_next, token, base, now, later, spread, matrix, made = refs
    token[...] = jnp.zeros(token.shape, jnp.float32)
    fields, deep, cycle, full, wide = plan.fields, plan.deep, plan.cycle, plan.full, plan.wide
    sections = offsets.shape[0]
    row, sector = place[0], place[1]
    terms = fields + 9
    rows = slice(LOW, LOW + wide)
    lane = lax.broadcasted_iota(jnp.int32, (wide, plan.packed), 1) // cycle
    own_lane = lax.broadcasted_iota(jnp.int32, (plan.mine, plan.packed), 1) // cycle
    at_radius = lax.broadcasted_iota(jnp.int32, (wide, full), 0) + sector * plan.mine - EXTRA
    inside = (at_radius >= 0) & (at_radius < plan.radial)
    block = plan.packed // cycle

    for side, w in enumerate((swirl, next_swirl)):
        for f, (axial, around, d, mix) in enumerate(coefficients(plan, speed, w, diffusion, coupling)):
            for number, factor in enumerate((d, *mix, *axial, *around)):
                spread[side * fields * terms + f * terms + number] = jnp.full((8, full), factor, jnp.float32)

    for buffer in (now, later):
        for side in range(2):
            def clear(field, carry, buffer=buffer, side=side):
                for first, after in ((0, LOW), (LOW + wide, buffer.shape[3])):
                    empty = jnp.zeros((buffer.shape[2], after - first, full), jnp.float32)
                    buffer[side, field, :, first:after, :] = empty
                return carry

            lax.fori_loop(0, fields, clear, 0)

    for side in range(2):
        def spread_out(field, carry, side=side):
            for plane in range(deep):
                parts = []
                for first in range(0, plan.sectors, block):
                    total = jnp.zeros((wide, plan.packed), jnp.float32)
                    for number in range(min(block, plan.sectors - first)):
                        turned = got[first + number, side * fields + field]
                        turn = (number - plane) * cycle % plan.packed
                        if turn:
                            turned = pltpu.roll(turned, turn, 1)
                        total = jnp.where(lane == number, turned, total)
                    parts.append(total)
                value = parts[0] if len(parts) == 1 else jnp.concatenate(parts, axis=1)
                base[side, field, 2 + plane, rows, :] = value
                now[side, field, 2 + plane, rows, :] = value
            return carry

        lax.fori_loop(0, fields, spread_out, 0)

    for section in range(sections):
        offset = offsets[section, jnp.minimum(row, offsets.shape[1] - 1)]
        for side in range(2):
            here = lax.rem(full - offset, full) if side == 0 else offset
            shift, cell = here // cycle, lax.rem(here, cycle)
            for target in range(plan.sectors):
                matrix[target * cycle : (target + 1) * cycle, :] = pltpu.roll(
                    weights[cell], lax.rem(target + shift, plan.sectors) * cycle, 1
                )
            other = 1 - side
            first = 2 if other == 1 else deep
            to = deep + 2 if side == 0 else 0
            pairs = [(field, plane) for field in range(fields) for plane in range(2)]
            values = [now[other, field, first + plane, rows, :] for field, plane in pairs]
            turn = matrix[...]
            together = wide % 8 == 0
            if together:
                values = [jnp.concatenate(values, axis=0)]
            results = [
                lax.dot_general(
                    value, turn, (((1,), (1,)), ((), ())), precision=highest, preferred_element_type=jnp.float32
                )
                for value in values
            ]
            for number, (field, plane) in enumerate(pairs):
                if together:
                    value = results[0][number * wide : (number + 1) * wide]
                else:
                    value = results[number]
                now[side, field, to + plane, rows, :] = value
                made[side, field, 2 * section + plane] = now[side, field, to + plane, LOW + EXTRA : LOW + EXTRA + plan.mine, :]
        if section == sections - 1:
            break
        size = deep - 2 * (section + 1)
        step_size = time_step if section == sections - 2 else 0.5 * time_step
        for side in range(2):
            begin = 2 + (deep - size if side == 0 else 0)

            def advance(number, carry, side=side, begin=begin, now=now, later=later, step_size=step_size):
                plane = begin + number
                for f in range(fields):
                    start = side * fields * terms + f * terms
                    factors = [spread[start + number] for number in range(terms)]
                    for first in range(0, wide, 8):
                        tall = min(8, wide - first)
                        factor = lambda k: factors[k] if tall == 8 else factors[k][:tall]
                        here = slice(LOW + first, LOW + first + tall)
                        center = now[side, f, plane, here, :]
                        total = factor(0) * (
                            now[side, f, plane, LOW + first - 1 : LOW + first - 1 + tall, :]
                            + now[side, f, plane, LOW + first + 1 : LOW + first + 1 + tall, :]
                        )
                        for e in range(fields):
                            total += factor(1 + e) * (center if e == f else now[side, e, plane, here, :])
                        for place_at, by in enumerate((-2, -1, 1, 2)):
                            total += factor(1 + fields + place_at) * now[side, f, plane + by, here, :]
                            total += factor(5 + fields + place_at) * pltpu.roll(center, -by % full, 1)
                        value = base[side, f, plane, here, :] + step_size * total
                        later[side, f, plane, here, :] = jnp.where(inside[first : first + tall], value, 0.0)
                return carry

            lax.fori_loop(0, size, advance, 0)
        now, later = later, now

    has_next = (row < offsets.shape[1]).astype(jnp.float32)
    for side, out in enumerate((to_here, to_next)):
        def hand_out(field, carry, side=side, out=out):
            for target in range(plan.sectors):
                total = jnp.zeros((plan.mine, plan.packed), jnp.float32)
                first = target // block * plan.packed
                for number in range(2 * sections):
                    turned = made[side, field, number, :, first : first + plan.packed]
                    turn = (number - target % block) * cycle % plan.packed
                    if turn:
                        turned = pltpu.roll(turned, turn, 1)
                    total = jnp.where(own_lane == number, turned, total)
                out[target, field] = total * has_next if side == 0 else total
            return carry

        lax.fori_loop(0, fields, hand_out, 0)


def zone(plan, place, offsets, scalars, next_swirl, weights, got):
    speed, swirl, diffusion, coupling = scalars
    buffer = held((2, plan.fields, plan.deep + 4, LOW + plan.wide + 8, plan.full))
    rows = -(-(LOW + plan.wide + 8) // 8) * 8
    need = (3 * 2 * plan.fields * (plan.deep + 4) + 2 * plan.fields * (plan.fields + 9)) * rows * plan.full * 4
    sent = jax.ShapeDtypeStruct((plan.sectors, plan.fields, plan.mine, plan.packed), jnp.float32)
    return pl.pallas_call(
        functools.partial(zone_kernel, plan),
        in_specs=[whole(SMEM)] * 7 + [whole(VMEM)] * 2,
        out_specs=[whole(VMEM)] * 3,
        out_shape=[sent, sent, held((8, plan.radial))],
        scratch_shapes=[
            buffer,
            buffer,
            buffer,
            held((2 * plan.fields * (plan.fields + 9), 8, plan.full)),
            held((plan.full, plan.full)),
            held((2, plan.fields, 2 * offsets.shape[0], plan.mine, plan.full)),
        ],
        cost_estimate=pl.CostEstimate(flops=10000000000, transcendentals=0, bytes_accessed=10000000),
        compiler_params=pltpu.CompilerParams(vmem_limit_bytes=need + 6 * 1024 * 1024),
        name="step_zone",
    )(place, offsets, speed, swirl, next_swirl, diffusion, coupling, weights, got)


def unpack_kernel(plan, got, _, *refs):
    *outs, token, tall = refs
    token[...] = jnp.zeros(token.shape, jnp.float32)
    for side in range(2):
        for field in range(plan.fields):
            for sector in range(plan.sectors):
                tall[sector * plan.mine : (sector + 1) * plan.mine, :] = got[sector, side * plan.fields + field]
            flat = tall[...].T
            for section, out in enumerate(outs):
                for plane in range(2):
                    start = (2 * section + plane) * plan.cycle
                    out[side, field, plane] = flat[start : start + plan.cycle]


def unpack(plan, got, sections, after):
    return pl.pallas_call(
        functools.partial(unpack_kernel, plan),
        in_specs=[whole(VMEM)] * 2,
        out_specs=[whole(VMEM)] * (sections + 1),
        out_shape=[held(plan.ghost)] * sections + [held((8, plan.radial))],
        scratch_shapes=[held((plan.radial, plan.packed))],
        cost_estimate=pl.CostEstimate(flops=10000000000, transcendentals=0, bytes_accessed=10000000),
        compiler_params=params(),
        name="unpack_ghosts",
    )(got, near(after[0]))


def edge_shape(plan, kind):
    return held((plan.fields, plan.kept(kind) // 4, 8, plan.radial))


def first_kernel(plan, ranges, kind, state, _, low_ref, high_ref):
    for first, after in ranges:
        start = plan.place(kind, first) // 4

        def body(tile, carry, first=first, start=start):
            for field in range(plan.fields):
                for step in range(4):
                    plane = first + tile * 4 + step
                    rows = slice(2 * step, 2 * step + 2)
                    low_ref[field, start + tile, rows, :] = state[field, plane, 0:2, :]
                    high_ref[field, start + tile, rows, :] = state[field, plane, plan.cycle - 2 : plan.cycle, :]
            return carry

        lax.fori_loop(0, (after - first) // 4, body, 0)


def first_edges(plan, kind, state, after):
    ranges = plan.ranges(kind)
    return pl.pallas_call(
        functools.partial(first_kernel, plan, ranges, kind),
        in_specs=[whole(VMEM), whole(pl.ANY)],
        out_specs=[whole(VMEM)] * 2,
        out_shape=[edge_shape(plan, kind)] * 2,
        cost_estimate=pl.CostEstimate(flops=10000000000, transcendentals=0, bytes_accessed=10000000),
        compiler_params=params(),
        name=f"first_edges_{kind}",
    )(near(state), after)


def coefficients(plan, speed, swirl, diffusion, coupling):
    twelfth = 1.0 / 12.0
    w = swirl[0]
    table = []
    for f in range(plan.fields):
        v, d = speed[f], diffusion[f]
        axial = ((-v - d) * twelfth, (8.0 * v + 16.0 * d) * twelfth, (16.0 * d - 8.0 * v) * twelfth, (v - d) * twelfth)
        cycle = ((-w - d) * twelfth, (8.0 * w + 16.0 * d) * twelfth, (16.0 * d - 8.0 * w) * twelfth, (w - d) * twelfth)
        mix = [coupling[f, e] - 7.0 * d if e == f else coupling[f, e] for e in range(plan.fields)]
        table.append((axial, cycle, d, mix))
    return table


def stage_kernel(plan, stage, kind, names, speed, swirl, diffusion, coupling, *refs):
    ref = dict(zip(names, refs))
    ranges = plan.ranges(kind)
    cycle, radial, last = plan.cycle, plan.radial, stage == 3
    state, work, spread = ref["state"], ref["work"], ref["spread"]
    terms = plan.fields + 9
    for f, (axial, around, d, mix) in enumerate(coefficients(plan, speed, swirl, diffusion, coupling)):
        for number, factor in enumerate((d, *mix, *axial, *around)):
            spread[f * terms + number] = jnp.full((8, radial), factor, jnp.float32)
    lane = lax.broadcasted_iota(jnp.int32, (8, radial), 1)
    not_first = lane > 0
    not_last = lane < radial - 1

    def cells(plane, level):
        if plane < 0:
            return ref["ghosts"][0, :, plane + 2]
        if plane >= plan.axial:
            return ref["ghosts"][1, :, plane - plan.axial]
        if level == 0:
            return state[:, plane]
        owner, at = plan.owner(plane)
        return ref["cells", level, owner][:, at]

    copies = []
    for number, (low, high) in enumerate(ranges):
        size = high - low
        for plane in range(low - 2, high + 2):
            work[:, plane - low + 2, LOW : LOW + cycle, :] = cells(plane, stage)
        for plane in range(low, high):
            owner, at = plan.owner(plane)
            rows = slice(2 * (at % 4), 2 * (at % 4) + 2)
            work[:, plane - low + 2, LOW - 2 : LOW, :] = ref["low halo", owner][:, at // 4, rows, :]
            work[:, plane - low + 2, LOW + cycle : LOW + cycle + 2, :] = ref["high halo", owner][:, at // 4, rows, :]
            if last:
                ref["earlier"][:, plane - low] = cells(plane, 1) + 2.0 * cells(plane, 2)
        start = plan.place(kind, low)

        def compute(tile, steps, low=low, start=start, number=number):
            for f in range(plan.fields):
                factors = [spread[f * terms + number] for number in range(terms)]
                values = {}
                for step in steps:
                    at = tile * 4 + step - start % 4
                    for row in range(0, cycle, 8):
                        here = slice(LOW + row, LOW + row + 8)
                        center = work[f, at + 2, here, :]
                        left = jnp.where(not_first, pltpu.roll(center, 1, 1), 0.0)
                        right = jnp.where(not_last, pltpu.roll(center, radial - 1, 1), 0.0)
                        total = factors[0] * (left + right)
                        for e in range(plan.fields):
                            total += factors[1 + e] * (center if e == f else work[e, at + 2, here, :])
                        for place, by in enumerate((-2, -1, 1, 2)):
                            total += factors[1 + plan.fields + place] * work[f, at + 2 + by, here, :]
                            beside = slice(LOW + row + by, LOW + row + by + 8)
                            total += factors[5 + plan.fields + place] * work[f, at + 2, beside, :]
                        base = state[f, low + at, row : row + 8, :]
                        if last:
                            value = (ref["earlier"][f, at, row : row + 8, :] + center - base) * (1.0 / 3.0)
                            value += (time_step / 6.0) * total
                        else:
                            value = base + (time_step if stage == 2 else 0.5 * time_step) * total
                        values[step, row] = value
                for (step, row), value in values.items():
                    at = tile * 4 + step - start % 4
                    if last:
                        ref["made"][number, f, at, row : row + 8, :] = value
                        continue
                    ref["out"][f, start + at, row : row + 8, :] = value
                    rows = slice(2 * step, 2 * step + 2)
                    if row == 0:
                        ref["low edge"][f, start // 4 + tile, rows, :] = value[:2]
                    if row == cycle - 8:
                        ref["high edge"][f, start // 4 + tile, rows, :] = value[6:]

        def whole_tile(tile, carry, compute=compute):
            compute(tile, range(4))
            return carry

        block = BLOCK // 4 if last else size // 4
        for first in range(0, size // 4, block):
            after = min(first + block, size // 4)
            lax.fori_loop(first, after, whole_tile, 0)
            if last:
                copies.append(
                    pltpu.make_async_copy(
                        ref["made"].at[number, :, 4 * first : 4 * after],
                        ref["result"].at[:, low + 4 * first : low + 4 * after],
                        ref["sem"].at[len(copies)],
                    )
                )
                copies[-1].start()
    for item in copies:
        item.wait()
    ref["token"][...] = jnp.zeros(ref["token"].shape, jnp.float32)


def stage_call(plan, stage, kind, scalars, state, levels, halos, ghosts, after, result=None):
    ranges = plan.ranges(kind)
    last = stage == 3
    longest = max(high - low for low, high in ranges)
    operands = {"state": near(state)}
    specs = [whole(VMEM)]

    def add(name, value):
        operands[name] = near(value)
        specs.append(whole(VMEM))

    kinds = {plan.owner(plane)[0] for low, high in ranges for plane in range(low, high)}
    for owner in sorted(kinds):
        add(("low halo", owner), halos[owner][0])
        add(("high halo", owner), halos[owner][1])
    for level in (1, 2, stage) if last else (stage,) if stage else ():
        edge = 2 if level == stage else 0
        planes = [plane for low, high in ranges for plane in range(max(0, low - edge), min(plan.axial, high + edge))]
        for owner in sorted({plan.owner(plane)[0] for plane in planes}):
            add(("cells", level, owner), levels[level][owner])
    if kind == "ends":
        add("ghosts", ghosts)
    for number, token in enumerate(after):
        add(("after", number), token)
    aliases = {}
    if result is not None:
        aliases = {len(scalars) + len(operands): 0}
        operands["earlier result"] = result
        specs.append(whole(pl.ANY))
    token = held((8, plan.radial))
    if last:
        outs = {"result": jax.ShapeDtypeStruct(state.shape, jnp.float32), "token": token}
    else:
        edges = edge_shape(plan, kind)
        cells = held((plan.fields, plan.kept(kind), plan.cycle, plan.radial))
        outs = {"out": cells, "low edge": edges, "high edge": edges, "token": token}
    scratch = {
        "work": held((plan.fields, longest + 4, plan.cycle + 16, plan.radial)),
        "spread": held((plan.fields * (plan.fields + 9), 8, plan.radial)),
    }
    if last:
        scratch["earlier"] = held((plan.fields, longest, plan.cycle, plan.radial))
        scratch["made"] = held((len(ranges), plan.fields, longest, plan.cycle, plan.radial))
        scratch["sem"] = pltpu.SemaphoreType.DMA((sum(-(-(high - low) // BLOCK) for low, high in ranges),))
    names = (*operands, *outs, *scratch)
    return pl.pallas_call(
        functools.partial(stage_kernel, plan, stage, kind, names),
        in_specs=[whole(SMEM)] * len(scalars) + specs,
        out_specs=[whole(pl.ANY if name == "result" else VMEM) for name in outs],
        out_shape=list(outs.values()),
        scratch_shapes=list(scratch.values()),
        input_output_aliases=aliases,
        cost_estimate=pl.CostEstimate(flops=10000000000, transcendentals=0, bytes_accessed=10000000),
        compiler_params=params(),
        name=f"stage{stage}_{kind}",
    )(*scalars, *operands.values())


def exchange(edges):
    size = lax.axis_size("sector")
    ahead = [(i, (i + 1) % size) for i in range(size)]
    back = [(i, (i - 1) % size) for i in range(size)]
    low_edges, high_edges = edges
    return lax.ppermute(high_edges, "sector", ahead), lax.ppermute(low_edges, "sector", back)


def on_device(state, interp_blocks, rotor_offset, axial_speed, row_swirl, diffusivity, coupling):
    plan = Plan(state, lax.axis_size("sector"))
    rows = lax.axis_size("row")
    sections = rotor_offset.shape[0]
    place = jnp.stack([lax.axis_index("row"), lax.axis_index("sector")]).astype(jnp.int32)
    scalars = (axial_speed, row_swirl, diffusivity, coupling)
    back = [(row + 1, row) for row in range(rows - 1)]
    ahead = [(row, row + 1) for row in range(rows - 1)]

    below = lax.ppermute(state[:, : plan.deep], "row", back)
    next_swirl = lax.ppermute(row_swirl, "row", back)
    weights = jnp.pad(interp_blocks, ((0, 0), (0, 0), (0, plan.full - interp_blocks.shape[2])))
    packed = pack(plan, state, below)
    levels, halos = [None], [{}]
    got = lax.all_to_all(packed, "sector", 0, 0, tiled=True)
    for kind in ("mid", "ends"):
        halos[0][kind] = exchange(first_edges(plan, kind, state, packed))
    token, result, ghosts = (), None, None

    def step(stage, kind):
        nonlocal token, result
        ghost = ghosts[stage] if kind == "ends" else None
        outs = stage_call(plan, stage, kind, scalars, state, levels, halos[stage], ghost, token, result if stage == sections - 1 else None)
        token = outs[-1:]
        if stage == sections - 1:
            result = outs[0]
            return None
        if len(levels) == stage + 1:
            levels.append({})
            halos.append({})
        levels[stage + 1][kind] = outs[0]
        return outs[1:3]

    def send(stage, kind, edges):
        halos[stage + 1][kind] = exchange(edges)

    def go(stage, kind):
        edges = step(stage, kind)
        if edges is not None:
            send(stage, kind, edges)

    downstream, to_next, *token = zone(plan, place, rotor_offset, scalars, next_swirl, weights, got)
    upstream = lax.ppermute(to_next, "row", ahead)
    mid_edges = step(0, "mid")
    joined = jnp.concatenate([upstream, downstream], axis=1)
    joined, *rest = lax.optimization_barrier((joined, *token, *mid_edges, *halos[0]["ends"]))
    token, mid_edges, halos[0]["ends"] = rest[:1], rest[1:3], rest[3:]
    returned = lax.all_to_all(joined, "sector", 0, 0, tiled=True)
    send(0, "mid", mid_edges)
    *ghosts, last_token = unpack(plan, returned, sections, token)
    token = (last_token,)
    go(0, "ends")
    for stage in range(1, sections):
        go(stage, "mid")
        go(stage, "ends")
    return result


def solution(mesh):
    return jax.shard_map(
        on_device,
        mesh=mesh,
        in_specs=(P(None, "row", "sector", None), P(), P(), P(), P("row"), P(), P()),
        out_specs=P(None, "row", "sector", None),
        check_vma=False,
    )
```

```python
import functools

import jax
import jax.numpy as jnp
from jax import lax
from jax.experimental import pallas as pl
from jax.experimental.pallas import tpu as pltpu
from jax.sharding import PartitionSpec as P

time_step = 0.4
highest = lax.Precision.HIGHEST
VMEM = pltpu.VMEM
SMEM = pltpu.SMEM
EXTRA = 4
BLOCK = 8
LOW = 8


def whole(space):
    return pl.BlockSpec(memory_space=space)


def held(shape):
    return pltpu.VMEM(tuple(shape), jnp.float32)


def near(value):
    return pltpu.with_memory_space_constraint(value, pltpu.VMEM)


def params():
    return pltpu.CompilerParams(vmem_limit_bytes=16 * 1024 * 1024)


class Plan:
    def __init__(self, state, sectors):
        self.fields, self.axial, self.cycle, self.radial = state.shape
        self.sectors = sectors
        self.base = self.axial // 4
        self.ghost = (2, self.fields, 2, self.cycle, self.radial)
        self.deep = 8
        self.full = self.cycle * sectors
        self.mine = self.radial // sectors
        self.wide = self.mine + 2 * EXTRA
        self.packed = self.deep * self.cycle


    def ranges(self, kind):
        if kind == "mid":
            return ((self.base, self.axial - self.base),)
        return ((0, self.base), (self.axial - self.base, self.axial))

    def kept(self, kind):
        return self.axial - 2 * self.base if kind == "mid" else 2 * self.base

    def owner(self, plane):
        kind = "mid" if self.base <= plane < self.axial - self.base else "ends"
        return kind, self.place(kind, plane)

    def place(self, kind, plane):
        if kind == "mid":
            return plane - self.base
        return plane if plane < self.axial // 2 else plane - self.axial + 2 * self.base


def pack_kernel(plan, state, below, out, planes, tall, sem):
    copy = pltpu.make_async_copy(state.at[:, plan.axial - plan.deep : plan.axial], planes, sem.at[0])
    copy.start()
    tall[...] = jnp.zeros(tall.shape, jnp.float32)
    copy.wait()
    for side, source in enumerate((planes, below)):
        for field in range(plan.fields):
            flat = source[field].reshape(plan.packed, plan.radial)
            tall[EXTRA : EXTRA + plan.radial, :] = flat.T
            for sector in range(plan.sectors):
                out[sector, side * plan.fields + field] = tall[sector * plan.mine : sector * plan.mine + plan.wide, :]


def pack(plan, state, below):
    return pl.pallas_call(
        functools.partial(pack_kernel, plan),
        in_specs=[whole(pl.ANY), whole(VMEM)],
        out_specs=whole(VMEM),
        out_shape=jax.ShapeDtypeStruct((plan.sectors, 2 * plan.fields, plan.wide, plan.packed), jnp.float32),
        scratch_shapes=[
            held((plan.fields, plan.deep, plan.cycle, plan.radial)),
            held((plan.radial + 2 * EXTRA, plan.packed)),
            pltpu.SemaphoreType.DMA((1,)),
        ],
        cost_estimate=pl.CostEstimate(flops=10000000000, transcendentals=0, bytes_accessed=10000000),
        compiler_params=params(),
        name="pack_zone",
    )(state, below)


def zone_kernel(plan, place, offsets, speed, swirl, next_swirl, diffusion, coupling, weights, got, *refs):
    to_here, to_next, token, base, now, later, spread, matrix, made = refs
    token[...] = jnp.zeros(token.shape, jnp.float32)
    fields, deep, cycle, full, wide = plan.fields, plan.deep, plan.cycle, plan.full, plan.wide
    sections = offsets.shape[0]
    row, sector = place[0], place[1]
    terms = fields + 9
    rows = slice(LOW, LOW + wide)
    lane = lax.broadcasted_iota(jnp.int32, (wide, plan.packed), 1) // cycle
    own_lane = lax.broadcasted_iota(jnp.int32, (plan.mine, plan.packed), 1) // cycle
    at_radius = lax.broadcasted_iota(jnp.int32, (wide, full), 0) + sector * plan.mine - EXTRA
    inside = (at_radius >= 0) & (at_radius < plan.radial)
    block = plan.packed // cycle

    for side, w in enumerate((swirl, next_swirl)):
        for f, (axial, around, d, mix) in enumerate(coefficients(plan, speed, w, diffusion, coupling)):
            for number, factor in enumerate((d, *mix, *axial, *around)):
                spread[side * fields * terms + f * terms + number] = jnp.full((8, full), factor, jnp.float32)

    for buffer in (now, later):
        for side in range(2):
            def clear(field, carry, buffer=buffer, side=side):
                for first, after in ((0, LOW), (LOW + wide, buffer.shape[3])):
                    empty = jnp.zeros((buffer.shape[2], after - first, full), jnp.float32)
                    buffer[side, field, :, first:after, :] = empty
                return carry

            lax.fori_loop(0, fields, clear, 0)

    for side in range(2):
        def spread_out(field, carry, side=side):
            for plane in range(deep):
                parts = []
                for first in range(0, plan.sectors, block):
                    total = jnp.zeros((wide, plan.packed), jnp.float32)
                    for number in range(min(block, plan.sectors - first)):
                        turned = got[first + number, side * fields + field]
                        turn = (number - plane) * cycle % plan.packed
                        if turn:
                            turned = pltpu.roll(turned, turn, 1)
                        total = jnp.where(lane == number, turned, total)
                    parts.append(total)
                value = parts[0] if len(parts) == 1 else jnp.concatenate(parts, axis=1)
                base[side, field, 2 + plane, rows, :] = value
                now[side, field, 2 + plane, rows, :] = value
            return carry

        lax.fori_loop(0, fields, spread_out, 0)

    for section in range(sections):
        offset = offsets[section, jnp.minimum(row, offsets.shape[1] - 1)]
        for side in range(2):
            here = lax.rem(full - offset, full) if side == 0 else offset
            shift, cell = here // cycle, lax.rem(here, cycle)
            for target in range(plan.sectors):
                matrix[target * cycle : (target + 1) * cycle, :] = pltpu.roll(
                    weights[cell], lax.rem(target + shift, plan.sectors) * cycle, 1
                )
            other = 1 - side
            first = 2 if other == 1 else deep
            to = deep + 2 if side == 0 else 0
            pairs = [(field, plane) for field in range(fields) for plane in range(2)]
            values = [now[other, field, first + plane, rows, :] for field, plane in pairs]
            turn = matrix[...]
            together = wide % 8 == 0
            if together:
                values = [jnp.concatenate(values, axis=0)]
            results = [
                lax.dot_general(
                    value, turn, (((1,), (1,)), ((), ())), precision=highest, preferred_element_type=jnp.float32
                )
                for value in values
            ]
            for number, (field, plane) in enumerate(pairs):
                if together:
                    value = results[0][number * wide : (number + 1) * wide]
                else:
                    value = results[number]
                now[side, field, to + plane, rows, :] = value
                made[side, field, 2 * section + plane] = now[side, field, to + plane, LOW + EXTRA : LOW + EXTRA + plan.mine, :]
        if section == sections - 1:
            break
        size = deep - 2 * (section + 1)
        step_size = time_step if section == sections - 2 else 0.5 * time_step
        for side in range(2):
            begin = 2 + (deep - size if side == 0 else 0)

            def advance(number, carry, side=side, begin=begin, now=now, later=later, step_size=step_size):
                plane = begin + number
                for f in range(fields):
                    start = side * fields * terms + f * terms
                    factors = [spread[start + number] for number in range(terms)]
                    for first in range(0, wide, 8):
                        tall = min(8, wide - first)
                        factor = lambda k: factors[k] if tall == 8 else factors[k][:tall]
                        here = slice(LOW + first, LOW + first + tall)
                        center = now[side, f, plane, here, :]
                        total = factor(0) * (
                            now[side, f, plane, LOW + first - 1 : LOW + first - 1 + tall, :]
                            + now[side, f, plane, LOW + first + 1 : LOW + first + 1 + tall, :]
                        )
                        for e in range(fields):
                            total += factor(1 + e) * (center if e == f else now[side, e, plane, here, :])
                        for place_at, by in enumerate((-2, -1, 1, 2)):
                            total += factor(1 + fields + place_at) * now[side, f, plane + by, here, :]
                            total += factor(5 + fields + place_at) * pltpu.roll(center, -by % full, 1)
                        value = base[side, f, plane, here, :] + step_size * total
                        later[side, f, plane, here, :] = jnp.where(inside[first : first + tall], value, 0.0)
                return carry

            lax.fori_loop(0, size, advance, 0)
        now, later = later, now

    has_next = (row < offsets.shape[1]).astype(jnp.float32)
    for side, out in enumerate((to_here, to_next)):
        def hand_out(field, carry, side=side, out=out):
            for target in range(plan.sectors):
                total = jnp.zeros((plan.mine, plan.packed), jnp.float32)
                first = target // block * plan.packed
                for number in range(2 * sections):
                    turned = made[side, field, number, :, first : first + plan.packed]
                    turn = (number - target % block) * cycle % plan.packed
                    if turn:
                        turned = pltpu.roll(turned, turn, 1)
                    total = jnp.where(own_lane == number, turned, total)
                out[target, field] = total * has_next if side == 0 else total
            return carry

        lax.fori_loop(0, fields, hand_out, 0)


def zone(plan, place, offsets, scalars, next_swirl, weights, got):
    speed, swirl, diffusion, coupling = scalars
    buffer = held((2, plan.fields, plan.deep + 4, LOW + plan.wide + 8, plan.full))
    rows = -(-(LOW + plan.wide + 8) // 8) * 8
    need = (3 * 2 * plan.fields * (plan.deep + 4) + 2 * plan.fields * (plan.fields + 9)) * rows * plan.full * 4
    sent = jax.ShapeDtypeStruct((plan.sectors, plan.fields, plan.mine, plan.packed), jnp.float32)
    return pl.pallas_call(
        functools.partial(zone_kernel, plan),
        in_specs=[whole(SMEM)] * 7 + [whole(VMEM)] * 2,
        out_specs=[whole(VMEM)] * 3,
        out_shape=[sent, sent, held((8, plan.radial))],
        scratch_shapes=[
            buffer,
            buffer,
            buffer,
            held((2 * plan.fields * (plan.fields + 9), 8, plan.full)),
            held((plan.full, plan.full)),
            held((2, plan.fields, 2 * offsets.shape[0], plan.mine, plan.full)),
        ],
        cost_estimate=pl.CostEstimate(flops=10000000000, transcendentals=0, bytes_accessed=10000000),
        compiler_params=pltpu.CompilerParams(vmem_limit_bytes=need + 6 * 1024 * 1024),
        name="step_zone",
    )(place, offsets, speed, swirl, next_swirl, diffusion, coupling, weights, got)


def unpack_kernel(plan, got, _, *refs):
    *outs, token, tall = refs
    token[...] = jnp.zeros(token.shape, jnp.float32)
    for side in range(2):
        for field in range(plan.fields):
            for sector in range(plan.sectors):
                tall[sector * plan.mine : (sector + 1) * plan.mine, :] = got[sector, side * plan.fields + field]
            flat = tall[...].T
            for section, out in enumerate(outs):
                for plane in range(2):
                    start = (2 * section + plane) * plan.cycle
                    out[side, field, plane] = flat[start : start + plan.cycle]


def unpack(plan, got, sections, after):
    return pl.pallas_call(
        functools.partial(unpack_kernel, plan),
        in_specs=[whole(VMEM)] * 2,
        out_specs=[whole(VMEM)] * (sections + 1),
        out_shape=[held(plan.ghost)] * sections + [held((8, plan.radial))],
        scratch_shapes=[held((plan.radial, plan.packed))],
        cost_estimate=pl.CostEstimate(flops=10000000000, transcendentals=0, bytes_accessed=10000000),
        compiler_params=params(),
        name="unpack_ghosts",
    )(got, near(after[0]))


def edge_shape(plan, kind):
    return held((plan.fields, plan.kept(kind) // 4, 8, plan.radial))


def first_kernel(plan, ranges, kind, state, _, low_ref, high_ref):
    for first, after in ranges:
        start = plan.place(kind, first) // 4

        def body(tile, carry, first=first, start=start):
            for field in range(plan.fields):
                for step in range(4):
                    plane = first + tile * 4 + step
                    rows = slice(2 * step, 2 * step + 2)
                    low_ref[field, start + tile, rows, :] = state[field, plane, 0:2, :]
                    high_ref[field, start + tile, rows, :] = state[field, plane, plan.cycle - 2 : plan.cycle, :]
            return carry

        lax.fori_loop(0, (after - first) // 4, body, 0)


def first_edges(plan, kind, state, after):
    ranges = plan.ranges(kind)
    return pl.pallas_call(
        functools.partial(first_kernel, plan, ranges, kind),
        in_specs=[whole(VMEM), whole(pl.ANY)],
        out_specs=[whole(VMEM)] * 2,
        out_shape=[edge_shape(plan, kind)] * 2,
        cost_estimate=pl.CostEstimate(flops=10000000000, transcendentals=0, bytes_accessed=10000000),
        compiler_params=params(),
        name=f"first_edges_{kind}",
    )(near(state), after)


def coefficients(plan, speed, swirl, diffusion, coupling):
    twelfth = 1.0 / 12.0
    w = swirl[0]
    table = []
    for f in range(plan.fields):
        v, d = speed[f], diffusion[f]
        axial = ((-v - d) * twelfth, (8.0 * v + 16.0 * d) * twelfth, (16.0 * d - 8.0 * v) * twelfth, (v - d) * twelfth)
        cycle = ((-w - d) * twelfth, (8.0 * w + 16.0 * d) * twelfth, (16.0 * d - 8.0 * w) * twelfth, (w - d) * twelfth)
        mix = [coupling[f, e] - 7.0 * d if e == f else coupling[f, e] for e in range(plan.fields)]
        table.append((axial, cycle, d, mix))
    return table


def stage_kernel(plan, stage, kind, names, speed, swirl, diffusion, coupling, *refs):
    ref = dict(zip(names, refs))
    ranges = plan.ranges(kind)
    cycle, radial, last = plan.cycle, plan.radial, stage == 3
    state, work, spread = ref["state"], ref["work"], ref["spread"]
    terms = plan.fields + 9
    for f, (axial, around, d, mix) in enumerate(coefficients(plan, speed, swirl, diffusion, coupling)):
        for number, factor in enumerate((d, *mix, *axial, *around)):
            spread[f * terms + number] = jnp.full((8, radial), factor, jnp.float32)
    lane = lax.broadcasted_iota(jnp.int32, (8, radial), 1)
    not_first = lane > 0
    not_last = lane < radial - 1

    def cells(plane, level):
        if plane < 0:
            return ref["ghosts"][0, :, plane + 2]
        if plane >= plan.axial:
            return ref["ghosts"][1, :, plane - plan.axial]
        if level == 0:
            return state[:, plane]
        owner, at = plan.owner(plane)
        return ref["cells", level, owner][:, at]

    copies = []
    for number, (low, high) in enumerate(ranges):
        size = high - low
        for plane in range(low - 2, high + 2):
            work[:, plane - low + 2, LOW : LOW + cycle, :] = cells(plane, stage)
        for plane in range(low, high):
            owner, at = plan.owner(plane)
            rows = slice(2 * (at % 4), 2 * (at % 4) + 2)
            work[:, plane - low + 2, LOW - 2 : LOW, :] = ref["low halo", owner][:, at // 4, rows, :]
            work[:, plane - low + 2, LOW + cycle : LOW + cycle + 2, :] = ref["high halo", owner][:, at // 4, rows, :]
            if last:
                ref["earlier"][:, plane - low] = cells(plane, 1) + 2.0 * cells(plane, 2)
        start = plan.place(kind, low)

        def compute(tile, steps, low=low, start=start, number=number):
            for f in range(plan.fields):
                factors = [spread[f * terms + number] for number in range(terms)]
                values = {}
                for step in steps:
                    at = tile * 4 + step - start % 4
                    for row in range(0, cycle, 8):
                        here = slice(LOW + row, LOW + row + 8)
                        center = work[f, at + 2, here, :]
                        left = jnp.where(not_first, pltpu.roll(center, 1, 1), 0.0)
                        right = jnp.where(not_last, pltpu.roll(center, radial - 1, 1), 0.0)
                        total = factors[0] * (left + right)
                        for e in range(plan.fields):
                            total += factors[1 + e] * (center if e == f else work[e, at + 2, here, :])
                        for place, by in enumerate((-2, -1, 1, 2)):
                            total += factors[1 + plan.fields + place] * work[f, at + 2 + by, here, :]
                            beside = slice(LOW + row + by, LOW + row + by + 8)
                            total += factors[5 + plan.fields + place] * work[f, at + 2, beside, :]
                        base = state[f, low + at, row : row + 8, :]
                        if last:
                            value = (ref["earlier"][f, at, row : row + 8, :] + center - base) * (1.0 / 3.0)
                            value += (time_step / 6.0) * total
                        else:
                            value = base + (time_step if stage == 2 else 0.5 * time_step) * total
                        values[step, row] = value
                for (step, row), value in values.items():
                    at = tile * 4 + step - start % 4
                    if last:
                        ref["made"][number, f, at, row : row + 8, :] = value
                        continue
                    ref["out"][f, start + at, row : row + 8, :] = value
                    rows = slice(2 * step, 2 * step + 2)
                    if row == 0:
                        ref["low edge"][f, start // 4 + tile, rows, :] = value[:2]
                    if row == cycle - 8:
                        ref["high edge"][f, start // 4 + tile, rows, :] = value[6:]

        def whole_tile(tile, carry, compute=compute):
            compute(tile, range(4))
            return carry

        block = BLOCK // 4 if last else size // 4
        for first in range(0, size // 4, block):
            after = min(first + block, size // 4)
            lax.fori_loop(first, after, whole_tile, 0)
            if last:
                copies.append(
                    pltpu.make_async_copy(
                        ref["made"].at[number, :, 4 * first : 4 * after],
                        ref["result"].at[:, low + 4 * first : low + 4 * after],
                        ref["sem"].at[len(copies)],
                    )
                )
                copies[-1].start()
    for item in copies:
        item.wait()
    ref["token"][...] = jnp.zeros(ref["token"].shape, jnp.float32)


def stage_call(plan, stage, kind, scalars, state, levels, halos, ghosts, after, result=None):
    ranges = plan.ranges(kind)
    last = stage == 3
    longest = max(high - low for low, high in ranges)
    operands = {"state": near(state)}
    specs = [whole(VMEM)]

    def add(name, value):
        operands[name] = near(value)
        specs.append(whole(VMEM))

    kinds = {plan.owner(plane)[0] for low, high in ranges for plane in range(low, high)}
    for owner in sorted(kinds):
        add(("low halo", owner), halos[owner][0])
        add(("high halo", owner), halos[owner][1])
    for level in (1, 2, stage) if last else (stage,) if stage else ():
        edge = 2 if level == stage else 0
        planes = [plane for low, high in ranges for plane in range(max(0, low - edge), min(plan.axial, high + edge))]
        for owner in sorted({plan.owner(plane)[0] for plane in planes}):
            add(("cells", level, owner), levels[level][owner])
    if kind == "ends":
        add("ghosts", ghosts)
    for number, token in enumerate(after):
        add(("after", number), token)
    aliases = {}
    if result is not None:
        aliases = {len(scalars) + len(operands): 0}
        operands["earlier result"] = result
        specs.append(whole(pl.ANY))
    token = held((8, plan.radial))
    if last:
        outs = {"result": jax.ShapeDtypeStruct(state.shape, jnp.float32), "token": token}
    else:
        edges = edge_shape(plan, kind)
        cells = held((plan.fields, plan.kept(kind), plan.cycle, plan.radial))
        outs = {"out": cells, "low edge": edges, "high edge": edges, "token": token}
    scratch = {
        "work": held((plan.fields, longest + 4, plan.cycle + 16, plan.radial)),
        "spread": held((plan.fields * (plan.fields + 9), 8, plan.radial)),
    }
    if last:
        scratch["earlier"] = held((plan.fields, longest, plan.cycle, plan.radial))
        scratch["made"] = held((len(ranges), plan.fields, longest, plan.cycle, plan.radial))
        scratch["sem"] = pltpu.SemaphoreType.DMA((sum(-(-(high - low) // BLOCK) for low, high in ranges),))
    names = (*operands, *outs, *scratch)
    return pl.pallas_call(
        functools.partial(stage_kernel, plan, stage, kind, names),
        in_specs=[whole(SMEM)] * len(scalars) + specs,
        out_specs=[whole(pl.ANY if name == "result" else VMEM) for name in outs],
        out_shape=list(outs.values()),
        scratch_shapes=list(scratch.values()),
        input_output_aliases=aliases,
        cost_estimate=pl.CostEstimate(flops=10000000000, transcendentals=0, bytes_accessed=10000000),
        compiler_params=params(),
        name=f"stage{stage}_{kind}",
    )(*scalars, *operands.values())


def exchange(edges):
    size = lax.axis_size("sector")
    ahead = [(i, (i + 1) % size) for i in range(size)]
    back = [(i, (i - 1) % size) for i in range(size)]
    low_edges, high_edges = edges
    return lax.ppermute(high_edges, "sector", ahead), lax.ppermute(low_edges, "sector", back)


def on_device(state, interp_blocks, rotor_offset, axial_speed, row_swirl, diffusivity, coupling):
    plan = Plan(state, lax.axis_size("sector"))
    rows = lax.axis_size("row")
    sections = rotor_offset.shape[0]
    place = jnp.stack([lax.axis_index("row"), lax.axis_index("sector")]).astype(jnp.int32)
    scalars = (axial_speed, row_swirl, diffusivity, coupling)
    back = [(row + 1, row) for row in range(rows - 1)]
    ahead = [(row, row + 1) for row in range(rows - 1)]

    below = lax.ppermute(state[:, : plan.deep], "row", back)
    next_swirl = lax.ppermute(row_swirl, "row", back)
    weights = jnp.pad(interp_blocks, ((0, 0), (0, 0), (0, plan.full - interp_blocks.shape[2])))
    packed = pack(plan, state, below)
    levels, halos = [None], [{}]
    got = lax.all_to_all(packed, "sector", 0, 0, tiled=True)
    for kind in ("mid", "ends"):
        halos[0][kind] = exchange(first_edges(plan, kind, state, packed))
    token, result, ghosts = (), None, None

    def step(stage, kind):
        nonlocal token, result
        ghost = ghosts[stage] if kind == "ends" else None
        outs = stage_call(plan, stage, kind, scalars, state, levels, halos[stage], ghost, token, result if stage == sections - 1 else None)
        token = outs[-1:]
        if stage == sections - 1:
            result = outs[0]
            return None
        if len(levels) == stage + 1:
            levels.append({})
            halos.append({})
        levels[stage + 1][kind] = outs[0]
        return outs[1:3]

    def send(stage, kind, edges):
        halos[stage + 1][kind] = exchange(edges)

    def go(stage, kind):
        edges = step(stage, kind)
        if edges is not None:
            send(stage, kind, edges)

    downstream, to_next, *token = zone(plan, place, rotor_offset, scalars, next_swirl, weights, got)
    upstream = lax.ppermute(to_next, "row", ahead)
    mid_edges = step(0, "mid")
    joined = jnp.concatenate([upstream, downstream], axis=1)
    joined, *rest = lax.optimization_barrier((joined, *token, *mid_edges))
    token, mid_edges = rest[:1], rest[1:]
    returned = lax.all_to_all(joined, "sector", 0, 0, tiled=True)
    send(0, "mid", mid_edges)
    *ghosts, last_token = unpack(plan, returned, sections, token)
    token = (last_token,)
    go(0, "ends")
    for stage in range(1, sections):
        go(stage, "mid")
        go(stage, "ends")
    return result


def solution(mesh):
    return jax.shard_map(
        on_device,
        mesh=mesh,
        in_specs=(P(None, "row", "sector", None), P(), P(), P(), P("row"), P(), P()),
        out_specs=P(None, "row", "sector", None),
        check_vma=False,
    )
```
